32 devices in a mesh: en: 2 (over x), ph: 4 (over y, core), blk: 4 (over z).
Axes of the slice: x: 2, y: 2, z: 4, core: 2. Of those that a mesh axis runs over, the one named last changes fastest.
Arguments:
- lesser_in: bfloat16 [6, 8, 512, 512], P('en', 'blk', 'ph'), may hold values from -6 to 6
- greater_in: bfloat16 [6, 8, 512, 512], P('en', 'blk', 'ph'), may hold values from -6 to 6
- inverse: bfloat16 [6, 8, 512, 512], P('en', 'blk', 'ph'), may hold values from -0.25 to 0.25
- offsets: int32 [6, 8], P('en', 'ph'), may hold values from -9 to 9, as said below
- couplings: float32 [6, 8], P('en', 'ph'), may hold values from 0.2 to 1
Outputs:
- lesser_out: bfloat16 [6, 8, 512, 512], P('en', 'blk', 'ph')
- greater_out: bfloat16 [6, 8, 512, 512], P('en', 'blk', 'ph')
The draws below stay inside these ranges and needn't reach their ends.
Inputs may be any that keep to these rules, and one draw needn't show every extreme that they name: `offsets`: both extremes occur in every draw.
All inputs are finite; a program needn't handle non-finite values.
Results may differ from the reference program's by a relative error of at most 0.0057.
Values may be sent and summed in bfloat16 or wider, within the bound.
No kernel may reach another device: no remote copies, remote signals or barrier semaphores. Data moves between devices by JAX's collectives and lax.ppermute only.
A program may use at most 64 MiB of HBM per device.

```python
import math
import jax
import jax.numpy as jnp
from jax import lax

O = 512
MAXOFF = 9
NE = 6
NB = 8
K = 8


def draw_offsets(key, part):
    values = jax.random.randint(key, (NE, K), -MAXOFF, MAXOFF + 1, dtype=jnp.int32)
    values = values.at[0, 0].set(MAXOFF)
    values = values.at[NE - 1, 0].set(-MAXOFF)
    return values


def levels(key, extent, shards, smallest, top_value):
    level, own = 1.0, jax.random.fold_in(key, 6)
    for position, blocks in shards:
        steps = jnp.exp(jax.random.uniform(jax.random.fold_in(own, position), (blocks,), jnp.float32, smallest / len(shards), top_value / len(shards)))
        level = level * jnp.repeat(steps, extent[position] // blocks).reshape([-1 if axis == position else 1 for axis in range(len(extent))])
    return level


def centred(own_key, dims, spread, bound, shards=(), kind=jnp.bfloat16):
    result = jax.random.normal(own_key, dims, jnp.float32) * spread
    if len(shards) > 0:
        result = levels(own_key, dims, shards, -0.22, 0.18) * result
    return jnp.clip(result, min=-bound, max=bound).astype(kind)


def setup_inputs(seed: int = 0) -> dict:
    keys = jax.random.split(jax.random.key(seed), 6)
    return {
        "lesser_in": centred(keys[0], (NE, NB, O, O), 1.0, 6.0, ((0, 2), (1, 4), (2, 4))),
        "greater_in": centred(keys[1], (NE, NB, O, O), 1.0, 6.0, ((0, 2), (1, 4), (2, 4))),
        "inverse": centred(keys[2], (NE, NB, O, O), O ** -0.5, 0.25, ((0, 2), (1, 4), (2, 4))),
        "offsets": draw_offsets(jax.random.fold_in(keys[5], 71), 0),
        "couplings": jnp.clip(jnp.exp(math.log(1.0) - 1.609438 * jax.random.uniform(keys[4], (NE, K), jnp.float32) ** levels(keys[4], (NE, K), ((0, 2), (1, 4)), -0.2, 0.2)), 0.2, 1.0),
    }


def reference(lesser_in, greater_in, inverse, offsets, couplings):
    padding = jnp.zeros((MAXOFF,) + lesser_in.shape[1:], jnp.bfloat16)
    lesser_pad = jnp.concatenate([padding, lesser_in, padding], axis=0)
    greater_pad = jnp.concatenate([padding, greater_in, padding], axis=0)

    def per_energy(packed):
        energy, shifts, weights, inverse_n = packed
        source = (energy + shifts + MAXOFF).astype(jnp.int32)
        inverse_f32 = inverse_n.astype(jnp.float32)
        results = []
        for padded in (lesser_pad, greater_pad):
            shifted = jnp.take(padded, source, axis=0).astype(jnp.float32)
            self_energy = jnp.einsum("k,kbij->bij", weights.astype(jnp.float32), shifted, precision=lax.Precision.HIGHEST).astype(jnp.bfloat16)
            left_product = jnp.einsum("bik,bkj->bij", inverse_f32, self_energy.astype(jnp.float32), precision=lax.Precision.HIGHEST).astype(jnp.bfloat16)
            results.append(jnp.einsum("bik,bjk->bij", left_product.astype(jnp.float32), inverse_f32, precision=lax.Precision.HIGHEST).astype(jnp.bfloat16))
        return results[0], results[1]

    energies = jnp.arange(NE, dtype=jnp.int32)
    lesser_out, greater_out = lax.map(per_energy, (energies, offsets, couplings, inverse))
    return lesser_out, greater_out
```

```python
import functools
import math

import jax
import jax.numpy as jnp
from jax import lax
from jax.experimental import pallas as pl
from jax.experimental.pallas import tpu as pltpu
from jax.sharding import PartitionSpec as P

MAXOFF = 9
BF16 = jnp.bfloat16


def mix_kernel(sources, index_ref, weight_ref, *refs):
    ins, out_ref = refs[:sources], refs[sources]
    e, blocks, rows, _ = out_ref.shape
    step = 16
    weights = [
        [weight_ref[n, m] for m in range(sources * e)] for n in range(e)
    ]
    for b in range(blocks):

        @pl.loop(0, rows // step)
        def _(i):
            at = pl.ds(pl.multiple_of(i * step, step), step)
            totals = [None] * e
            for t in range(sources):
                for m in range(e):
                    g = ins[t][m, b, at, :].astype(jnp.float32)
                    for n in range(e):
                        term = weights[n][t * e + m] * g
                        totals[n] = term if totals[n] is None else totals[n] + term
            for n in range(e):
                out_ref[n, b, at, :] = totals[n].astype(out_ref.dtype)


def mix(ins, index, weights, owned):
    e, _, rows, o = ins[0].shape
    chunk = math.gcd(rows, 32)
    spec = pl.BlockSpec((e, owned, chunk, o), lambda i, at: (0, at[0], i, 0))
    return pl.pallas_call(
        functools.partial(mix_kernel, len(ins)),
        grid_spec=pltpu.PrefetchScalarGridSpec(
            num_scalar_prefetch=1,
            grid=(rows // chunk,),
            in_specs=[pl.BlockSpec(memory_space=pltpu.SMEM)] + [spec] * len(ins),
            out_specs=pl.BlockSpec((e, owned, chunk, o), lambda i, at: (0, 0, i, 0)),
        ),
        out_shape=jax.ShapeDtypeStruct((e, owned, rows, o), BF16),
        cost_estimate=pl.CostEstimate(
            flops=2 * len(ins) * e * e * owned * rows * o,
            bytes_accessed=2 * (len(ins) + 1) * e * owned * rows * o,
            transcendentals=0,
        ),
        name="mix",
    )(index.reshape(1), weights, *ins)


def product_kernel(pieces, lefts, place_ref, *refs):
    a_in, s_in = refs[:pieces], refs[pieces : 2 * pieces]
    outs = refs[2 * pieces : 2 * pieces + lefts]
    a_full, s_full, sems = refs[2 * pieces + lefts :]
    e, blocks, rows, _ = outs[0].shape
    copies = []
    for n in range(e):
        batch = []
        for k, (ins, full) in enumerate(((a_in, a_full), (s_in, s_full))):
            for i in range(pieces):
                at = pl.ds(pl.multiple_of(place_ref[i] * rows, rows), rows)
                batch.append(
                    pltpu.make_async_copy(
                        ins[i].at[n], full.at[n, :, at, :], sems.at[n, k, i]
                    )
                )
        for copy in batch:
            copy.start()
        copies.append(batch)
    for n in range(e):
        for copy in copies[n]:
            copy.wait()
        for b in range(blocks):
            left = jnp.concatenate(
                [
                    a_full[n, b, pl.ds(pl.multiple_of(place_ref[i] * rows, rows), rows), :]
                    for i in range(lefts)
                ],
                axis=0,
            )
            first = jnp.dot(
                left, s_full[n, b], preferred_element_type=jnp.float32
            ).astype(BF16)
            both = lax.dot_general(
                first,
                a_full[n, b],
                (((1,), (1,)), ((), ())),
                preferred_element_type=jnp.float32,
            ).astype(BF16)
            for i in range(lefts):
                outs[i][n, b] = both[i * rows : (i + 1) * rows]


def product(a_pieces, s_pieces, places, lefts):
    pieces = len(a_pieces)
    e, blocks, rows, o = a_pieces[0].shape
    anywhere = pl.BlockSpec(memory_space=pl.ANY)
    full = pltpu.VMEM((e, blocks, pieces * rows, o), BF16)
    return pl.pallas_call(
        functools.partial(product_kernel, pieces, lefts),
        in_specs=[pl.BlockSpec(memory_space=pltpu.SMEM)] + [anywhere] * (2 * pieces),
        out_specs=[pl.BlockSpec(memory_space=pltpu.VMEM)] * lefts,
        out_shape=[jax.ShapeDtypeStruct((e, blocks, rows, o), BF16)] * lefts,
        scratch_shapes=[full, full, pltpu.SemaphoreType.DMA((e, 2, pieces))],
        compiler_params=pltpu.CompilerParams(vmem_limit_bytes=32 * 1024 * 1024),
        cost_estimate=pl.CostEstimate(
            flops=4 * e * blocks * lefts * rows * o * o,
            bytes_accessed=2 * e * blocks * rows * o * (2 * pieces + lefts),
            transcendentals=0,
        ),
        name="product",
    )(places, *a_pieces, *s_pieces)


def solution(mesh):
    en, ph = mesh.shape["en"], mesh.shape["ph"]

    def on_device(lesser_in, greater_in, inverse, offsets, couplings):
        e, nb, r, o = lesser_in.shape
        owners = math.gcd(nb, ph)
        lanes = ph // owners
        owned = nb // owners
        en_at, ph_at = lax.axis_index("en"), lax.axis_index("ph")
        owner, lane = ph_at // lanes, ph_at % lanes

        def to_owner(x, d):
            pairs = [
                (p, (p // lanes + d) % owners * lanes + p % lanes) for p in range(ph)
            ]
            return lax.ppermute(x, "ph", pairs)

        def to_lane(x, d):
            pairs = [
                (p, p // lanes * lanes + (p % lanes + d) % lanes) for p in range(ph)
            ]
            return lax.ppermute(x, "ph", pairs)

        def to_energy(x, t):
            return lax.ppermute(x, "en", [((i + t) % en, i) for i in range(en)])

        def blocks_of(x, at):
            return lax.dynamic_slice_in_dim(x, at * owned, owned, axis=1)

        reach = (MAXOFF + e - 1) // e
        shifts = [t for t in range(1, en) if t <= reach or en - t <= reach]
        sources = len(shifts) + 1

        lesser_from = [lesser_in] + [to_energy(lesser_in, t) for t in shifts]
        greater_own = blocks_of(greater_in, owner)
        greater_rows = [greater_own] + [
            to_owner(blocks_of(greater_in, (owner + d) % owners), d) for d in range(1, owners)
        ]
        inverse_rows = [blocks_of(inverse, owner)] + [
            to_owner(blocks_of(inverse, (owner + d) % owners), d) for d in range(1, owners)
        ]

        small = lax.all_gather(
            jnp.stack([offsets.astype(jnp.float32), couplings]), "ph", axis=2, tiled=True
        )
        away = jnp.stack(
            [((en_at + t) % en - en_at) * e for t in [0] + shifts]
        )
        apart = (away[:, None] + jnp.arange(e)[None, :]).reshape(1, -1) - jnp.arange(e)[:, None]
        weights = jnp.sum(
            jnp.where(
                small[0][:, None, :] == apart[:, :, None].astype(jnp.float32),
                small[1][:, None, :],
                jnp.float32(0.0),
            ),
            axis=2,
        )

        zero = jnp.zeros((), jnp.int32)
        lesser_rows = [None] * owners
        for d in range(1, owners):
            lesser_rows[d] = to_owner(mix(lesser_from, (owner + d) % owners, weights, owned), d)
        lesser_rows[0] = mix(lesser_from, owner, weights, owned)
        greater_mixed = [
            mix([rows] + [to_energy(rows, t) for t in shifts], zero, weights, owned)
            for rows in greater_rows
        ]

        places = jnp.stack(
            [
                (owner - d) % owners * lanes + (lane - q) % lanes
                for q in range(lanes)
                for d in range(owners)
            ]
        )

        def all_lanes(pieces):
            return pieces + [to_lane(x, q) for q in range(1, lanes) for x in pieces]

        inverse_full = all_lanes(inverse_rows)

        def finish(sigma_rows):
            outs = product(inverse_full, all_lanes(sigma_rows), places, owners)
            result = jnp.zeros((e, nb, r, o), BF16)
            for d in range(owners):
                back = outs[d] if d == 0 else to_owner(outs[d], owners - d)
                result = lax.dynamic_update_slice_in_dim(
                    result, back, (owner + d) % owners * owned, axis=1
                )
            return result

        return finish(lesser_rows), finish(greater_mixed)

    block, coupled = P("en", "blk", "ph", None), P("en", "ph")
    return jax.shard_map(
        on_device,
        mesh=mesh,
        in_specs=(block, block, block, coupled, coupled),
        out_specs=(block, block),
        check_vma=False,
    )
```

```python
import functools
import math

import jax
import jax.numpy as jnp
from jax import lax
from jax.experimental import pallas as pl
from jax.experimental.pallas import tpu as pltpu
from jax.sharding import PartitionSpec as P

MAXOFF = 9
BF16 = jnp.bfloat16


def mix_kernel(sources, index_ref, weight_ref, *refs):
    ins, out_ref = refs[:sources], refs[sources]
    e, blocks, rows, _ = out_ref.shape
    step = 16
    weights = [[weight_ref[n, m] for m in range(sources * e)] for n in range(e)]
    for b in range(blocks):
        block = index_ref[0] * blocks + b

        @pl.loop(0, rows // step)
        def _(i):
            at = pl.ds(pl.multiple_of(i * step, step), step)
            totals = [None] * e
            for t in range(sources):
                for m in range(e):
                    g = ins[t][m, block, at, :].astype(jnp.float32)
                    for n in range(e):
                        term = weights[n][t * e + m] * g
                        totals[n] = term if totals[n] is None else totals[n] + term
            for n in range(e):
                out_ref[n, b, at, :] = totals[n].astype(out_ref.dtype)


def mix(ins, index, weights, owned):
    e, _, rows, o = ins[0].shape
    scalars, whole = pl.BlockSpec(memory_space=pltpu.SMEM), pl.BlockSpec(memory_space=pltpu.VMEM)
    return pl.pallas_call(
        functools.partial(mix_kernel, len(ins)),
        in_specs=[scalars, scalars] + [whole] * len(ins),
        out_specs=whole,
        out_shape=jax.ShapeDtypeStruct((e, owned, rows, o), BF16),
        compiler_params=pltpu.CompilerParams(vmem_limit_bytes=32 * 1024 * 1024),
        cost_estimate=pl.CostEstimate(
            flops=2 * len(ins) * e * e * owned * rows * o,
            bytes_accessed=2 * (len(ins) + 1) * e * owned * rows * o,
            transcendentals=0,
        ),
        name="mix",
    )(index.reshape(1), weights, *ins)


def product_kernel(pieces, lefts, place_ref, *refs):
    a_in, s_in = refs[:pieces], refs[pieces : 2 * pieces]
    outs = refs[2 * pieces :]
    e, blocks, rows, _ = outs[0].shape
    spans = [pl.ds(pl.multiple_of(place_ref[j] * rows, rows), rows) for j in range(pieces)]
    for n in range(e):
        for b in range(blocks):
            left = jnp.concatenate(
                [
                    jnp.concatenate([a_in[i][n, b, :, at] for at in spans], axis=1)
                    for i in range(lefts)
                ],
                axis=0,
            )
            first = jnp.dot(
                left,
                jnp.concatenate([s[n, b] for s in s_in], axis=0),
                preferred_element_type=jnp.float32,
            ).astype(BF16)
            both = lax.dot_general(
                first,
                jnp.concatenate([a[n, b] for a in a_in], axis=0),
                (((1,), (1,)), ((), ())),
                preferred_element_type=jnp.float32,
            ).astype(BF16)
            for i in range(lefts):
                for j, at in enumerate(spans):
                    outs[i][n, b, :, at] = both[i * rows : (i + 1) * rows, j * rows : (j + 1) * rows]


def product(a_pieces, s_pieces, places, lefts):
    pieces = len(a_pieces)
    e, blocks, rows, o = a_pieces[0].shape
    whole = pl.BlockSpec(memory_space=pltpu.VMEM)
    return pl.pallas_call(
        functools.partial(product_kernel, pieces, lefts),
        in_specs=[pl.BlockSpec(memory_space=pltpu.SMEM)] + [whole] * (2 * pieces),
        out_specs=[whole] * lefts,
        out_shape=[jax.ShapeDtypeStruct((e, blocks, rows, o), BF16)] * lefts,
        compiler_params=pltpu.CompilerParams(vmem_limit_bytes=32 * 1024 * 1024),
        cost_estimate=pl.CostEstimate(
            flops=4 * e * blocks * lefts * rows * o * o,
            bytes_accessed=2 * e * blocks * rows * o * (2 * pieces + lefts),
            transcendentals=0,
        ),
        name="product",
    )(places, *a_pieces, *s_pieces)


def solution(mesh):
    en, ph = mesh.shape["en"], mesh.shape["ph"]

    def on_device(lesser_in, greater_in, inverse, offsets, couplings):
        e, nb, r, o = lesser_in.shape
        owners = math.gcd(nb, ph)
        lanes = ph // owners
        owned = nb // owners
        en_at, ph_at = lax.axis_index("en"), lax.axis_index("ph")
        owner, lane = lax.div(ph_at, lanes), lax.rem(ph_at, lanes)

        def to_owner(x, d):
            pairs = [
                (p, (p // lanes + d) % owners * lanes + p % lanes) for p in range(ph)
            ]
            return lax.ppermute(x, "ph", pairs)

        def to_lane(x, d):
            pairs = [
                (p, p // lanes * lanes + (p % lanes + d) % lanes) for p in range(ph)
            ]
            return lax.ppermute(x, "ph", pairs)

        def to_energy(x, t):
            return lax.ppermute(x, "en", [((i + t) % en, i) for i in range(en)])

        def blocks_of(x, at):
            return lax.dynamic_slice_in_dim(x, at * owned, owned, axis=1)

        reach = (MAXOFF + e - 1) // e
        shifts = [t for t in range(1, en) if t <= reach or en - t <= reach]
        sources = len(shifts) + 1

        own = jnp.stack([offsets.astype(jnp.float32), couplings])
        small = jnp.concatenate(
            [own]
            + [lax.ppermute(own, "ph", [((p + q) % ph, p) for p in range(ph)]) for q in range(1, ph)],
            axis=2,
        )
        away = jnp.stack([((en_at + t) % en - en_at) * e for t in [0] + shifts])
        apart = (away[:, None] + jnp.arange(e)[None, :]).reshape(1, -1) - jnp.arange(e)[:, None]
        weights = jnp.sum(
            jnp.where(
                small[0][:, None, :] == apart[:, :, None].astype(jnp.float32),
                small[1][:, None, :],
                jnp.float32(0.0),
            ),
            axis=2,
        )

        lesser_from = [lesser_in] + [to_energy(lesser_in, t) for t in shifts]
        inverse_rows = [blocks_of(inverse, owner)] + [
            to_owner(blocks_of(inverse, (owner + d) % owners), d) for d in range(1, owners)
        ]
        greater_in, small = lax.optimization_barrier((greater_in, small))
        greater_rows = [blocks_of(greater_in, owner)] + [
            to_owner(blocks_of(greater_in, (owner + d) % owners), d) for d in range(1, owners)
        ]

        zero = jnp.zeros((), jnp.int32)
        lesser_rows = [None] * owners
        for d in range(1, owners):
            lesser_rows[d] = to_owner(mix(lesser_from, (owner + d) % owners, weights, owned), d)
        lesser_rows[0] = mix(lesser_from, owner, weights, owned)
        greater_mixed = [
            mix([rows] + [to_energy(rows, t) for t in shifts], zero, weights, owned)
            for rows in greater_rows
        ]

        places = jnp.stack(
            [
                (owner - d) % owners * lanes + (lane - q) % lanes
                for q in range(lanes)
                for d in range(owners)
            ]
        )

        def all_lanes(pieces):
            return pieces + [to_lane(x, q) for q in range(1, lanes) for x in pieces]

        inverse_full = all_lanes(inverse_rows)

        def finish(sigma_rows):
            outs = product(inverse_full, all_lanes(sigma_rows), places, owners)
            result = jnp.zeros((e, nb, r, o), BF16)
            for d in range(owners):
                back = outs[d] if d == 0 else to_owner(outs[d], owners - d)
                result = lax.dynamic_update_slice_in_dim(
                    result, back, (owner + d) % owners * owned, axis=1
                )
            return result

        return finish(lesser_rows), finish(greater_mixed)

    block, coupled = P("en", "blk", "ph", None), P("en", "ph")
    return jax.shard_map(
        on_device,
        mesh=mesh,
        in_specs=(block, block, block, coupled, coupled),
        out_specs=(block, block),
        check_vma=False,
    )
```

```python
import functools
import math

import jax
import jax.numpy as jnp
from jax import lax
from jax.experimental import pallas as pl
from jax.experimental.pallas import tpu as pltpu
from jax.sharding import PartitionSpec as P

MAXOFF = 9
BF16 = jnp.bfloat16
STEP = 16
WHOLE = pl.BlockSpec(memory_space=pltpu.VMEM)
SCALARS = pl.BlockSpec(memory_space=pltpu.SMEM)


def call(kernel, outs, flops, name, *args, scalars=0):
    moved = sum(x.size for x in args) + sum(math.prod(x) for x in outs)
    return pl.pallas_call(
        kernel,
        in_specs=[SCALARS] * scalars + [WHOLE] * (len(args) - scalars),
        out_specs=[WHOLE] * len(outs),
        out_shape=[jax.ShapeDtypeStruct(x, BF16) for x in outs],
        compiler_params=pltpu.CompilerParams(vmem_limit_bytes=32 * 1024 * 1024),
        cost_estimate=pl.CostEstimate(
            flops=flops, bytes_accessed=2 * moved, transcendentals=0
        ),
        name=name,
    )(*args)


def weighted(weight_ref, rows, columns, load):
    totals = [None] * len(rows)
    for m in columns:
        g = load(m).astype(jnp.float32)
        for i, n in enumerate(rows):
            term = weight_ref[n, m] * g
            totals[i] = term if totals[i] is None else totals[i] + term
    return totals


def chunks(rows, body):
    @pl.loop(0, rows // STEP)
    def _(i):
        body(pl.ds(pl.multiple_of(i * STEP, STEP), STEP))


def mix(whole, others, index, weights, owned):
    e, _, rows, o = whole.shape
    sources = 1 + len(others)

    def kernel(index_ref, weight_ref, *refs):
        out_ref = refs[-1]
        blocks = out_ref.shape[1]
        for b in range(blocks):
            block = index_ref[0] * blocks + b

            def body(at):
                def load(m):
                    if m < e:
                        return refs[0][m, block, at, :]
                    return refs[m // e][m % e, b, at, :]

                totals = weighted(weight_ref, range(e), range(sources * e), load)
                for n in range(e):
                    out_ref[n, b, at, :] = totals[n].astype(BF16)

            chunks(rows, body)

    shape = (e, owned, rows, o)
    flops = 2 * sources * e * math.prod(shape)
    return call(kernel, [shape], flops, "mix", index.reshape(1), weights, whole, *others, scalars=2)[0]


def partial_sums(row_pieces, weights):
    e, owned, rows, o = row_pieces[0].shape
    pieces = len(row_pieces)

    def kernel(weight_ref, *refs):
        for d in range(pieces):
            for b in range(owned):

                def body(at):
                    totals = weighted(
                        weight_ref, range(e), range(e), lambda m: refs[d][m, b, at, :]
                    )
                    for n in range(e):
                        refs[pieces + n][d, b, at, :] = totals[n].astype(BF16)

                chunks(rows, body)

    shape = (pieces, owned, rows, o)
    return call(
        kernel, [shape] * e, 2 * e * e * math.prod(shape), "partial_sums", weights, *row_pieces, scalars=1
    )


def add_partial(n, row_pieces, received, weights):
    e, owned, rows, o = row_pieces[0].shape
    pieces = len(row_pieces)

    def kernel(weight_ref, *refs):
        for d in range(pieces):
            for b in range(owned):

                def body(at):
                    (total,) = weighted(
                        weight_ref, [n], range(e), lambda m: refs[d][m, b, at, :]
                    )
                    for other in refs[pieces:-1]:
                        total = total + other[d, b, at, :].astype(jnp.float32)
                    refs[-1][d, b, at, :] = total.astype(BF16)

                chunks(rows, body)

    shape = (pieces, owned, rows, o)
    return call(
        kernel, [shape], 2 * e * math.prod(shape), "add_partial", weights, *row_pieces, *received, scalars=1
    )[0]


def product(energies, a_pieces, s_arrays, s_at, places, lefts):
    pieces = len(a_pieces)
    _, owned, rows, o = a_pieces[0].shape

    def kernel(place_ref, *refs):
        a_in, s_in = refs[:pieces], refs[pieces : pieces + len(s_arrays)]
        outs = refs[pieces + len(s_arrays) :]
        spans = [pl.ds(pl.multiple_of(place_ref[j] * rows, rows), rows) for j in range(pieces)]
        for k, n in enumerate(energies):
            for b in range(owned):
                left = jnp.concatenate(
                    [
                        jnp.concatenate([a_in[i][n, b, :, at] for at in spans], axis=1)
                        for i in range(lefts)
                    ],
                    axis=0,
                )
                at_piece = [s_at(n, j) for j in range(pieces)]
                sigma = jnp.concatenate([s_in[which][lead, b] for which, lead in at_piece], axis=0)
                first = jnp.dot(left, sigma, preferred_element_type=jnp.float32).astype(BF16)
                both = lax.dot_general(
                    first,
                    jnp.concatenate([a[n, b] for a in a_in], axis=0),
                    (((1,), (1,)), ((), ())),
                    preferred_element_type=jnp.float32,
                ).astype(BF16)
                for i in range(lefts):
                    for j, at in enumerate(spans):
                        outs[i][k, b, :, at] = both[i * rows : (i + 1) * rows, j * rows : (j + 1) * rows]

    shape = (len(energies), owned, rows, o)
    return call(
        kernel,
        [shape] * lefts,
        4 * lefts * o * math.prod(shape),
        "product",
        places,
        *a_pieces,
        *s_arrays,
        scalars=1,
    )


def after(x, *earlier):
    return lax.optimization_barrier((x,) + earlier)[0]


def solution(mesh):
    en, ph = mesh.shape["en"], mesh.shape["ph"]

    def on_device(lesser_in, greater_in, inverse, offsets, couplings):
        e, nb, r, o = lesser_in.shape
        owners = math.gcd(nb, ph)
        lanes = ph // owners
        owned = nb // owners
        en_at, ph_at = lax.axis_index("en"), lax.axis_index("ph")
        owner, lane = lax.div(ph_at, lanes), lax.rem(ph_at, lanes)

        def place_of(d, q):
            back = lax.rem(owner + owners - d, owners) if d else owner
            beside = lax.rem(lane + lanes - q, lanes) if q else lane
            return back * lanes + beside

        def owner_at(d):
            return lax.rem(owner + d, owners) if d else owner

        def to_owner(x, d):
            pairs = [(p, (p // lanes + d) % owners * lanes + p % lanes) for p in range(ph)]
            return lax.ppermute(x, "ph", pairs)

        def to_lane(x, q):
            pairs = [(p, p // lanes * lanes + (p % lanes + q) % lanes) for p in range(ph)]
            return lax.ppermute(x, "ph", pairs)

        def from_energy(x, t):
            return lax.ppermute(x, "en", [((i + t) % en, i) for i in range(en)])

        def blocks_of(x, d):
            return lax.dynamic_slice_in_dim(x, owner_at(d) * owned, owned, axis=1)

        reach = (MAXOFF + e - 1) // e
        shifts = [t for t in range(1, en) if t <= reach or en - t <= reach]

        lesser_part = [blocks_of(lesser_in, d) for d in range(1, owners)]
        lesser_from = [[from_energy(x, t) for t in shifts] for x in lesser_part]

        mine = after(jnp.stack([offsets.astype(jnp.float32), couplings]), *lesser_part)
        column = jnp.concatenate([mine] + [to_owner(mine, d) for d in range(1, owners)], axis=2)

        greater_part = [after(blocks_of(greater_in, d), mine) for d in range(1, owners)]
        greater_rows = [to_owner(x, d + 1) for d, x in enumerate(greater_part)]
        inverse_part = [after(blocks_of(inverse, d), *greater_part) for d in range(1, owners)]
        inverse_rows = [to_owner(x, d + 1) for d, x in enumerate(inverse_part)]
        lesser_own = after(blocks_of(lesser_in, 0), *inverse_part)
        lesser_from.insert(0, [from_energy(lesser_own, t) for t in shifts])
        inverse_rows.insert(0, after(blocks_of(inverse, 0), lesser_own))
        greater_rows.insert(0, after(blocks_of(greater_in, 0), lesser_own))

        small = jnp.concatenate([column] + [to_lane(column, q) for q in range(1, lanes)], axis=2)
        away = jnp.stack([(lax.rem(en_at + t, en) - en_at) * e for t in [0] + shifts])
        apart = (away[:, None] + jnp.arange(e)[None, :]).reshape(1, -1) - jnp.arange(e)[:, None]
        weights = jnp.sum(
            jnp.where(
                small[0][:, None, :] == apart[:, :, None].astype(jnp.float32),
                small[1][:, None, :],
                jnp.float32(0.0),
            ),
            axis=2,
        )
        weights_for = [
            lax.ppermute(
                weights[:, (i + 1) * e : (i + 2) * e], "en", [(j, (j + t) % en) for j in range(en)]
            )
            for i, t in enumerate(shifts)
        ]

        lesser_rows = [None] * owners
        last = weights
        for d in range(1, owners):
            mixed = mix(after(lesser_in, last), lesser_from[d], owner_at(d), weights, owned)
            lesser_rows[d] = to_owner(mixed, d)
            last = mixed
        received = [[] for _ in range(e)]
        for t, weight in zip(shifts, weights_for):
            for n, part in enumerate(partial_sums(greater_rows, after(weight, last))):
                received[n].append(from_energy(part, t))
                last = part
        lesser_rows[0] = mix(after(lesser_in, last), lesser_from[0], owner, weights, owned)
        last = lesser_rows[0]

        def all_lanes(pieces):
            return pieces + [to_lane(x, q) for q in range(1, lanes) for x in pieces]

        places = jnp.stack([place_of(d, q) for q in range(lanes) for d in range(owners)])
        inverse_full = all_lanes(inverse_rows)

        def put(result, outs, n):
            for d, out in enumerate(outs):
                back = to_owner(out, owners - d) if d else out
                result = lax.dynamic_update_slice(result, back, (n, owner_at(d) * owned, 0, 0))
            return result

        lesser_out = jnp.zeros((e, nb, r, o), BF16)
        greater_out = jnp.zeros((e, nb, r, o), BF16)
        for n in range(e):
            sigma = add_partial(n, greater_rows, received[n], after(weights, last))
            outs = product(
                [n],
                inverse_full,
                all_lanes([sigma]),
                lambda n, j: (j // owners, j % owners),
                places,
                owners,
            )
            greater_out = put(greater_out, outs, n)
            last = outs[-1]
            if n == 0:
                outs = product(
                    range(e),
                    inverse_full,
                    all_lanes(lesser_rows),
                    lambda n, j: (j, n),
                    after(places, last),
                    owners,
                )
                lesser_out = put(lesser_out, outs, 0)
                last = outs[-1]

        return lesser_out, greater_out

    block, coupled = P("en", "blk", "ph", None), P("en", "ph")
    return jax.shard_map(
        on_device,
        mesh=mesh,
        in_specs=(block, block, block, coupled, coupled),
        out_specs=(block, block),
        check_vma=False,
    )
```

```python
import functools
import math

import jax
import jax.numpy as jnp
from jax import lax
from jax.experimental import pallas as pl
from jax.experimental.pallas import tpu as pltpu
from jax.sharding import PartitionSpec as P

MAXOFF = 9
BF16 = jnp.bfloat16
STEP = 16
WHOLE = pl.BlockSpec(memory_space=pltpu.VMEM)
SCALARS = pl.BlockSpec(memory_space=pltpu.SMEM)


def call(kernel, outs, name, *args, scalars=0):
    return pl.pallas_call(
        kernel,
        in_specs=[SCALARS] * scalars + [WHOLE] * (len(args) - scalars),
        out_specs=[WHOLE] * len(outs),
        out_shape=[jax.ShapeDtypeStruct(x, BF16) for x in outs],
        compiler_params=pltpu.CompilerParams(vmem_limit_bytes=32 * 1024 * 1024),
        cost_estimate=pl.CostEstimate(flops=1, bytes_accessed=1, transcendentals=0),
        name=name,
    )(*args)


def weighted(weight_ref, rows, columns, load):
    totals = [None] * len(rows)
    for m in columns:
        g = load(m).astype(jnp.float32)
        for i, n in enumerate(rows):
            term = weight_ref[n, m] * g
            totals[i] = term if totals[i] is None else totals[i] + term
    return totals


def chunks(rows, body):
    @pl.loop(0, rows // STEP)
    def _(i):
        body(pl.ds(pl.multiple_of(i * STEP, STEP), STEP))


def mix(whole, others, index, weights, owned):
    e, _, rows, o = whole.shape
    sources = 1 + len(others)

    def kernel(index_ref, weight_ref, *refs):
        out_ref = refs[-1]
        blocks = out_ref.shape[1]
        for b in range(blocks):
            block = index_ref[0] * blocks + b

            def body(at):
                def load(m):
                    if m < e:
                        return refs[0][m, block, at, :]
                    return refs[m // e][m % e, b, at, :]

                totals = weighted(weight_ref, range(e), range(sources * e), load)
                for n in range(e):
                    out_ref[n, b, at, :] = totals[n].astype(BF16)

            chunks(rows, body)

    shape = (e, owned, rows, o)
    return call(kernel, [shape], "mix", index.reshape(1), weights, whole, *others, scalars=2)[0]


def partial_sums(row_pieces, weights):
    e, owned, rows, o = row_pieces[0].shape
    pieces = len(row_pieces)

    def kernel(weight_ref, *refs):
        for d in range(pieces):
            for b in range(owned):

                def body(at):
                    totals = weighted(
                        weight_ref, range(e), range(e), lambda m: refs[d][m, b, at, :]
                    )
                    for n in range(e):
                        refs[pieces + n][d, b, at, :] = totals[n].astype(BF16)

                chunks(rows, body)

    shape = (pieces, owned, rows, o)
    return call(
        kernel, [shape] * e, "partial_sums", weights, *row_pieces, scalars=1
    )


def add_partial(n, row_pieces, received, weights):
    e, owned, rows, o = row_pieces[0].shape
    pieces = len(row_pieces)

    def kernel(weight_ref, *refs):
        for d in range(pieces):
            for b in range(owned):

                def body(at):
                    (total,) = weighted(
                        weight_ref, [n], range(e), lambda m: refs[d][m, b, at, :]
                    )
                    for other in refs[pieces:-1]:
                        total = total + other[d, b, at, :].astype(jnp.float32)
                    refs[-1][d, b, at, :] = total.astype(BF16)

                chunks(rows, body)

    shape = (pieces, owned, rows, o)
    return call(
        kernel, [shape], "add_partial", weights, *row_pieces, *received, scalars=1
    )[0]


def product(energies, a_pieces, s_arrays, s_at, places, lefts):
    pieces = len(a_pieces)
    _, owned, rows, o = a_pieces[0].shape

    def kernel(place_ref, *refs):
        a_in, s_in = refs[:pieces], refs[pieces : pieces + len(s_arrays)]
        outs = refs[pieces + len(s_arrays) :]
        spans = [pl.ds(pl.multiple_of(place_ref[j] * rows, rows), rows) for j in range(pieces)]
        for k, n in enumerate(energies):
            for b in range(owned):
                left = jnp.concatenate(
                    [
                        jnp.concatenate([a_in[i][n, b, :, at] for at in spans], axis=1)
                        for i in range(lefts)
                    ],
                    axis=0,
                )
                at_piece = [s_at(n, j) for j in range(pieces)]
                sigma = jnp.concatenate([s_in[which][lead, b] for which, lead in at_piece], axis=0)
                first = jnp.dot(left, sigma, preferred_element_type=jnp.float32).astype(BF16)
                both = lax.dot_general(
                    first,
                    jnp.concatenate([a[n, b] for a in a_in], axis=0),
                    (((1,), (1,)), ((), ())),
                    preferred_element_type=jnp.float32,
                ).astype(BF16)
                for i in range(lefts):
                    for j, at in enumerate(spans):
                        outs[i][k, b, :, at] = both[i * rows : (i + 1) * rows, j * rows : (j + 1) * rows]

    shape = (len(energies), owned, rows, o)
    return call(
        kernel,
        [shape] * lefts,
        "product",
        places,
        *a_pieces,
        *s_arrays,
        scalars=1,
    )


def after(x, *earlier):
    return lax.optimization_barrier((x,) + earlier)[0]


def solution(mesh):
    en, ph = mesh.shape["en"], mesh.shape["ph"]

    def on_device(lesser_in, greater_in, inverse, offsets, couplings):
        e, nb, r, o = lesser_in.shape
        owners = math.gcd(nb, ph)
        lanes = ph // owners
        owned = nb // owners
        en_at, ph_at = lax.axis_index("en"), lax.axis_index("ph")
        owner, lane = lax.div(ph_at, lanes), lax.rem(ph_at, lanes)

        def place_of(d, q):
            back = lax.rem(owner + owners - d, owners) if d else owner
            beside = lax.rem(lane + lanes - q, lanes) if q else lane
            return back * lanes + beside

        def owner_at(d):
            return lax.rem(owner + d, owners) if d else owner

        def to_owner(x, d):
            pairs = [(p, (p // lanes + d) % owners * lanes + p % lanes) for p in range(ph)]
            return lax.ppermute(x, "ph", pairs)

        def to_lane(x, q):
            pairs = [(p, p // lanes * lanes + (p % lanes + q) % lanes) for p in range(ph)]
            return lax.ppermute(x, "ph", pairs)

        def from_energy(x, t):
            return lax.ppermute(x, "en", [((i + t) % en, i) for i in range(en)])

        def blocks_of(x, d):
            return lax.dynamic_slice_in_dim(x, owner_at(d) * owned, owned, axis=1)

        reach = (MAXOFF + e - 1) // e
        shifts = [t for t in range(1, en) if t <= reach or en - t <= reach]

        lesser_part = [blocks_of(lesser_in, d) for d in range(1, owners)]
        lesser_from = [[from_energy(x, t) for t in shifts] for x in lesser_part]

        mine = after(jnp.stack([offsets.astype(jnp.float32), couplings]), *lesser_part)
        column = jnp.concatenate([mine] + [to_owner(mine, d) for d in range(1, owners)], axis=2)

        greater_part = [after(blocks_of(greater_in, d), mine) for d in range(1, owners)]
        greater_rows = [to_owner(x, d + 1) for d, x in enumerate(greater_part)]
        inverse_part = [after(blocks_of(inverse, d), *greater_part) for d in range(1, owners)]
        inverse_rows = [to_owner(x, d + 1) for d, x in enumerate(inverse_part)]
        lesser_own = after(blocks_of(lesser_in, 0), *inverse_part)
        lesser_from.insert(0, [from_energy(lesser_own, t) for t in shifts])
        inverse_rows.insert(0, after(blocks_of(inverse, 0), lesser_own))
        greater_rows.insert(0, after(blocks_of(greater_in, 0), lesser_own))

        small = jnp.concatenate([column] + [to_lane(column, q) for q in range(1, lanes)], axis=2)
        away = jnp.stack([(lax.rem(en_at + t, en) - en_at) * e for t in [0] + shifts])
        apart = (away[:, None] + jnp.arange(e)[None, :]).reshape(1, -1) - jnp.arange(e)[:, None]
        weights = jnp.sum(
            jnp.where(
                small[0][:, None, :] == apart[:, :, None].astype(jnp.float32),
                small[1][:, None, :],
                jnp.float32(0.0),
            ),
            axis=2,
        )
        weights_for = [
            lax.ppermute(
                weights[:, (i + 1) * e : (i + 2) * e], "en", [(j, (j + t) % en) for j in range(en)]
            )
            for i, t in enumerate(shifts)
        ]

        lesser_rows = [None] * owners
        last = weights
        for d in range(1, owners):
            mixed = mix(after(lesser_in, last), lesser_from[d], owner_at(d), weights, owned)
            lesser_rows[d] = to_owner(mixed, d)
            last = mixed
        received = [[] for _ in range(e)]
        for t, weight in zip(shifts, weights_for):
            for n, part in enumerate(partial_sums(greater_rows, after(weight, last))):
                received[n].append(from_energy(part, t))
                last = part
        lesser_rows[0] = mix(after(lesser_in, last), lesser_from[0], owner, weights, owned)
        last = lesser_rows[0]

        def all_lanes(pieces):
            return pieces + [to_lane(x, q) for q in range(1, lanes) for x in pieces]

        places = jnp.stack([place_of(d, q) for q in range(lanes) for d in range(owners)])
        inverse_full = all_lanes(inverse_rows)

        def put(result, outs, n):
            for d, out in enumerate(outs):
                back = to_owner(out, owners - d) if d else out
                result = lax.dynamic_update_slice(result, back, (n, owner_at(d) * owned, 0, 0))
            return result

        lesser_out = jnp.zeros((e, nb, r, o), BF16)
        greater_out = jnp.zeros((e, nb, r, o), BF16)
        for n in range(e):
            sigma = add_partial(n, greater_rows, received[n], after(weights, last))
            outs = product(
                [n],
                inverse_full,
                all_lanes([sigma]),
                lambda n, j: (j // owners, j % owners),
                places,
                owners,
            )
            greater_out = put(greater_out, outs, n)
            last = outs[-1]
            if n == 0:
                outs = product(
                    range(e),
                    inverse_full,
                    all_lanes(lesser_rows),
                    lambda n, j: (j, n),
                    after(places, last),
                    owners,
                )
                lesser_out = put(lesser_out, outs, 0)
                last = outs[-1]

        return lesser_out, greater_out

    block, coupled = P("en", "blk", "ph", None), P("en", "ph")
    return jax.shard_map(
        on_device,
        mesh=mesh,
        in_specs=(block, block, block, coupled, coupled),
        out_specs=(block, block),
        check_vma=False,
    )
```

```python
import functools
import math

import jax
import jax.numpy as jnp
from jax import lax
from jax.experimental import pallas as pl
from jax.experimental.pallas import tpu as pltpu
from jax.sharding import PartitionSpec as P

MAXOFF = 9
BF16 = jnp.bfloat16
STEP = 16
WHOLE = pl.BlockSpec(memory_space=pltpu.VMEM)
SCALARS = pl.BlockSpec(memory_space=pltpu.SMEM)


def call(kernel, outs, name, *args, scalars=0):
    return pl.pallas_call(
        kernel,
        in_specs=[SCALARS] * scalars + [WHOLE] * (len(args) - scalars),
        out_specs=[WHOLE] * len(outs),
        out_shape=[jax.ShapeDtypeStruct(x, BF16) for x in outs],
        compiler_params=pltpu.CompilerParams(vmem_limit_bytes=12 * 1024 * 1024),
        cost_estimate=pl.CostEstimate(flops=1, bytes_accessed=1, transcendentals=0),
        name=name,
    )(*args)


def slices(arrays, index, owned):
    def kernel(index_ref, *refs):
        for i in range(len(arrays)):
            for b in range(owned):
                refs[len(arrays) + i][:, b] = refs[i][:, index_ref[i] * owned + b]

    shapes = [x.shape[:1] + (owned,) + x.shape[2:] for x in arrays]
    return call(kernel, shapes, "slices", jnp.stack(index), *arrays, scalars=1)


def weight_tables(en, en_at, shifts, pieces):
    _, e, _ = pieces[0].shape
    sources = len(shifts) + 1

    def kernel(at_ref, *refs):
        at, outs = at_ref[0], refs[len(pieces) :]
        for i, t in enumerate([0] + list(shifts)):
            away = (lax.rem(at + t, en) - at) * e
            for n in range(e):
                totals = [jnp.float32(0.0)] * e
                for ref in refs[: len(pieces)]:
                    for k in range(ref.shape[2]):
                        shift = ref[0, n, k].astype(jnp.int32) - away + n
                        for m in range(e):
                            totals[m] += jnp.where(shift == m, ref[1, n, k], jnp.float32(0.0))
                for m in range(e):
                    outs[i][n, m] = totals[m]

    return pl.pallas_call(
        kernel,
        in_specs=[SCALARS] * (1 + len(pieces)),
        out_specs=[SCALARS] * sources,
        out_shape=[jax.ShapeDtypeStruct((e, e), jnp.float32)] * sources,
        cost_estimate=pl.CostEstimate(flops=1, bytes_accessed=1, transcendentals=0),
        name="weight_tables",
    )(en_at.reshape(1), *pieces)


def weighted(tables, rows, sources, load):
    totals = [None] * len(rows)
    for t in range(sources):
        for m in range(tables[t].shape[1]):
            g = load(t, m).astype(jnp.float32)
            for i, n in enumerate(rows):
                term = tables[t][n, m] * g
                totals[i] = term if totals[i] is None else totals[i] + term
    return totals


def chunks(rows, body):
    @pl.loop(0, rows // STEP, unroll=math.gcd(rows // STEP, 4))
    def _(i):
        body(pl.ds(pl.multiple_of(i * STEP, STEP), STEP))


def mix(whole, others, index, tables, owned):
    e, _, rows, o = whole.shape
    sources = 1 + len(others)

    def kernel(index_ref, *refs):
        weight_refs, ins, out_ref = refs[:sources], refs[sources:-1], refs[-1]
        for b in range(owned):
            block = index_ref[0] * owned + b

            def body(at):
                def load(t, m):
                    return ins[t][m, b if t else block, at, :]

                totals = weighted(weight_refs, range(e), sources, load)
                for n in range(e):
                    out_ref[n, b, at, :] = totals[n].astype(BF16)

            chunks(rows, body)

    shape = (e, owned, rows, o)
    return call(kernel, [shape], "mix", index.reshape(1), *tables, whole, *others, scalars=1 + sources)[0]


def partial_sums(whole, others, index, table, owned):
    e, _, rows, o = whole.shape
    pieces = 1 + len(others)

    def kernel(index_ref, table_ref, *refs):
        for d in range(pieces):
            for b in range(owned):
                block = b if d else index_ref[0] * owned + b

                def body(at):
                    totals = weighted(
                        [table_ref], range(e), 1, lambda t, m: refs[d][m, block, at, :]
                    )
                    for n in range(e):
                        refs[pieces + n][d, b, at, :] = totals[n].astype(BF16)

                chunks(rows, body)

    shape = (pieces, owned, rows, o)
    return call(kernel, [shape] * e, "partial_sums", index.reshape(1), table, whole, *others, scalars=2)


def add_partial(n, whole, others, index, received, table, owned):
    e, _, rows, o = whole.shape
    pieces = 1 + len(others)

    def kernel(index_ref, table_ref, *refs):
        for d in range(pieces):
            for b in range(owned):
                block = b if d else index_ref[0] * owned + b

                def body(at):
                    (total,) = weighted(
                        [table_ref], [n], 1, lambda t, m: refs[d][m, block, at, :]
                    )
                    for other in refs[pieces:-1]:
                        total = total + other[d, b, at, :].astype(jnp.float32)
                    refs[-1][d, b, at, :] = total.astype(BF16)

                chunks(rows, body)

    shape = (pieces, owned, rows, o)
    return call(
        kernel, [shape], "add_partial", index.reshape(1), table, whole, *others, *received, scalars=2
    )[0]


def product(energies, a_pieces, s_arrays, s_at, places, lefts):
    pieces = len(a_pieces)
    _, owned, rows, o = a_pieces[0].shape

    def kernel(place_ref, *refs):
        a_in, s_in = refs[:pieces], refs[pieces : pieces + len(s_arrays)]
        outs = refs[pieces + len(s_arrays) :]
        spans = [pl.ds(pl.multiple_of(place_ref[j] * rows, rows), rows) for j in range(pieces)]
        for k, n in enumerate(energies):
            for b in range(owned):
                left = jnp.concatenate(
                    [
                        jnp.concatenate([a_in[i][n, b, :, at] for at in spans], axis=1)
                        for i in range(lefts)
                    ],
                    axis=0,
                )
                at_piece = [s_at(n, j) for j in range(pieces)]
                sigma = jnp.concatenate([s_in[which][lead, b] for which, lead in at_piece], axis=0)
                first = jnp.dot(left, sigma, preferred_element_type=jnp.float32).astype(BF16)
                both = lax.dot_general(
                    first,
                    jnp.concatenate([a[n, b] for a in a_in], axis=0),
                    (((1,), (1,)), ((), ())),
                    preferred_element_type=jnp.float32,
                ).astype(BF16)
                for i in range(lefts):
                    for j, at in enumerate(spans):
                        outs[i][k, b, :, at] = both[i * rows : (i + 1) * rows, j * rows : (j + 1) * rows]

    shape = (len(energies), owned, rows, o)
    return call(
        kernel,
        [shape] * lefts,
        "product",
        places,
        *a_pieces,
        *s_arrays,
        scalars=1,
    )


def after(x, *earlier):
    return lax.optimization_barrier((x,) + earlier)[0]


def ordered(xs, *earlier):
    return [after(x, *earlier) for x in xs]


def solution(mesh):
    en, ph = mesh.shape["en"], mesh.shape["ph"]

    def on_device(lesser_in, greater_in, inverse, offsets, couplings):
        e, nb, r, o = lesser_in.shape
        owners = math.gcd(nb, ph)
        lanes = ph // owners
        owned = nb // owners
        en_at, ph_at = lax.axis_index("en"), lax.axis_index("ph")
        owner, lane = lax.div(ph_at, lanes), lax.rem(ph_at, lanes)

        def place_of(d, q):
            back = lax.rem(owner + owners - d, owners) if d else owner
            beside = lax.rem(lane + lanes - q, lanes) if q else lane
            return back * lanes + beside

        def owner_at(d):
            return lax.rem(owner + d, owners) if d else owner

        def to_owner(x, d):
            pairs = [(p, (p // lanes + d) % owners * lanes + p % lanes) for p in range(ph)]
            return lax.ppermute(x, "ph", pairs)

        def to_lane(x, q):
            pairs = [(p, p // lanes * lanes + (p % lanes + q) % lanes) for p in range(ph)]
            return lax.ppermute(x, "ph", pairs)

        def from_energy(x, t):
            return lax.ppermute(x, "en", [((i + t) % en, i) for i in range(en)])

        reach = (MAXOFF + e - 1) // e
        shifts = [t for t in range(1, en) if t <= reach or en - t <= reach]

        mine = jnp.stack([offsets.astype(jnp.float32), couplings])
        column = jnp.concatenate([mine] + [to_owner(mine, d) for d in range(1, owners)], axis=2)

        away = [owner_at(d) for d in range(1, owners)]
        greater_part = slices([greater_in] * len(away), ordered(away, mine), owned)
        greater_rows = [to_owner(x, d + 1) for d, x in enumerate(greater_part)]
        lesser_part = slices([lesser_in] * len(away), ordered(away, *greater_part), owned)
        lesser_from = [[from_energy(x, t) for t in shifts] for x in lesser_part]

        def all_lanes(pieces):
            return pieces + [to_lane(x, q) for q in range(1, lanes) for x in pieces]

        inverse_part = slices([inverse] * len(away), ordered(away, *lesser_part), owned)
        inverse_rows = [to_owner(x, d + 1) for d, x in enumerate(inverse_part)]

        tables = weight_tables(en, after(en_at, *inverse_part), shifts, all_lanes([column]))
        tables_for = [
            lax.ppermute(table, "en", [(i, (i + t) % en) for i in range(en)])
            for t, table in zip(shifts, tables[1:])
        ]
        (lesser_own,) = slices([lesser_in], [after(owner, *tables)], owned)
        lesser_from.insert(0, [from_energy(lesser_own, t) for t in shifts])

        lesser_rows = [None] * owners
        last = (lesser_own,)
        for d in range(1, owners):
            mixed = mix(lesser_in, lesser_from[d], after(owner_at(d), *last), tables, owned)
            lesser_rows[d] = to_owner(mixed, d)
            last = (mixed,)
        (inverse_own,) = slices([inverse], [after(owner, *last)], owned)
        inverse_lanes = [[to_lane(inverse_own, q) for q in range(1, lanes)]]
        last = (inverse_own, *inverse_lanes[0])
        received = [[] for _ in range(e)]
        for t, table in zip(shifts, tables_for):
            parts = partial_sums(greater_in, greater_rows, after(owner, *last), table, owned)
            for n, part in enumerate(parts):
                received[n].append(from_energy(part, t))
            last = tuple(parts)
        inverse_lanes += [[to_lane(x, q) for q in range(1, lanes)] for x in inverse_rows]
        last += sum(map(tuple, inverse_lanes[1:]), ())
        lesser_rows[0] = mix(lesser_in, lesser_from[0], after(owner, *last), tables, owned)
        lesser_lanes = [[to_lane(lesser_rows[0], q) for q in range(1, lanes)]]
        last = (lesser_rows[0], *lesser_lanes[0])

        places = jnp.stack([place_of(d, q) for q in range(lanes) for d in range(owners)])

        def lane_order(rows, beside):
            return rows + [x[q] for q in range(lanes - 1) for x in beside]

        inverse_full = lane_order([inverse_own] + inverse_rows, inverse_lanes)

        def put(result, outs, n):
            for d, out in enumerate(outs):
                back = to_owner(out, owners - d) if d else out
                result = lax.dynamic_update_slice(result, back, (n, owner_at(d) * owned, 0, 0))
            return result

        lesser_out = jnp.zeros((e, nb, r, o), BF16)
        greater_out = jnp.zeros((e, nb, r, o), BF16)
        for n in range(e):
            sigma = add_partial(
                n, greater_in, greater_rows, after(owner, *last), received[n], tables[0], owned
            )
            outs = product(
                [n],
                inverse_full,
                all_lanes([sigma]),
                lambda n, j: (j // owners, j % owners),
                places,
                owners,
            )
            greater_out = put(greater_out, outs, n)
            last = tuple(outs)
            if n == 0:
                lesser_lanes += [[to_lane(x, q) for q in range(1, lanes)] for x in lesser_rows[1:]]
                outs = product(
                    range(e),
                    inverse_full,
                    lane_order(lesser_rows, lesser_lanes),
                    lambda n, j: (j, n),
                    after(places, *last),
                    owners,
                )
                lesser_out = put(lesser_out, outs, 0)
                last = tuple(outs)

        return lesser_out, greater_out

    block, coupled = P("en", "blk", "ph", None), P("en", "ph")
    return jax.shard_map(
        on_device,
        mesh=mesh,
        in_specs=(block, block, block, coupled, coupled),
        out_specs=(block, block),
        check_vma=False,
    )
```

```python
import math

import jax
import jax.numpy as jnp
from jax import lax
from jax.experimental import pallas as pl
from jax.experimental.pallas import tpu as pltpu
from jax.sharding import PartitionSpec as P

MAXOFF = 9
BF16 = jnp.bfloat16
STEP = 16
LANES = 128
WHOLE = pl.BlockSpec(memory_space=pltpu.VMEM)
PARAMS = pltpu.CompilerParams(vmem_limit_bytes=12 * 1024 * 1024)
COST = pl.CostEstimate(flops=1, bytes_accessed=1, transcendentals=0)


def call(kernel, outs, name, *args):
    outs = [x if isinstance(x, jax.ShapeDtypeStruct) else jax.ShapeDtypeStruct(x, BF16) for x in outs]
    return pl.pallas_call(
        kernel,
        in_specs=[WHOLE] * len(args),
        out_specs=[WHOLE] * len(outs),
        out_shape=outs,
        compiler_params=PARAMS,
        cost_estimate=COST,
        name=name,
    )(*args)


def after(xs, *earlier):
    return lax.optimization_barrier((tuple(xs), earlier))[0]


def chunks(rows, body):
    @pl.loop(0, rows // STEP, unroll=math.gcd(rows // STEP, 4))
    def _(i):
        body(pl.ds(pl.multiple_of(i * STEP, STEP), STEP))


def weighted(tables, energies, load):
    totals = [None] * len(energies)
    for t, table in enumerate(tables):
        for m in range(table.shape[0]):
            g = load(t, m).astype(jnp.float32)
            for i, n in enumerate(energies):
                row = table[m, n : n + 1, :]
                term = jnp.concatenate([row] * (g.shape[1] // LANES), axis=1) * g
                totals[i] = term if totals[i] is None else totals[i] + term
    return totals


def solution(mesh):
    en, ph = mesh.shape["en"], mesh.shape["ph"]

    def on_device(lesser_in, greater_in, inverse, offsets, couplings):
        e, nb, r, o = lesser_in.shape
        held = offsets.shape[1]
        owners = math.gcd(nb, ph)
        lanes = ph // owners
        owned = nb // owners
        pieces = ph
        others = range(1, owners)
        reach = (MAXOFF + e - 1) // e
        shifts = [t for t in range(1, en) if t <= reach or en - t <= reach]
        block = (e, owned, r, o)
        tile = -(-e // 8) * 8

        def owner_at(d):
            return lax.rem(lax.div(lax.axis_index("ph"), lanes) + d, owners)

        def place_of(j):
            at = lax.axis_index("ph")
            back = lax.rem(lax.div(at, lanes) + owners - j % owners, owners)
            return back * lanes + lax.rem(lax.rem(at, lanes) + lanes - j // owners, lanes)

        def to_owner(x, d):
            pairs = [(p, (p // lanes + d) % owners * lanes + p % lanes) for p in range(ph)]
            return lax.ppermute(x, "ph", pairs)

        def to_lanes(x):
            return [
                lax.ppermute(
                    x, "ph", [(p, p // lanes * lanes + (p % lanes + q) % lanes) for p in range(ph)]
                )
                for q in range(1, lanes)
            ]

        def from_energy(x, t):
            return lax.ppermute(x, "en", [((i + t) % en, i) for i in range(en)])

        def slices(wanted, earlier=()):
            def kernel(*refs):
                for i, (_, d) in enumerate(wanted):
                    for b in range(owned):
                        refs[len(wanted) + i][:, b] = refs[i][:, owner_at(d) * owned + b]

            arrays = after([x for x, _ in wanted], *earlier)
            return call(kernel, [block] * len(wanted), "slices", *arrays)

        def first(offsets_ref, couplings_ref, lesser_ref, greater_ref, packed_ref, *refs):
            packed_ref[...] = jnp.zeros_like(packed_ref)
            packed_ref[0, :e, :held] = offsets_ref[...].astype(jnp.float32)
            packed_ref[1, :e, :held] = couplings_ref[...]
            for i, d in enumerate(others):
                for b in range(owned):
                    refs[i][:, b] = greater_ref[:, owner_at(d) * owned + b]
                    refs[owners - 1 + i][:, b] = lesser_ref[:, owner_at(d) * owned + b]

        def join(*refs):
            for i, ref in enumerate(refs[:-1]):
                refs[-1][i] = ref[...]

        def weights(*refs):
            ins, outs = refs[:lanes], refs[lanes:]
            at = lax.axis_index("en")
            row = lax.broadcasted_iota(jnp.int32, (tile, LANES), 0)
            for i, t in enumerate([0] + shifts):
                away = (lax.rem(at + t, en) - at) * e
                for m in range(e):
                    apart = (away + m - row).astype(jnp.float32)
                    total = jnp.zeros((tile, LANES), jnp.float32)
                    for ref in ins:
                        for d in range(owners):
                            total += jnp.where(ref[d, 0] == apart, ref[d, 1], 0.0)
                    outs[i][m] = jnp.broadcast_to(
                        jnp.sum(total, axis=1, keepdims=True), (tile, LANES)
                    )

        def mix(tables, received, d, earlier):
            def kernel(*refs):
                table_refs, ins = refs[: len(tables)], refs[len(tables) : -1]
                for b in range(owned):
                    at_block = owner_at(d) * owned + b

                    def body(at):
                        totals = weighted(
                            table_refs, range(e), lambda t, m: ins[t][m, b if t else at_block, at, :]
                        )
                        for n in range(e):
                            refs[-1][n, b, at, :] = totals[n].astype(BF16)

                    chunks(r, body)

            return call(kernel, [block], "mix", *after(tables, *earlier), lesser_in, *received)[0]

        def greater_at(refs, m, d, b, at):
            return refs[d][m, b if d else owner_at(0) * owned + b, at, :]

        def partial_sums(table, rows, earlier):
            def kernel(table_ref, *refs):
                for d in range(owners):
                    for b in range(owned):

                        def body(at):
                            totals = weighted(
                                [table_ref], range(e), lambda t, m: greater_at(refs, m, d, b, at)
                            )
                            for n in range(e):
                                refs[owners + n][d, b, at, :] = totals[n].astype(BF16)

                        chunks(r, body)

            (table,) = after([table], *earlier)
            return call(kernel, [(owners,) + block[1:]] * e, "partial_sums", table, greater_in, *rows)

        def add_partial(n, table, rows, received, earlier):
            def kernel(table_ref, *refs):
                for d in range(owners):
                    for b in range(owned):

                        def body(at):
                            (total,) = weighted(
                                [table_ref], [n], lambda t, m: greater_at(refs, m, d, b, at)
                            )
                            for ref in refs[owners:-1]:
                                total = total + ref[d, b, at, :].astype(jnp.float32)
                            refs[-1][d, b, at, :] = total.astype(BF16)

                        chunks(r, body)

            (table,) = after([table], *earlier)
            return call(
                kernel, [(owners,) + block[1:]], "add_partial", table, greater_in, *rows, *received
            )[0]

        def product(energies, inverse_pieces, sigma, sigma_at, earlier):
            def kernel(*refs):
                a_in, s_in, outs = refs[:pieces], refs[pieces:-owners], refs[-owners:]
                spans = [pl.ds(pl.multiple_of(place_of(j) * r, r), r) for j in range(pieces)]
                for k, n in enumerate(energies):
                    for b in range(owned):
                        left = jnp.concatenate(
                            [
                                jnp.concatenate([a_in[i][n, b, :, at] for at in spans], axis=1)
                                for i in range(owners)
                            ],
                            axis=0,
                        )
                        stands = [sigma_at(n, j) for j in range(pieces)]
                        right = jnp.concatenate([s_in[i][lead, b] for i, lead in stands], axis=0)
                        half = jnp.dot(left, right, preferred_element_type=jnp.float32).astype(BF16)
                        full = lax.dot_general(
                            half,
                            jnp.concatenate([a[n, b] for a in a_in], axis=0),
                            (((1,), (1,)), ((), ())),
                            preferred_element_type=jnp.float32,
                        ).astype(BF16)
                        for i in range(owners):
                            for j, at in enumerate(spans):
                                outs[i][k, b, :, at] = full[i * r : (i + 1) * r, j * r : (j + 1) * r]

            shape = (len(energies),) + block[1:]
            return call(kernel, [shape] * owners, "product", *after(inverse_pieces, *earlier), *sigma)

        def back_to_rows(outs):
            return [outs[0]] + [to_owner(outs[d], owners - d) for d in others]

        def place(result, parts, earlier):
            def kernel(*refs):
                sems, ins, out = refs[-1], refs[: len(parts)], refs[-2]
                copies = [
                    pltpu.make_async_copy(
                        ins[i],
                        out.at[pl.ds(n, x.shape[0]), pl.ds(owner_at(d) * owned, owned)],
                        sems.at[i],
                    )
                    for i, (n, d, x) in enumerate(parts)
                ]
                for copy in copies:
                    copy.start()
                for copy in copies:
                    copy.wait()

            arrays = after([x for _, _, x in parts], *earlier)
            far = pl.BlockSpec(memory_space=pltpu.HBM)
            return pl.pallas_call(
                kernel,
                in_specs=[WHOLE] * len(parts) + [far] * (result is not None),
                out_specs=far,
                out_shape=jax.ShapeDtypeStruct((e, nb, r, o), BF16),
                scratch_shapes=[pltpu.SemaphoreType.DMA((len(parts),))],
                input_output_aliases={} if result is None else {len(parts): 0},
                compiler_params=PARAMS,
                cost_estimate=COST,
                name="place",
            )(*arrays, *([] if result is None else [result]))

        packed, *parts = call(
            first,
            [jax.ShapeDtypeStruct((2, tile, LANES), jnp.float32)] + [block] * (2 * len(others)),
            "first",
            offsets,
            couplings,
            lesser_in,
            greater_in,
        )
        greater_part, lesser_part = parts[: owners - 1], parts[owners - 1 :]
        packed_from = [packed] + [to_owner(packed, d) for d in others]
        lesser_from = [[from_energy(x, t) for t in shifts] for x in lesser_part]
        greater_part = after(greater_part, *packed_from)
        greater_rows = [to_owner(x, d) for d, x in zip(others, greater_part)]

        (column,) = call(
            join,
            [jax.ShapeDtypeStruct((owners, 2, tile, LANES), jnp.float32)],
            "join",
            *after(packed_from, *greater_part),
        )
        tables = call(
            weights,
            [jax.ShapeDtypeStruct((e, tile, LANES), jnp.float32)] * (1 + len(shifts)),
            "weights",
            column,
            *to_lanes(column),
        )
        tables_for = [
            lax.ppermute(table, "en", [(i, (i + t) % en) for i in range(en)])
            for t, table in zip(shifts, tables[1:])
        ]

        inverse_part = slices([(inverse, d) for d in others], tables)
        inverse_rows = [to_owner(x, d) for d, x in zip(others, inverse_part)]
        (lesser_own,) = slices([(lesser_in, 0)], inverse_part)
        lesser_from.insert(0, [from_energy(lesser_own, t) for t in shifts])

        last = [lesser_own]
        lesser_rows = [None]
        for d in others:
            last = [mix(tables, lesser_from[d], d, last)]
            lesser_rows.append(to_owner(last[0], d))
        (inverse_own,) = slices([(inverse, 0)], last)
        inverse_lanes = [to_lanes(inverse_own)]
        last = [inverse_own, *inverse_lanes[0]]
        received = [[] for _ in range(e)]
        for t, table in zip(shifts, tables_for):
            last = partial_sums(table, greater_rows, last)
            for n, part in enumerate(last):
                received[n].append(from_energy(part, t))
        inverse_lanes += [to_lanes(x) for x in inverse_rows]
        lesser_rows[0] = mix(tables, lesser_from[0], 0, [*last, *sum(inverse_lanes[1:], [])])
        lesser_lanes = [to_lanes(lesser_rows[0])]
        last = [lesser_rows[0], *lesser_lanes[0]]

        def in_order(rows, beside):
            return rows + [x[q] for q in range(lanes - 1) for x in beside]

        inverse_full = in_order([inverse_own] + inverse_rows, inverse_lanes)

        lesser_out = greater_out = None
        for n in range(e):
            sigma = add_partial(n, tables[0], greater_rows, received[n], last)
            outs = product(
                [n],
                inverse_full,
                [sigma] + to_lanes(sigma),
                lambda n, j: (j // owners, j % owners),
                [],
            )
            greater_back = back_to_rows(outs)
            last = outs
            if n == 0:
                lesser_lanes += [to_lanes(x) for x in lesser_rows[1:]]
                outs = product(
                    range(e), inverse_full, in_order(lesser_rows, lesser_lanes), lambda n, j: (j, n), last
                )
                lesser_back = back_to_rows(outs)
                last = outs
            if n < e - 1:
                greater_out = place(greater_out, [(n, d, x) for d, x in enumerate(greater_back)], [])
            else:
                lesser_out = place(None, [(0, d, x) for d, x in enumerate(lesser_back)], last)
                greater_out = place(greater_out, [(n, 0, outs[0])], [lesser_out])
                greater_out = place(greater_out, [(n, d, greater_back[d]) for d in others], [])

        return lesser_out, greater_out

    block, coupled = P("en", "blk", "ph", None), P("en", "ph")
    return jax.shard_map(
        on_device,
        mesh=mesh,
        in_specs=(block, block, block, coupled, coupled),
        out_specs=(block, block),
        check_vma=False,
    )
```

```python
import math

import jax
import jax.numpy as jnp
from jax import lax
from jax.experimental import pallas as pl
from jax.experimental.pallas import tpu as pltpu
from jax.sharding import PartitionSpec as P

MAXOFF = 9
BF16 = jnp.bfloat16
STEP = 16
LANES = 128
WHOLE = pl.BlockSpec(memory_space=pltpu.VMEM)
PARAMS = pltpu.CompilerParams(vmem_limit_bytes=12 * 1024 * 1024)
COST = pl.CostEstimate(flops=1, bytes_accessed=1, transcendentals=0)


def call(kernel, outs, name, *args):
    outs = [x if isinstance(x, jax.ShapeDtypeStruct) else jax.ShapeDtypeStruct(x, BF16) for x in outs]
    return pl.pallas_call(
        kernel,
        in_specs=[WHOLE] * len(args),
        out_specs=[WHOLE] * len(outs),
        out_shape=outs,
        compiler_params=PARAMS,
        cost_estimate=COST,
        name=name,
    )(*args)


def after(xs, *earlier):
    return lax.optimization_barrier((tuple(xs), earlier))[0]


def chunks(rows, body):
    @pl.loop(0, rows // STEP, unroll=math.gcd(rows // STEP, 4))
    def _(i):
        body(pl.ds(pl.multiple_of(i * STEP, STEP), STEP))


def weighted(tables, energies, load):
    totals = [None] * len(energies)
    for t, table in enumerate(tables):
        for m in range(table.shape[0]):
            g = load(t, m).astype(jnp.float32)
            for i, n in enumerate(energies):
                row = table[m, n : n + 1, :]
                term = jnp.concatenate([row] * (g.shape[1] // LANES), axis=1) * g
                totals[i] = term if totals[i] is None else totals[i] + term
    return totals


def solution(mesh):
    en, ph = mesh.shape["en"], mesh.shape["ph"]

    def on_device(lesser_in, greater_in, inverse, offsets, couplings):
        e, nb, r, o = lesser_in.shape
        held = offsets.shape[1]
        owners = math.gcd(nb, ph)
        lanes = ph // owners
        owned = nb // owners
        pieces = ph
        others = range(1, owners)
        reach = (MAXOFF + e - 1) // e
        shifts = [t for t in range(1, en) if t <= reach or en - t <= reach]
        block = (e, owned, r, o)
        tile = -(-e // 8) * 8
        tail = -(-4 * held // 16) * 16

        def owner_at(d):
            return lax.rem(lax.div(lax.axis_index("ph"), lanes) + d, owners)

        def place_of(j):
            at = lax.axis_index("ph")
            back = lax.rem(lax.div(at, lanes) + owners - j % owners, owners)
            return back * lanes + lax.rem(lax.rem(at, lanes) + lanes - j // owners, lanes)

        def to_owner(x, d):
            pairs = [(p, (p // lanes + d) % owners * lanes + p % lanes) for p in range(ph)]
            return lax.ppermute(x, "ph", pairs)

        def to_lanes(x):
            return [
                lax.ppermute(
                    x, "ph", [(p, p // lanes * lanes + (p % lanes + q) % lanes) for p in range(ph)]
                )
                for q in range(1, lanes)
            ]

        def from_energy(x, t):
            return lax.ppermute(x, "en", [((i + t) % en, i) for i in range(en)])

        def first(offsets_ref, couplings_ref, lesser_ref, greater_ref, inverse_ref, *refs):
            outs, (offsets_at, couplings_at, sems) = refs[:-3], refs[-3:]
            leads, inverses, lessers = (outs[i :: 3][: owners - 1] for i in range(3))
            copies = [(offsets_ref, offsets_at), (couplings_ref, couplings_at)]
            for i, d in enumerate(others):
                blocks = pl.ds(owner_at(d) * owned, owned)
                for n in range(e):
                    for b in range(owned):
                        to = leads[i].at[pl.ds((n * owned + b) * r, r)]
                        copies.append((greater_ref.at[n, owner_at(d) * owned + b], to))
                copies.append((lesser_ref.at[:, blocks], lessers[i]))
                copies.append((inverse_ref.at[:, blocks], inverses[i]))
            own = pl.ds(owner_at(0) * owned, owned)
            copies += [(inverse_ref.at[:, own], outs[-2]), (lesser_ref.at[:, own], outs[-1])]
            copies = [pltpu.make_async_copy(x, y, sems.at[i]) for i, (x, y) in enumerate(copies)]
            for copy in copies:
                copy.start()
            for copy in copies[:2]:
                copy.wait()
            rest = couplings_at[...]
            parts = [offsets_at[...].astype(jnp.float32)]
            for _ in range(3):
                parts.append(rest.astype(BF16).astype(jnp.float32))
                rest = rest - parts[-1]
            row = lax.broadcasted_iota(jnp.int32, (tail, e), 0)
            packed = jnp.zeros((tail, e), jnp.float32)
            for i, x in enumerate(parts):
                for k in range(held):
                    packed = jnp.where(row == i * held + k, x[k : k + 1, :], packed)
            packed = jnp.concatenate([packed, jnp.zeros((tail, LANES - e), jnp.float32)], axis=1)
            for out in leads:
                out[e * owned * r :, :LANES] = packed.astype(BF16)
                out[e * owned * r :, LANES:] = jnp.zeros((tail, o - LANES), BF16)
            for copy in copies[2:]:
                copy.wait()

        def join(*refs):
            for d in range(owners):
                refs[-1][d] = refs[d][e * owned * r :, :LANES]

        def from_hbm(kernel, outs, name, scratch, *args):
            far = pl.BlockSpec(memory_space=pltpu.HBM)
            return pl.pallas_call(
                kernel,
                in_specs=[far] * len(args),
                out_specs=[WHOLE] * len(outs),
                out_shape=[jax.ShapeDtypeStruct(x, BF16) for x in outs],
                scratch_shapes=scratch,
                compiler_params=PARAMS,
                cost_estimate=COST,
                name=name,
            )(*args)

        def weights(*refs):
            ins, outs = refs[:lanes], refs[lanes:]
            at = lax.axis_index("en")
            row = lax.broadcasted_iota(jnp.int32, (tile, LANES), 0)
            lane = lax.broadcasted_iota(jnp.int32, (tile, LANES), 1)
            pairs = []
            for ref in ins:
                for d in range(owners):
                    x = ref[d].astype(jnp.float32)
                    for k in range(held):
                        shift, *terms = [x[i * held + k : i * held + k + 1, :] for i in range(4)]
                        pairs.append((shift, terms[0] + terms[1] + terms[2]))
            for i, t in enumerate([0] + shifts):
                away = (lax.rem(at + t, en) - at) * e
                for m in range(e):
                    apart = (away + m - lane[:1]).astype(jnp.float32)
                    total = jnp.zeros((1, LANES), jnp.float32)
                    for shift, coupling in pairs:
                        total += jnp.where(shift == apart, coupling, 0.0)
                    spread = jnp.where(row == lane, jnp.broadcast_to(total, (tile, LANES)), 0.0)
                    outs[i][m] = jnp.broadcast_to(
                        jnp.sum(spread, axis=1, keepdims=True), (tile, LANES)
                    )

        def mix(tables, received, d, groups, earlier):
            def kernel(*refs):
                table_refs, refs = refs[: len(tables)], refs[len(tables) :]
                ins, outs = refs[: 1 + len(received)], refs[1 + len(received) :]
                for b in range(owned):
                    at_block = owner_at(d) * owned + b

                    def body(at):
                        totals = weighted(
                            table_refs, range(e), lambda t, m: ins[t][m, b if t else at_block, at, :]
                        )
                        for out, group in zip(outs, groups):
                            for i, n in enumerate(group):
                                out[i, b, at, :] = totals[n].astype(BF16)

                    chunks(r, body)

            shapes = [(len(group),) + block[1:] for group in groups]
            return call(kernel, shapes, "mix", *after(tables, *earlier), lesser_in, *received)

        def greater_at(refs, m, d, b, at):
            if not d:
                return refs[0][m, owner_at(0) * owned + b, at, :]
            return refs[d][pl.ds(pl.multiple_of((m * owned + b) * r + at.start, STEP), STEP), :]

        def partial_sums(table, rows, groups, earlier):
            def kernel(table_ref, *refs):
                for d in range(owners):
                    for b in range(owned):

                        def body(at):
                            totals = weighted(
                                [table_ref], range(e), lambda t, m: greater_at(refs, m, d, b, at)
                            )
                            for out, group in zip(refs[owners:], groups):
                                for i, n in enumerate(group):
                                    out[i, d, b, at, :] = totals[n].astype(BF16)

                        chunks(r, body)

            (table,) = after([table], *earlier)
            shapes = [(len(group), owners) + block[1:] for group in groups]
            return call(kernel, shapes, "partial_sums", table, greater_in, *rows)

        def add_partial(group, table, rows, received, earlier):
            def kernel(table_ref, *refs):
                for d in range(owners):
                    for b in range(owned):

                        def body(at):
                            totals = weighted(
                                [table_ref], group, lambda t, m: greater_at(refs, m, d, b, at)
                            )
                            for i in range(len(group)):
                                for ref in refs[owners:-owners]:
                                    totals[i] += ref[i, d, b, at, :].astype(jnp.float32)
                                refs[d - owners][i, b, at, :] = totals[i].astype(BF16)

                        chunks(r, body)

            (table,) = after([table], *earlier)
            shape = (len(group),) + block[1:]
            return call(kernel, [shape] * owners, "add_partial", table, greater_in, *rows, *received)

        def product(jobs, earlier):
            arrays = []
            for job in jobs:
                for x, _ in [*job[0], *job[1]]:
                    if not any(x is y for y in arrays):
                        arrays.append(x)
            where = {id(x): i for i, x in enumerate(arrays)}

            def kernel(*refs):
                outs = refs[-owners:]
                spans = [pl.ds(pl.multiple_of(place_of(j) * r, r), r) for j in range(pieces)]
                for k, job in enumerate(jobs):
                    a_in, s_in = ([(refs[where[id(x)]], index) for x, index in part] for part in job)
                    for b in range(owned):
                        left = jnp.concatenate(
                            [
                                jnp.concatenate([a[(*index, b, slice(None), at)] for at in spans], axis=1)
                                for a, index in a_in[:owners]
                            ],
                            axis=0,
                        )
                        right = jnp.concatenate([x[(*index, b)] for x, index in s_in], axis=0)
                        half = jnp.dot(left, right, preferred_element_type=jnp.float32).astype(BF16)
                        full = lax.dot_general(
                            half,
                            jnp.concatenate([a[(*index, b)] for a, index in a_in], axis=0),
                            (((1,), (1,)), ((), ())),
                            preferred_element_type=jnp.float32,
                        ).astype(BF16)
                        for i in range(owners):
                            for j, at in enumerate(spans):
                                outs[i][k, b, :, at] = full[i * r : (i + 1) * r, j * r : (j + 1) * r]

            shape = (len(jobs),) + block[1:]
            return call(kernel, [shape] * owners, "product", *after(arrays, *earlier))

        def back_to_rows(outs):
            return [outs[0]] + [to_owner(outs[d], owners - d) for d in others]

        def place(result, parts, earlier):
            arrays = []
            for _, _, x, _, _ in parts:
                if not any(x is y for y in arrays):
                    arrays.append(x)
            where = {id(x): i for i, x in enumerate(arrays)}

            def kernel(*refs):
                sems, out = refs[-1], refs[-2]
                copies = [
                    pltpu.make_async_copy(
                        refs[where[id(x)]].at[k],
                        out.at[n, pl.ds(owner_at(d) * owned, owned)],
                        sems.at[i],
                    )
                    for i, (n, d, x, k, _) in enumerate(parts)
                ]
                for copy in copies:
                    copy.start()
                for copy in copies:
                    copy.wait()

            far = pl.BlockSpec(memory_space=pltpu.HBM)
            return pl.pallas_call(
                kernel,
                in_specs=[WHOLE] * len(arrays) + [far] * (result is not None),
                out_specs=far,
                out_shape=jax.ShapeDtypeStruct((e, nb, r, o), BF16),
                scratch_shapes=[pltpu.SemaphoreType.DMA((len(parts),))],
                input_output_aliases={} if result is None else {len(arrays): 0},
                compiler_params=PARAMS,
                cost_estimate=COST,
                name="place",
            )(*after(arrays, *earlier), *([] if result is None else [result]))

        def in_order(own, rows, beside):
            return [own, *rows, *(x for q in range(lanes - 1) for x in [y[q] for y in beside])]

        def at(arrays, index):
            return [(x, index) for x in arrays]

        shapes = [(e * owned * r + tail, o), block, block]
        *parts, inverse_own, lesser_own = from_hbm(
            first,
            shapes * len(others) + [block] * 2,
            "first",
            [
                pltpu.VMEM((held, e), jnp.int32),
                pltpu.VMEM((held, e), jnp.float32),
                pltpu.SemaphoreType.DMA((4 + (e * owned + 2) * len(others),)),
            ],
            offsets.T,
            couplings.T,
            lesser_in,
            greater_in,
            inverse,
        )
        leads, inverses, lessers = (parts[i::3] for i in range(3))
        greater_rows = [to_owner(x, d) for d, x in zip(others, leads)]
        lesser_from = [[from_energy(x, t) for t in shifts] for x in lessers]
        inverse_rows = [to_owner(x, d) for d, x in zip(others, inverses)]

        (joined,) = call(join, [(owners, tail, LANES)], "join", leads[0], *greater_rows)
        tables = call(
            weights,
            [jax.ShapeDtypeStruct((e, tile, LANES), jnp.float32)] * (1 + len(shifts)),
            "weights",
            joined,
            *to_lanes(joined),
        )
        tables_for = [
            lax.ppermute(table, "en", [(i, (i + t) % en) for i in range(en)])
            for t, table in zip(shifts, tables[1:])
        ]
        lesser_own_from = [from_energy(lesser_own, t) for t in shifts]

        groups = [tuple(range(e - 1)), (e - 1,)] if e > 1 else [(0,)]
        singles = [(n,) for n in range(e)]
        lesser_rows = []
        last = []
        for d, came in zip(others, lesser_from):
            last = mix(tables, came, d, groups, last)
            lesser_rows.append([to_owner(x, d) for x in last])
        inverse_own_beside = to_lanes(inverse_own)
        last = [*last, *inverse_own_beside]
        received = [[] for _ in singles]
        for t, table in zip(shifts, tables_for):
            last = partial_sums(table, greater_rows, singles, last)
            for g, part in enumerate(last):
                received[g].append(from_energy(part, t))
        inverse_rows = list(after(inverse_rows, *last))
        inverse_rows_beside = [to_lanes(x) for x in inverse_rows]
        lesser_mixed = mix(tables, lesser_own_from, 0, groups, last)
        lesser_mixed_beside = [to_lanes(x) for x in lesser_mixed]
        last = lesser_mixed

        def find(groups, n):
            return next((g, group.index(n)) for g, group in enumerate(groups) if n in group)

        def inverse_at(n):
            beside = [at(inverse_own_beside, (n,)), *(at(x, (n,)) for x in inverse_rows_beside)]
            return in_order((inverse_own, (n,)), at(inverse_rows, (n,)), beside)

        def lesser_job(n):
            g, i = find(groups, n)
            h, k = find(groups, n)
            rows = [x[g] for x in lesser_rows]
            beside = [at(lesser_mixed_beside[h], (k,))] + [at(x[g], (i,)) for x in lesser_rows_beside]
            return inverse_at(n), in_order((lesser_mixed[h], (k,)), at(rows, (i,)), beside)

        lesser_rows_beside = [[to_lanes(x) for x in rows] for rows in lesser_rows]

        results = {"L": None, "G": None}
        waiting = {"L": [], "G": []}

        def put(kind, some, earlier):
            parts = [part for part in waiting[kind] if some(part)]
            waiting[kind] = [part for part in waiting[kind] if not some(part)]
            if parts:
                results[kind] = place(results[kind], parts, earlier)
                return [results[kind]]
            return earlier

        last = [*last, *[x[-1] for x in lesser_rows]]
        sigmas = {}
        steps = ["a0", "L0"]
        for n in range(1, e):
            steps.append(f"a{n}")
            if n == 2:
                steps.append("pL0")
            steps.append("L1+G0" if n == 1 else f"G{n - 1}")
        steps.append(f"G{e - 1}")
        for step in steps:
            if step[0] == "p":
                last = put(step[1], lambda part: len(step) < 3 or part[4] == int(step[2]), last)
                continue
            if step[0] == "a":
                g = int(step[1])
                group = singles[g]
                sigma = add_partial(group, tables[0], greater_rows, received[g], last)
                last = sigma
                sigmas[g] = (sigma, [to_lanes(x) for x in sigma])
                continue
            jobs, made = [], []
            for kind, g in step.split("+"):
                g = int(g)
                for i, n in enumerate(groups[g] if kind == "L" else singles[g]):
                    made.append((kind, n, g))
                    if kind == "L":
                        jobs.append(lesser_job(n))
                    else:
                        sigma, beside = sigmas[g]
                        beside = [at(x, (i,)) for x in beside]
                        jobs.append((inverse_at(n), in_order((sigma[0], (i,)), at(sigma[1:], (i,)), beside)))
            last = product(jobs, last)
            back = back_to_rows(last)
            for k, (kind, n, g) in enumerate(made):
                waiting[kind] += [(n, d, x, k, g) for d, x in enumerate(back)]
        last = put("L", lambda part: part[1] == 0, last)
        last = put("G", lambda part: part[1] == 0, last)
        for kind, g in [*(("L", g) for g in range(len(groups))), *(("G", n) for n in range(e))]:
            last = put(kind, lambda part: part[4] == g, last)
        lesser_out, greater_out = results["L"], results["G"]
        return lesser_out, greater_out

    block, coupled = P("en", "blk", "ph", None), P("en", "ph")
    return jax.shard_map(
        on_device,
        mesh=mesh,
        in_specs=(block, block, block, coupled, coupled),
        out_specs=(block, block),
        check_vma=False,
    )
```

```python
import math

import jax
import jax.numpy as jnp
from jax import lax
from jax.experimental import pallas as pl
from jax.experimental.pallas import tpu as pltpu
from jax.sharding import PartitionSpec as P

MAXOFF = 9
BF16 = jnp.bfloat16
STEP = 16
LANES = 128
WHOLE = pl.BlockSpec(memory_space=pltpu.VMEM)
PARAMS = pltpu.CompilerParams(vmem_limit_bytes=12 * 1024 * 1024)
COST = pl.CostEstimate(flops=1, bytes_accessed=1, transcendentals=0)


def call(kernel, outs, name, *args):
    outs = [x if isinstance(x, jax.ShapeDtypeStruct) else jax.ShapeDtypeStruct(x, BF16) for x in outs]
    return pl.pallas_call(
        kernel,
        in_specs=[WHOLE] * len(args),
        out_specs=[WHOLE] * len(outs),
        out_shape=outs,
        compiler_params=PARAMS,
        cost_estimate=COST,
        name=name,
    )(*args)


def after(xs, *earlier):
    return lax.optimization_barrier((tuple(xs), earlier))[0]


def chunks(rows, body):
    @pl.loop(0, rows // STEP, unroll=math.gcd(rows // STEP, 4))
    def _(i):
        body(pl.ds(pl.multiple_of(i * STEP, STEP), STEP))


def weighted(tables, energies, load):
    totals = [None] * len(energies)
    for t, table in enumerate(tables):
        for m in range(table.shape[0]):
            g = load(t, m).astype(jnp.float32)
            for i, n in enumerate(energies):
                row = table[m, n : n + 1, :]
                term = jnp.concatenate([row] * (g.shape[1] // LANES), axis=1) * g
                totals[i] = term if totals[i] is None else totals[i] + term
    return totals


def solution(mesh):
    en, ph = mesh.shape["en"], mesh.shape["ph"]

    def on_device(lesser_in, greater_in, inverse, offsets, couplings):
        e, nb, r, o = lesser_in.shape
        held = offsets.shape[1]
        owners = math.gcd(nb, ph)
        lanes = ph // owners
        owned = nb // owners
        pieces = ph
        others = range(1, owners)
        reach = (MAXOFF + e - 1) // e
        shifts = [t for t in range(1, en) if t <= reach or en - t <= reach]
        block = (e, owned, r, o)
        tile = -(-e // 8) * 8
        tail = -(-4 * held // 16) * 16

        def owner_at(d):
            return lax.rem(lax.div(lax.axis_index("ph"), lanes) + d, owners)

        def place_of(j):
            at = lax.axis_index("ph")
            back = lax.rem(lax.div(at, lanes) + owners - j % owners, owners)
            return back * lanes + lax.rem(lax.rem(at, lanes) + lanes - j // owners, lanes)

        def to_owner(x, d):
            pairs = [(p, (p // lanes + d) % owners * lanes + p % lanes) for p in range(ph)]
            return lax.ppermute(x, "ph", pairs)

        def to_lanes(x):
            return [
                lax.ppermute(
                    x, "ph", [(p, p // lanes * lanes + (p % lanes + q) % lanes) for p in range(ph)]
                )
                for q in range(1, lanes)
            ]

        def from_energy(x, t):
            return lax.ppermute(x, "en", [((i + t) % en, i) for i in range(en)])

        cuts = [(0, e - 1), (e - 1, 1)]

        def first(offsets_ref, couplings_ref, lesser_ref, greater_ref, inverse_ref, *refs):
            outs, (offsets_at, couplings_at, sems) = refs[:-3], refs[-3:]
            leads, inverses, greaters, lessers = (outs[i :: 4][: owners - 1] for i in range(4))
            copies = [(offsets_ref, offsets_at), (couplings_ref, couplings_at)]
            for i, d in enumerate(others):
                blocks = pl.ds(owner_at(d) * owned, owned)
                for n in range(e - 1):
                    for b in range(owned):
                        to = leads[i].at[pl.ds((n * owned + b) * r, r)]
                        copies.append((inverse_ref.at[n, owner_at(d) * owned + b], to))
                copies.append((lesser_ref.at[:, blocks], lessers[i]))
                copies.append((greater_ref.at[:, blocks], greaters[i]))
                copies.append((inverse_ref.at[pl.ds(e - 1, 1), blocks], inverses[i]))
            own = pl.ds(owner_at(0) * owned, owned)
            copies += [(inverse_ref.at[:, own], outs[-1 - len(cuts)]), *((lesser_ref.at[pl.ds(n, k), own], outs[-len(cuts) + i]) for i, (n, k) in enumerate(cuts))]
            copies = [pltpu.make_async_copy(x, y, sems.at[i]) for i, (x, y) in enumerate(copies)]
            for copy in copies:
                copy.start()
            for copy in copies[:2]:
                copy.wait()
            rest = couplings_at[...]
            parts = [offsets_at[...].astype(jnp.float32)]
            for _ in range(3):
                parts.append(rest.astype(BF16).astype(jnp.float32))
                rest = rest - parts[-1]
            row = lax.broadcasted_iota(jnp.int32, (tail, e), 0)
            packed = jnp.zeros((tail, e), jnp.float32)
            for i, x in enumerate(parts):
                for k in range(held):
                    packed = jnp.where(row == i * held + k, x[k : k + 1, :], packed)
            packed = jnp.concatenate([packed, jnp.zeros((tail, LANES - e), jnp.float32)], axis=1)
            for out in leads:
                out[(e - 1) * owned * r :, :LANES] = packed.astype(BF16)
                out[(e - 1) * owned * r :, LANES:] = jnp.zeros((tail, o - LANES), BF16)
            for copy in copies[2:]:
                copy.wait()

        def join(*refs):
            for d in range(owners):
                refs[owners][d] = refs[d][(e - 1) * owned * r :, :LANES]
            for d in others:
                for n in range(e - 1):
                    for b in range(owned):
                        at_row = (n * owned + b) * r
                        refs[owners + d][n, b] = refs[d][at_row : at_row + r]

        def from_hbm(kernel, outs, name, scratch, *args):
            far = pl.BlockSpec(memory_space=pltpu.HBM)
            return pl.pallas_call(
                kernel,
                in_specs=[far] * len(args),
                out_specs=[WHOLE] * len(outs),
                out_shape=[jax.ShapeDtypeStruct(x, BF16) for x in outs],
                scratch_shapes=scratch,
                compiler_params=pltpu.CompilerParams(vmem_limit_bytes=61 * 1024 * 1024),
                cost_estimate=COST,
                name=name,
            )(*args)

        def weights(*refs):
            ins, outs = refs[:lanes], refs[lanes:]
            at = lax.axis_index("en")
            row = lax.broadcasted_iota(jnp.int32, (tile, LANES), 0)
            lane = lax.broadcasted_iota(jnp.int32, (tile, LANES), 1)
            pairs = []
            for ref in ins:
                for d in range(owners):
                    x = ref[d].astype(jnp.float32)
                    for k in range(held):
                        shift, *terms = [x[i * held + k : i * held + k + 1, :] for i in range(4)]
                        pairs.append((shift, terms[0] + terms[1] + terms[2]))
            for i, t in enumerate([0] + shifts):
                away = (lax.rem(at + t, en) - at) * e
                for m in range(e):
                    apart = (away + m - lane[:1]).astype(jnp.float32)
                    total = jnp.zeros((1, LANES), jnp.float32)
                    for shift, coupling in pairs:
                        total += jnp.where(shift == apart, coupling, 0.0)
                    spread = jnp.where(row == lane, jnp.broadcast_to(total, (tile, LANES)), 0.0)
                    outs[i][m] = jnp.broadcast_to(
                        jnp.sum(spread, axis=1, keepdims=True), (tile, LANES)
                    )

        def mix(tables, received, d, groups, passengers, earlier):
            flat = [x for came in received for x in came]
            stands = [
                [(1 + i, k) for i, x in enumerate(flat) if any(x is y for y in came) for k in range(x.shape[0])]
                for came in received
            ]

            def load(ins, t, m, at_block, b, at):
                if not t:
                    return ins[0][m, at_block, at, :]
                i, k = stands[t - 1][m]
                return ins[i][k, b, at, :]

            def kernel(*refs):
                table_refs, refs = refs[: len(tables)], refs[len(tables) :]
                ins, refs = refs[: 1 + len(flat)], refs[1 + len(flat) :]
                outs = refs[len(passengers) :]
                for i in range(len(passengers)):
                    outs[-1][len(groups[-1]) + i] = refs[i][0]
                for b in range(owned):
                    at_block = owner_at(d) * owned + b

                    def body(at):
                        totals = weighted(
                            table_refs, range(e), lambda t, m: load(ins, t, m, at_block, b, at)
                        )
                        for out, group in zip(outs, groups):
                            for i, n in enumerate(group):
                                out[i, b, at, :] = totals[n].astype(BF16)

                    chunks(r, body)

            shapes = [(len(group),) + block[1:] for group in groups]
            shapes[-1] = (len(groups[-1]) + len(passengers),) + block[1:]
            return call(kernel, shapes, "mix", *after(tables, *earlier), lesser_in, *flat, *passengers)

        def greater_at(refs, m, d, b, at):
            return refs[d][m, b if d else owner_at(0) * owned + b, at, :]

        def partial_sums(table, rows, groups, earlier):
            def kernel(table_ref, *refs):
                for d in range(owners):
                    for b in range(owned):

                        def body(at):
                            totals = weighted(
                                [table_ref], range(e), lambda t, m: greater_at(refs, m, d, b, at)
                            )
                            for out, group in zip(refs[owners:], groups):
                                for i, n in enumerate(group):
                                    out[i, d, b, at, :] = totals[n].astype(BF16)

                        chunks(r, body)

            (table,) = after([table], *earlier)
            spare = [STEP] * (len(groups) - 1) + [0]
            shapes = [(len(group), owners, owned, r + x, o) for group, x in zip(groups, spare)]
            return call(kernel, shapes, "partial_sums", table, greater_in, *rows)

        def add_partial(group, table, rows, received, earlier):
            def kernel(table_ref, *refs):
                for d in range(owners):
                    for b in range(owned):

                        def body(at):
                            totals = weighted(
                                [table_ref], group, lambda t, m: greater_at(refs, m, d, b, at)
                            )
                            for i in range(len(group)):
                                for ref in refs[owners:-owners]:
                                    totals[i] += ref[i, d, b, at, :].astype(jnp.float32)
                                refs[d - owners][i, b, at, :] = totals[i].astype(BF16)

                        chunks(r, body)

            (table,) = after([table], *earlier)
            shape = (len(group),) + block[1:]
            return call(kernel, [shape] * owners, "add_partial", table, greater_in, *rows, *received)

        def product(jobs, earlier, pad=0):
            arrays = []
            for job in jobs:
                for x, _ in [*job[0], *job[1]]:
                    if not any(x is y for y in arrays):
                        arrays.append(x)
            where = {id(x): i for i, x in enumerate(arrays)}

            def kernel(*refs):
                outs = refs[-owners:]
                spans = [pl.ds(pl.multiple_of(place_of(j) * r, r), r) for j in range(pieces)]
                for k, job in enumerate(jobs):
                    a_in, s_in = ([(refs[where[id(x)]], index) for x, index in part] for part in job)
                    for b in range(owned):
                        left = jnp.concatenate(
                            [
                                jnp.concatenate([a[(*index, b, slice(None), at)] for at in spans], axis=1)
                                for a, index in a_in[:owners]
                            ],
                            axis=0,
                        )
                        right = jnp.concatenate([x[(*index, b)] for x, index in s_in], axis=0)
                        half = jnp.dot(left, right, preferred_element_type=jnp.float32).astype(BF16)
                        full = lax.dot_general(
                            half,
                            jnp.concatenate([a[(*index, b)] for a, index in a_in], axis=0),
                            (((1,), (1,)), ((), ())),
                            preferred_element_type=jnp.float32,
                        ).astype(BF16)
                        for i in range(owners):
                            for j, at in enumerate(spans):
                                outs[i][k, b, :r, at] = full[i * r : (i + 1) * r, j * r : (j + 1) * r]

            shapes = [(len(jobs), owned, r + pad if d else r, o) for d in range(owners)]
            return call(kernel, shapes, "product", *after(arrays, *earlier))

        def back_to_rows(outs):
            return [outs[0]] + [to_owner(outs[d], owners - d) for d in others]

        def place(result, parts, earlier):
            arrays = []
            for _, _, x, _, _ in parts:
                if not any(x is y for y in arrays):
                    arrays.append(x)
            where = {id(x): i for i, x in enumerate(arrays)}

            def kernel(*refs):
                sems, out = refs[-1], refs[-2]
                copies = [
                    pltpu.make_async_copy(
                        refs[where[id(x)]].at[k, :, pl.ds(0, r)],
                        out.at[n, pl.ds(owner_at(d) * owned, owned)],
                        sems.at[i],
                    )
                    for i, (n, d, x, k, _) in enumerate(parts)
                ]
                for copy in copies:
                    copy.start()
                for copy in copies:
                    copy.wait()

            far = pl.BlockSpec(memory_space=pltpu.HBM)
            return pl.pallas_call(
                kernel,
                in_specs=[WHOLE] * len(arrays) + [far] * (result is not None),
                out_specs=far,
                out_shape=jax.ShapeDtypeStruct((e, nb, r, o), BF16),
                scratch_shapes=[pltpu.SemaphoreType.DMA((len(parts),))],
                input_output_aliases={} if result is None else {len(arrays): 0},
                compiler_params=PARAMS,
                cost_estimate=COST,
                name="place",
            )(*after(arrays, *earlier), *([] if result is None else [result]))

        def in_order(own, rows, beside):
            return [own, *rows, *(x for q in range(lanes - 1) for x in [y[q] for y in beside])]

        def at(arrays, index):
            return [(x, index) for x in arrays]

        shapes = [((e - 1) * owned * r + tail, o), (1,) + block[1:], block, block]
        parts = from_hbm(
            first,
            shapes * len(others) + [block] + [(k,) + block[1:] for _, k in cuts],
            "first",
            [
                pltpu.VMEM((held, e), jnp.int32),
                pltpu.VMEM((held, e), jnp.float32),
                pltpu.SemaphoreType.DMA((3 + len(cuts) + ((e - 1) * owned + 3) * len(others),)),
            ],
            offsets.T,
            couplings.T,
            lesser_in,
            greater_in,
            inverse,
        )
        parts, (inverse_own, *lesser_own) = parts[: 4 * len(others)], parts[4 * len(others) :]
        leads, inverses, greaters, lessers = (parts[i::4] for i in range(4))
        leads_from = [to_owner(x, d) for d, x in zip(others, leads)]
        lesser_from = [[[from_energy(x, t)] for t in shifts] for x in lessers]
        greater_rows = [to_owner(x, d) for d, x in zip(others, greaters)]

        joined, *inverse_rows = call(
            join, [(owners, tail, LANES)] + [(e - 1,) + block[1:]] * len(others), "join", leads[0], *leads_from
        )
        tables = call(
            weights,
            [jax.ShapeDtypeStruct((e, tile, LANES), jnp.float32)] * (1 + len(shifts)),
            "weights",
            joined,
            *to_lanes(joined),
        )
        tables_for = [
            lax.ppermute(table, "en", [(i, (i + t) % en) for i in range(en)])
            for t, table in zip(shifts, tables[1:])
        ]
        lesser_own = after(lesser_own, *tables)
        lesser_own_from = [[from_energy(x, t) for x in lesser_own] for t in shifts]

        groups = [tuple(range(e - 1)), (e - 1,)]
        singles = [(n,) for n in range(e)]
        lesser_rows = []
        last = tables_for
        for i, (d, came) in enumerate(zip(others, lesser_from)):
            last = mix(tables, came, d, groups, [inverses[i]], last)
            lesser_rows.append([to_owner(x, d) for x in last])
        inverse_own_beside = to_lanes(inverse_own)
        last = [*last, *inverse_own_beside]
        received = [[] for _ in singles]
        for t, table in zip(shifts, tables_for):
            last = partial_sums(table, greater_rows, singles, last)
            for g, part in enumerate(last):
                received[g].append(from_energy(part, t))
        inverse_rows_beside = [to_lanes(x) for x in inverse_rows]
        lesser_mixed = mix(tables, lesser_own_from, 0, groups, [], last)
        lesser_mixed_beside = [to_lanes(x) for x in lesser_mixed]
        last = lesser_mixed

        def find(groups, n):
            return next((g, group.index(n)) for g, group in enumerate(groups) if n in group)

        def inverse_at(n):
            own = [at(inverse_own_beside, (n,))]
            if n < e - 1:
                beside = [at(x, (n,)) for x in inverse_rows_beside]
                return in_order((inverse_own, (n,)), at(inverse_rows, (n,)), own + beside)
            at_n = len(groups[-1])
            beside = [at(x[-1], (at_n,)) for x in lesser_rows_beside]
            return in_order((inverse_own, (n,)), at([x[-1] for x in lesser_rows], (at_n,)), own + beside)

        def lesser_job(n):
            g, i = find(groups, n)
            h, k = find(groups, n)
            rows = [x[g] for x in lesser_rows]
            beside = [at(lesser_mixed_beside[h], (k,))]
            for x in lesser_rows_beside:
                beside.append(at(x[g], (i,)))
            return inverse_at(n), in_order((lesser_mixed[h], (k,)), at(rows, (i,)), beside)

        lesser_rows_beside = [[*(to_lanes(x) for x in rows[:-1]), None] for rows in lesser_rows]

        results = {"L": None, "G": None}
        waiting = {"L": [], "G": []}

        def put(kind, some, earlier):
            parts = [part for part in waiting[kind] if some(part)]
            waiting[kind] = [part for part in waiting[kind] if not some(part)]
            if parts:
                results[kind] = place(results[kind], parts, earlier)
                return [results[kind]]
            return earlier

        sigmas = {}
        steps = ["L0", "a0", "L1+G0"]
        for n in range(1, e):
            steps.append(f"a{n}")
            steps.append("pL0" if n == 1 else f"G{n - 1}")
        steps.append(f"G{e - 1}")
        for step in steps:
            if step[0] == "p":
                last = put(step[1], lambda part: len(step) < 3 or part[4] == int(step[2]), last)
                continue
            if step[0] == "a":
                g = int(step[1])
                group = singles[g]
                sigma = add_partial(group, tables[0], greater_rows, received[g], last)
                last = sigma
                sigmas[g] = (sigma, [to_lanes(x) for x in sigma])
                continue
            jobs, made = [], []
            for kind, g in step.split("+"):
                g = int(g)
                for i, n in enumerate(groups[g] if kind == "L" else singles[g]):
                    made.append((kind, n, g))
                    if kind == "L":
                        jobs.append(lesser_job(n))
                    else:
                        sigma, beside = sigmas[g]
                        beside = [at(x, (i,)) for x in beside]
                        jobs.append((inverse_at(n), in_order((sigma[0], (i,)), at(sigma[1:], (i,)), beside)))
            last = product(jobs, last, STEP if step == "L0" else 0)
            back = back_to_rows(last)
            if step == "L0":
                for rows, beside in zip(lesser_rows, lesser_rows_beside):
                    rows[-1] = after([rows[-1]], *last)[0]
                    beside[-1] = to_lanes(rows[-1])
            for k, (kind, n, g) in enumerate(made):
                waiting[kind] += [(n, d, x, k, g) for d, x in enumerate(back)]
        last = put("L", lambda part: part[1] == 0, last)
        last = put("G", lambda part: part[1] == 0, last)
        for kind, g in [*(("L", g) for g in range(len(groups))), *(("G", n) for n in range(e))]:
            last = put(kind, lambda part: part[4] == g, last)
        lesser_out, greater_out = results["L"], results["G"]
        return lesser_out, greater_out

    block, coupled = P("en", "blk", "ph", None), P("en", "ph")
    return jax.shard_map(
        on_device,
        mesh=mesh,
        in_specs=(block, block, block, coupled, coupled),
        out_specs=(block, block),
        check_vma=False,
    )
```

```python
import math

import jax
import jax.numpy as jnp
from jax import lax
from jax.experimental import pallas as pl
from jax.experimental.pallas import tpu as pltpu
from jax.sharding import PartitionSpec as P

MAXOFF = 9
BF16 = jnp.bfloat16
STEP = 16
LANES = 128
WHOLE = pl.BlockSpec(memory_space=pltpu.VMEM)
PARAMS = pltpu.CompilerParams(vmem_limit_bytes=12 * 1024 * 1024)
COST = pl.CostEstimate(flops=1, bytes_accessed=1, transcendentals=0)


def call(kernel, outs, name, *args):
    outs = [x if isinstance(x, jax.ShapeDtypeStruct) else jax.ShapeDtypeStruct(x, BF16) for x in outs]
    return pl.pallas_call(
        kernel,
        in_specs=[WHOLE] * len(args),
        out_specs=[WHOLE] * len(outs),
        out_shape=outs,
        compiler_params=PARAMS,
        cost_estimate=COST,
        name=name,
    )(*args)


def after(xs, *earlier):
    return lax.optimization_barrier((tuple(xs), earlier))[0]


def chunks(rows, body):
    @pl.loop(0, rows // STEP, unroll=math.gcd(rows // STEP, 4))
    def _(i):
        body(pl.ds(pl.multiple_of(i * STEP, STEP), STEP))


def weighted(tables, energies, load):
    totals = [None] * len(energies)
    for t, table in enumerate(tables):
        for m in range(table.shape[0]):
            g = load(t, m).astype(jnp.float32)
            for i, n in enumerate(energies):
                row = table[m, n : n + 1, :]
                term = jnp.concatenate([row] * (g.shape[1] // LANES), axis=1) * g
                totals[i] = term if totals[i] is None else totals[i] + term
    return totals


def solution(mesh):
    en, ph = mesh.shape["en"], mesh.shape["ph"]

    def on_device(lesser_in, greater_in, inverse, offsets, couplings):
        e, nb, r, o = lesser_in.shape
        held = offsets.shape[1]
        owners = math.gcd(nb, ph)
        lanes = ph // owners
        owned = nb // owners
        pieces = ph
        others = range(1, owners)
        reach = (MAXOFF + e - 1) // e
        shifts = [t for t in range(1, en) if t <= reach or en - t <= reach]
        block = (e, owned, r, o)
        tile = -(-e // 8) * 8
        tail = -(-4 * held // 16) * 16

        def owner_at(d):
            return lax.rem(lax.div(lax.axis_index("ph"), lanes) + d, owners)

        def place_of(j):
            at = lax.axis_index("ph")
            back = lax.rem(lax.div(at, lanes) + owners - j % owners, owners)
            return back * lanes + lax.rem(lax.rem(at, lanes) + lanes - j // owners, lanes)

        def to_owner(x, d):
            pairs = [(p, (p // lanes + d) % owners * lanes + p % lanes) for p in range(ph)]
            return lax.ppermute(x, "ph", pairs)

        def to_lanes(x):
            return [
                lax.ppermute(
                    x, "ph", [(p, p // lanes * lanes + (p % lanes + q) % lanes) for p in range(ph)]
                )
                for q in range(1, lanes)
            ]

        def from_energy(x, t):
            return lax.ppermute(x, "en", [((i + t) % en, i) for i in range(en)])


        def lead(offsets_ref, couplings_ref, inverse_ref, *refs):
            leads, (offsets_at, couplings_at, sems) = refs[:-3], refs[-3:]
            copies = [(offsets_ref, offsets_at), (couplings_ref, couplings_at)]
            for i, d in enumerate(others):
                for n in range(e):
                    for b in range(owned):
                        to = leads[i].at[pl.ds((n * owned + b) * r, r)]
                        copies.append((inverse_ref.at[n, owner_at(d) * owned + b], to))
            copies = [pltpu.make_async_copy(x, y, sems.at[i]) for i, (x, y) in enumerate(copies)]
            for copy in copies:
                copy.start()
            for copy in copies[:2]:
                copy.wait()
            rest = couplings_at[...]
            parts = [offsets_at[...].astype(jnp.float32)]
            for _ in range(3):
                parts.append(rest.astype(BF16).astype(jnp.float32))
                rest = rest - parts[-1]
            row = lax.broadcasted_iota(jnp.int32, (tail, e), 0)
            packed = jnp.zeros((tail, e), jnp.float32)
            for i, x in enumerate(parts):
                for k in range(held):
                    packed = jnp.where(row == i * held + k, x[k : k + 1, :], packed)
            packed = jnp.concatenate([packed, jnp.zeros((tail, LANES - e), jnp.float32)], axis=1)
            for out in leads:
                out[e * owned * r :, :LANES] = packed.astype(BF16)
                out[e * owned * r :, LANES:] = jnp.zeros((tail, o - LANES), BF16)
            for copy in copies[2:]:
                copy.wait()

        def cut(wanted, earlier):
            arrays = after([x for x, *_ in wanted], *earlier)

            def kernel(*refs):
                ins, outs, sems = refs[: len(wanted)], refs[len(wanted) : -1], refs[-1]
                copies = []
                for i, (_, d, n, k) in enumerate(wanted):
                    at_d = pl.ds(owner_at(d) * owned, owned)
                    copies.append(pltpu.make_async_copy(ins[i].at[pl.ds(n, k), at_d], outs[i], sems.at[i]))
                for copy in copies:
                    copy.start()
                for copy in copies:
                    copy.wait()

            shapes = [(k,) + block[1:] for *_, k in wanted]
            return from_hbm(kernel, shapes, "cut", [pltpu.SemaphoreType.DMA((len(wanted),))], *arrays)

        def join(*refs):
            for d in range(owners):
                refs[owners][d] = refs[d][e * owned * r :, :LANES]
            for d in others:
                for n in range(e):
                    for b in range(owned):
                        at_row = (n * owned + b) * r
                        refs[owners + d][n, b] = refs[d][at_row : at_row + r]

        def from_hbm(kernel, outs, name, scratch, *args):
            far = pl.BlockSpec(memory_space=pltpu.HBM)
            return pl.pallas_call(
                kernel,
                in_specs=[far] * len(args),
                out_specs=[WHOLE] * len(outs),
                out_shape=[jax.ShapeDtypeStruct(x, BF16) for x in outs],
                scratch_shapes=scratch,
                compiler_params=pltpu.CompilerParams(vmem_limit_bytes=61 * 1024 * 1024),
                cost_estimate=COST,
                name=name,
            )(*args)

        def weights(*refs):
            ins, outs = refs[:lanes], refs[lanes:]
            at = lax.axis_index("en")
            row = lax.broadcasted_iota(jnp.int32, (tile, LANES), 0)
            lane = lax.broadcasted_iota(jnp.int32, (tile, LANES), 1)
            pairs = []
            for ref in ins:
                for d in range(owners):
                    x = ref[d].astype(jnp.float32)
                    for k in range(held):
                        shift, *terms = [x[i * held + k : i * held + k + 1, :] for i in range(4)]
                        pairs.append((shift, terms[0] + terms[1] + terms[2]))
            for i, t in enumerate([0] + shifts):
                away = (lax.rem(at + t, en) - at) * e
                for m in range(e):
                    apart = (away + m - lane[:1]).astype(jnp.float32)
                    total = jnp.zeros((1, LANES), jnp.float32)
                    for shift, coupling in pairs:
                        total += jnp.where(shift == apart, coupling, 0.0)
                    spread = jnp.where(row == lane, jnp.broadcast_to(total, (tile, LANES)), 0.0)
                    outs[i][m] = jnp.broadcast_to(
                        jnp.sum(spread, axis=1, keepdims=True), (tile, LANES)
                    )

        def mix(tables, received, d, groups, earlier):
            flat = [x for came in received for x in came]
            stands = [
                [(1 + i, k) for i, x in enumerate(flat) if any(x is y for y in came) for k in range(x.shape[0])]
                for came in received
            ]

            def load(ins, t, m, at_block, b, at):
                if not t:
                    return ins[0][m, at_block, at, :]
                i, k = stands[t - 1][m]
                return ins[i][k, b, at, :]

            def kernel(*refs):
                table_refs, refs = refs[: len(tables)], refs[len(tables) :]
                ins, outs = refs[: 1 + len(flat)], refs[1 + len(flat) :]
                for b in range(owned):
                    at_block = owner_at(d) * owned + b

                    def body(at):
                        totals = weighted(
                            table_refs, range(e), lambda t, m: load(ins, t, m, at_block, b, at)
                        )
                        for out, group in zip(outs, groups):
                            for i, n in enumerate(group):
                                out[i, b, at, :] = totals[n].astype(BF16)

                    chunks(r, body)

            shapes = [(len(group),) + block[1:] for group in groups]
            return call(kernel, shapes, "mix", *after(tables, *earlier), lesser_in, *flat)

        def greater_at(refs, m, d, b, at):
            return refs[d][m, b if d else owner_at(0) * owned + b, at, :]

        def partial_sums(table, rows, groups, earlier):
            def kernel(table_ref, *refs):
                for d in range(owners):
                    for b in range(owned):

                        def body(at):
                            totals = weighted(
                                [table_ref], range(e), lambda t, m: greater_at(refs, m, d, b, at)
                            )
                            for out, group in zip(refs[owners:], groups):
                                for i, n in enumerate(group):
                                    out[i, d, b, at, :] = totals[n].astype(BF16)

                        chunks(r, body)

            (table,) = after([table], *earlier)
            spare = [STEP] * (len(groups) - 1) + [0]
            shapes = [(len(group), owners, owned, r + x, o) for group, x in zip(groups, spare)]
            return call(kernel, shapes, "partial_sums", table, greater_in, *rows)

        def add_partial(group, table, rows, received, earlier):
            def kernel(table_ref, *refs):
                for d in range(owners):
                    for b in range(owned):

                        def body(at):
                            totals = weighted(
                                [table_ref], group, lambda t, m: greater_at(refs, m, d, b, at)
                            )
                            for i in range(len(group)):
                                for ref in refs[owners:-owners]:
                                    totals[i] += ref[i, d, b, at, :].astype(jnp.float32)
                                refs[d - owners][i, b, at, :] = totals[i].astype(BF16)

                        chunks(r, body)

            (table,) = after([table], *earlier)
            shape = (len(group),) + block[1:]
            return call(kernel, [shape] * owners, "add_partial", table, greater_in, *rows, *received)

        def product(jobs, earlier, pad=0):
            arrays = []
            for job in jobs:
                for x, _ in [*job[0], *job[1]]:
                    if not any(x is y for y in arrays):
                        arrays.append(x)
            where = {id(x): i for i, x in enumerate(arrays)}

            def kernel(*refs):
                outs = refs[-owners:]
                spans = [pl.ds(pl.multiple_of(place_of(j) * r, r), r) for j in range(pieces)]
                for k, job in enumerate(jobs):
                    a_in, s_in = ([(refs[where[id(x)]], index) for x, index in part] for part in job)
                    for b in range(owned):
                        left = jnp.concatenate(
                            [
                                jnp.concatenate([a[(*index, b, slice(0, r), at)] for at in spans], axis=1)
                                for a, index in a_in[:owners]
                            ],
                            axis=0,
                        )
                        right = jnp.concatenate([x[(*index, b, slice(0, r))] for x, index in s_in], axis=0)
                        half = jnp.dot(left, right, preferred_element_type=jnp.float32).astype(BF16)
                        full = lax.dot_general(
                            half,
                            jnp.concatenate([a[(*index, b, slice(0, r))] for a, index in a_in], axis=0),
                            (((1,), (1,)), ((), ())),
                            preferred_element_type=jnp.float32,
                        ).astype(BF16)
                        for i in range(owners):
                            for j, at in enumerate(spans):
                                outs[i][k, b, :r, at] = full[i * r : (i + 1) * r, j * r : (j + 1) * r]

            shapes = [(len(jobs), owned, r + pad if d else r, o) for d in range(owners)]
            return call(kernel, shapes, "product", *after(arrays, *earlier))

        def back_to_rows(outs):
            return [outs[0]] + [to_owner(outs[d], owners - d) for d in others]

        def place(result, parts, earlier):
            arrays = []
            for _, _, x, _, _ in parts:
                if not any(x is y for y in arrays):
                    arrays.append(x)
            where = {id(x): i for i, x in enumerate(arrays)}

            def kernel(*refs):
                sems, out = refs[-1], refs[-2]
                copies = [
                    pltpu.make_async_copy(
                        refs[where[id(x)]].at[k, :, pl.ds(0, r)],
                        out.at[n, pl.ds(owner_at(d) * owned, owned)],
                        sems.at[i],
                    )
                    for i, (n, d, x, k, _) in enumerate(parts)
                ]
                for copy in copies:
                    copy.start()
                for copy in copies:
                    copy.wait()

            far = pl.BlockSpec(memory_space=pltpu.HBM)
            return pl.pallas_call(
                kernel,
                in_specs=[WHOLE] * len(arrays) + [far] * (result is not None),
                out_specs=far,
                out_shape=jax.ShapeDtypeStruct((e, nb, r, o), BF16),
                scratch_shapes=[pltpu.SemaphoreType.DMA((len(parts),))],
                input_output_aliases={} if result is None else {len(arrays): 0},
                compiler_params=PARAMS,
                cost_estimate=COST,
                name="place",
            )(*after(arrays, *earlier), *([] if result is None else [result]))

        def in_order(own, rows, beside):
            return [own, *rows, *(x for q in range(lanes - 1) for x in [y[q] for y in beside])]

        def at(arrays, index):
            return [(x, index) for x in arrays]

        leads = from_hbm(
            lead,
            [(e * owned * r + tail, o)] * len(others),
            "lead",
            [
                pltpu.VMEM((held, e), jnp.int32),
                pltpu.VMEM((held, e), jnp.float32),
                pltpu.SemaphoreType.DMA((2 + e * owned * len(others),)),
            ],
            offsets.T,
            couplings.T,
            inverse,
        )
        leads_from = [to_owner(x, d) for d, x in zip(others, leads)]
        lessers = cut([(lesser_in, d, 0, e) for d in others], leads)
        lesser_from = [[[from_energy(x, t)] for t in shifts] for x in lessers]
        greaters = cut([(greater_in, d, 0, e) for d in others], lessers)
        greater_rows = [to_owner(x, d) for d, x in zip(others, greaters)]
        (inverse_own,) = cut([(inverse, 0, 0, e)], greaters)
        lesser_own = cut([(lesser_in, 0, n, k) for n, k in ((0, e - 1), (e - 1, 1))], [inverse_own])

        joined, *inverse_rows = call(
            join, [(owners, tail, LANES)] + [block] * len(others), "join", leads[0], *leads_from
        )
        tables = call(
            weights,
            [jax.ShapeDtypeStruct((e, tile, LANES), jnp.float32)] * (1 + len(shifts)),
            "weights",
            joined,
            *to_lanes(joined),
        )
        tables_for = [
            lax.ppermute(table, "en", [(i, (i + t) % en) for i in range(en)])
            for t, table in zip(shifts, tables[1:])
        ]
        lesser_own = after(lesser_own, *tables)
        lesser_own_from = [[from_energy(x, t) for x in lesser_own] for t in shifts]

        groups = [tuple(range(e - 1)), (e - 1,)]
        singles = [(n,) for n in range(e)]
        lesser_rows = []
        last = []
        for d, came in zip(others, lesser_from):
            last = mix(tables, came, d, groups, last)
            lesser_rows.append([to_owner(x, d) for x in last])
        inverse_own_beside = to_lanes(inverse_own)
        last = [*last, *inverse_own_beside]
        received = [[] for _ in singles]
        for t, table in zip(shifts, tables_for):
            last = partial_sums(table, greater_rows, singles, last)
            for g, part in enumerate(last):
                received[g].append(from_energy(part, t))
        inverse_rows_beside = [to_lanes(x) for x in inverse_rows]
        lesser_mixed = mix(tables, lesser_own_from, 0, groups, last)
        lesser_mixed_beside = [to_lanes(x) for x in lesser_mixed]
        last = lesser_mixed

        def find(groups, n):
            return next((g, group.index(n)) for g, group in enumerate(groups) if n in group)

        def inverse_at(n):
            beside = [at(inverse_own_beside, (n,)), *(at(x, (n,)) for x in inverse_rows_beside)]
            return in_order((inverse_own, (n,)), at(inverse_rows, (n,)), beside)

        def lesser_job(n):
            g, i = find(groups, n)
            h, k = find(groups, n)
            rows = [x[g] for x in lesser_rows]
            beside = [at(lesser_mixed_beside[h], (k,))]
            for x in lesser_rows_beside:
                beside.append(at(x[g], (i,)))
            return inverse_at(n), in_order((lesser_mixed[h], (k,)), at(rows, (i,)), beside)

        lesser_rows_beside = [[*(to_lanes(x) for x in rows[:-1]), None] for rows in lesser_rows]

        results = {"L": None, "G": None}
        waiting = {"L": [], "G": []}

        def put(kind, some, earlier):
            parts = [part for part in waiting[kind] if some(part)]
            waiting[kind] = [part for part in waiting[kind] if not some(part)]
            if parts:
                results[kind] = place(results[kind], parts, earlier)
                return [results[kind]]
            return earlier

        sigmas = {}
        steps = ["L0", "a0", "L1+G0"]
        for n in range(1, e):
            steps.append(f"a{n}")
            steps.append("pL0" if n == 1 else f"G{n - 1}")
        steps.append(f"G{e - 1}")
        for step in steps:
            if step[0] == "p":
                last = put(step[1], lambda part: len(step) < 3 or part[4] == int(step[2]), last)
                continue
            if step[0] == "a":
                g = int(step[1])
                group = singles[g]
                sigma = add_partial(group, tables[0], greater_rows, received[g], last)
                last = sigma
                sigmas[g] = (sigma, [to_lanes(x) for x in sigma])
                continue
            jobs, made = [], []
            for kind, g in step.split("+"):
                g = int(g)
                for i, n in enumerate(groups[g] if kind == "L" else singles[g]):
                    made.append((kind, n, g))
                    if kind == "L":
                        jobs.append(lesser_job(n))
                    else:
                        sigma, beside = sigmas[g]
                        beside = [at(x, (i,)) for x in beside]
                        jobs.append((inverse_at(n), in_order((sigma[0], (i,)), at(sigma[1:], (i,)), beside)))
            last = product(jobs, last, STEP if step == "L0" else 0)
            back = back_to_rows(last)
            if step == "L0":
                for rows, beside in zip(lesser_rows, lesser_rows_beside):
                    rows[-1] = after([rows[-1]], *last)[0]
                    beside[-1] = to_lanes(rows[-1])
            for k, (kind, n, g) in enumerate(made):
                waiting[kind] += [(n, d, x, k, g) for d, x in enumerate(back)]
        last = put("L", lambda part: part[1] == 0, last)
        last = put("G", lambda part: part[1] == 0, last)
        for kind, g in [*(("L", g) for g in range(len(groups))), *(("G", n) for n in range(e))]:
            last = put(kind, lambda part: part[4] == g, last)
        lesser_out, greater_out = results["L"], results["G"]
        return lesser_out, greater_out

    block, coupled = P("en", "blk", "ph", None), P("en", "ph")
    return jax.shard_map(
        on_device,
        mesh=mesh,
        in_specs=(block, block, block, coupled, coupled),
        out_specs=(block, block),
        check_vma=False,
    )
```

```python
import math

import jax
import jax.numpy as jnp
from jax import lax
from jax.experimental import pallas as pl
from jax.experimental.pallas import tpu as pltpu
from jax.sharding import PartitionSpec as P

MAXOFF = 9
BF16 = jnp.bfloat16
STEP = 16
LANES = 128
WHOLE = pl.BlockSpec(memory_space=pltpu.VMEM)
PARAMS = pltpu.CompilerParams(vmem_limit_bytes=12 * 1024 * 1024)
COST = pl.CostEstimate(flops=1, bytes_accessed=1, transcendentals=0)


def call(kernel, outs, name, *args):
    outs = [x if isinstance(x, jax.ShapeDtypeStruct) else jax.ShapeDtypeStruct(x, BF16) for x in outs]
    return pl.pallas_call(
        kernel,
        in_specs=[WHOLE] * len(args),
        out_specs=[WHOLE] * len(outs),
        out_shape=outs,
        compiler_params=PARAMS,
        cost_estimate=COST,
        name=name,
    )(*args)


def after(xs, *earlier):
    return lax.optimization_barrier((tuple(xs), earlier))[0]


def chunks(rows, body):
    @pl.loop(0, rows // STEP, unroll=math.gcd(rows // STEP, 4))
    def _(i):
        body(pl.ds(pl.multiple_of(i * STEP, STEP), STEP))


def weighted(tables, energies, load):
    totals = [None] * len(energies)
    for t, table in enumerate(tables):
        for m in range(table.shape[0]):
            g = load(t, m).astype(jnp.float32)
            for i, n in enumerate(energies):
                row = table[m, n : n + 1, :]
                term = jnp.concatenate([row] * (g.shape[1] // LANES), axis=1) * g
                totals[i] = term if totals[i] is None else totals[i] + term
    return totals


def solution(mesh):
    en, ph = mesh.shape["en"], mesh.shape["ph"]

    def on_device(lesser_in, greater_in, inverse, offsets, couplings):
        e, nb, r, o = lesser_in.shape
        held = offsets.shape[1]
        owners = math.gcd(nb, ph)
        lanes = ph // owners
        owned = nb // owners
        pieces = ph
        others = range(1, owners)
        reach = (MAXOFF + e - 1) // e
        shifts = [t for t in range(1, en) if t <= reach or en - t <= reach]
        block = (e, owned, r, o)
        tile = -(-e // 8) * 8
        tail = -(-4 * held // 16) * 16

        def owner_at(d):
            return lax.rem(lax.div(lax.axis_index("ph"), lanes) + d, owners)

        def place_of(j):
            at = lax.axis_index("ph")
            back = lax.rem(lax.div(at, lanes) + owners - j % owners, owners)
            return back * lanes + lax.rem(lax.rem(at, lanes) + lanes - j // owners, lanes)

        def to_owner(x, d):
            pairs = [(p, (p // lanes + d) % owners * lanes + p % lanes) for p in range(ph)]
            return lax.ppermute(x, "ph", pairs)

        def to_lanes(x):
            return [
                lax.ppermute(
                    x, "ph", [(p, p // lanes * lanes + (p % lanes + q) % lanes) for p in range(ph)]
                )
                for q in range(1, lanes)
            ]

        def from_energy(x, t):
            return lax.ppermute(x, "en", [((i + t) % en, i) for i in range(en)])


        def lead(offsets_ref, couplings_ref, inverse_ref, *refs):
            leads, (offsets_at, couplings_at, sems) = refs[:-3], refs[-3:]
            copies = [(offsets_ref, offsets_at), (couplings_ref, couplings_at)]
            for i, d in enumerate(others):
                for n in range(e):
                    for b in range(owned):
                        to = leads[i].at[pl.ds((n * owned + b) * r, r)]
                        copies.append((inverse_ref.at[n, owner_at(d) * owned + b], to))
            copies = [pltpu.make_async_copy(x, y, sems.at[i]) for i, (x, y) in enumerate(copies)]
            for copy in copies:
                copy.start()
            for copy in copies[:2]:
                copy.wait()
            rest = couplings_at[...]
            parts = [offsets_at[...].astype(jnp.float32)]
            for _ in range(3):
                parts.append(rest.astype(BF16).astype(jnp.float32))
                rest = rest - parts[-1]
            row = lax.broadcasted_iota(jnp.int32, (tail, e), 0)
            packed = jnp.zeros((tail, e), jnp.float32)
            for i, x in enumerate(parts):
                for k in range(held):
                    packed = jnp.where(row == i * held + k, x[k : k + 1, :], packed)
            packed = jnp.concatenate([packed, jnp.zeros((tail, LANES - e), jnp.float32)], axis=1)
            for out in leads:
                out[e * owned * r :, :LANES] = packed.astype(BF16)
                out[e * owned * r :, LANES:] = jnp.zeros((tail, o - LANES), BF16)
            for copy in copies[2:]:
                copy.wait()

        def cut(wanted, earlier):
            arrays = after([x for x, *_ in wanted], *earlier)

            def kernel(*refs):
                ins, outs, sems = refs[: len(wanted)], refs[len(wanted) : -1], refs[-1]
                copies = []
                for i, (_, d, n, k) in enumerate(wanted):
                    at_d = pl.ds(owner_at(d) * owned, owned)
                    copies.append(pltpu.make_async_copy(ins[i].at[pl.ds(n, k), at_d], outs[i], sems.at[i]))
                for copy in copies:
                    copy.start()
                for copy in copies:
                    copy.wait()

            shapes = [(k,) + block[1:] for *_, k in wanted]
            return from_hbm(kernel, shapes, "cut", [pltpu.SemaphoreType.DMA((len(wanted),))], *arrays)

        def join(*refs):
            for d in range(owners):
                refs[owners][d] = refs[d][e * owned * r :, :LANES]
            for d in others:
                for n in range(e):
                    for b in range(owned):
                        at_row = (n * owned + b) * r
                        refs[owners + d][n, b] = refs[d][at_row : at_row + r]

        def from_hbm(kernel, outs, name, scratch, *args):
            far = pl.BlockSpec(memory_space=pltpu.HBM)
            return pl.pallas_call(
                kernel,
                in_specs=[far] * len(args),
                out_specs=[WHOLE] * len(outs),
                out_shape=[jax.ShapeDtypeStruct(x, BF16) for x in outs],
                scratch_shapes=scratch,
                compiler_params=pltpu.CompilerParams(vmem_limit_bytes=61 * 1024 * 1024),
                cost_estimate=COST,
                name=name,
            )(*args)

        def weights(*refs):
            ins, outs = refs[:lanes], refs[lanes:]
            at = lax.axis_index("en")
            row = lax.broadcasted_iota(jnp.int32, (tile, LANES), 0)
            lane = lax.broadcasted_iota(jnp.int32, (tile, LANES), 1)
            pairs = []
            for ref in ins:
                for d in range(owners):
                    x = ref[d].astype(jnp.float32)
                    for k in range(held):
                        shift, *terms = [x[i * held + k : i * held + k + 1, :] for i in range(4)]
                        pairs.append((shift, terms[0] + terms[1] + terms[2]))
            for i, t in enumerate([0] + shifts):
                away = (lax.rem(at + t, en) - at) * e
                for m in range(e):
                    apart = (away + m - lane[:1]).astype(jnp.float32)
                    total = jnp.zeros((1, LANES), jnp.float32)
                    for shift, coupling in pairs:
                        total += jnp.where(shift == apart, coupling, 0.0)
                    spread = jnp.where(row == lane, jnp.broadcast_to(total, (tile, LANES)), 0.0)
                    outs[i][m] = jnp.broadcast_to(
                        jnp.sum(spread, axis=1, keepdims=True), (tile, LANES)
                    )

        def mix(tables, received, d, groups, earlier):
            flat = [x for came in received for x in came]
            stands = [
                [(1 + i, k) for i, x in enumerate(flat) if any(x is y for y in came) for k in range(x.shape[0])]
                for came in received
            ]

            def load(ins, t, m, at_block, b, at):
                if not t:
                    return ins[0][m, at_block, at, :]
                i, k = stands[t - 1][m]
                return ins[i][k, b, at, :]

            def kernel(*refs):
                table_refs, refs = refs[: len(tables)], refs[len(tables) :]
                ins, outs = refs[: 1 + len(flat)], refs[1 + len(flat) :]
                for b in range(owned):
                    at_block = owner_at(d) * owned + b

                    def body(at):
                        totals = weighted(
                            table_refs, range(e), lambda t, m: load(ins, t, m, at_block, b, at)
                        )
                        for out, group in zip(outs, groups):
                            for i, n in enumerate(group):
                                out[i, b, at, :] = totals[n].astype(BF16)

                    chunks(r, body)

            shapes = [(len(group),) + block[1:] for group in groups]
            return call(kernel, shapes, "mix", *after(tables, *earlier), lesser_in, *flat)

        def greater_at(refs, m, d, b, at):
            return refs[d][m, b if d else owner_at(0) * owned + b, at, :]

        def partial_sums(table, rows, groups, earlier):
            def kernel(table_ref, *refs):
                for d in range(owners):
                    for b in range(owned):

                        def body(at):
                            totals = weighted(
                                [table_ref], range(e), lambda t, m: greater_at(refs, m, d, b, at)
                            )
                            for out, group in zip(refs[owners:], groups):
                                for i, n in enumerate(group):
                                    out[i, d, b, at, :] = totals[n].astype(BF16)

                        chunks(r, body)

            (table,) = after([table], *earlier)
            spare = [STEP] + [0] * (len(groups) - 1)
            shapes = [(len(group), owners, owned, r + x, o) for group, x in zip(groups, spare)]
            return call(kernel, shapes, "partial_sums", table, greater_in, *rows)

        def add_partial(group, table, rows, received, earlier):
            def kernel(table_ref, *refs):
                for d in range(owners):
                    for b in range(owned):

                        def body(at):
                            totals = weighted(
                                [table_ref], group, lambda t, m: greater_at(refs, m, d, b, at)
                            )
                            for i in range(len(group)):
                                for ref in refs[owners:-owners]:
                                    totals[i] += ref[i, d, b, at, :].astype(jnp.float32)
                                refs[d - owners][i, b, at, :] = totals[i].astype(BF16)

                        chunks(r, body)

            (table,) = after([table], *earlier)
            shape = (len(group),) + block[1:]
            return call(kernel, [shape] * owners, "add_partial", table, greater_in, *rows, *received)

        def product(jobs, earlier):
            arrays = []
            for job in jobs:
                for x, _ in [*job[0], *job[1]]:
                    if not any(x is y for y in arrays):
                        arrays.append(x)
            where = {id(x): i for i, x in enumerate(arrays)}

            def kernel(*refs):
                outs = refs[-owners:]
                spans = [pl.ds(pl.multiple_of(place_of(j) * r, r), r) for j in range(pieces)]
                for k, job in enumerate(jobs):
                    a_in, s_in = ([(refs[where[id(x)]], index) for x, index in part] for part in job)
                    for b in range(owned):
                        left = jnp.concatenate(
                            [
                                jnp.concatenate([a[(*index, b, slice(None), at)] for at in spans], axis=1)
                                for a, index in a_in[:owners]
                            ],
                            axis=0,
                        )
                        right = jnp.concatenate([x[(*index, b)] for x, index in s_in], axis=0)
                        half = jnp.dot(left, right, preferred_element_type=jnp.float32).astype(BF16)
                        full = lax.dot_general(
                            half,
                            jnp.concatenate([a[(*index, b)] for a, index in a_in], axis=0),
                            (((1,), (1,)), ((), ())),
                            preferred_element_type=jnp.float32,
                        ).astype(BF16)
                        for i in range(owners):
                            for j, at in enumerate(spans):
                                outs[i][k, b, :, at] = full[i * r : (i + 1) * r, j * r : (j + 1) * r]

            shape = (len(jobs),) + block[1:]
            return call(kernel, [shape] * owners, "product", *after(arrays, *earlier))

        def back_to_rows(outs):
            return [outs[0]] + [to_owner(outs[d], owners - d) for d in others]

        def place(result, parts, earlier):
            arrays = []
            for _, _, x, _, _ in parts:
                if not any(x is y for y in arrays):
                    arrays.append(x)
            where = {id(x): i for i, x in enumerate(arrays)}

            def kernel(*refs):
                sems, out = refs[-1], refs[-2]
                copies = [
                    pltpu.make_async_copy(
                        refs[where[id(x)]].at[k],
                        out.at[n, pl.ds(owner_at(d) * owned, owned)],
                        sems.at[i],
                    )
                    for i, (n, d, x, k, _) in enumerate(parts)
                ]
                for copy in copies:
                    copy.start()
                for copy in copies:
                    copy.wait()

            far = pl.BlockSpec(memory_space=pltpu.HBM)
            return pl.pallas_call(
                kernel,
                in_specs=[WHOLE] * len(arrays) + [far] * (result is not None),
                out_specs=far,
                out_shape=jax.ShapeDtypeStruct((e, nb, r, o), BF16),
                scratch_shapes=[pltpu.SemaphoreType.DMA((len(parts),))],
                input_output_aliases={} if result is None else {len(arrays): 0},
                compiler_params=PARAMS,
                cost_estimate=COST,
                name="place",
            )(*after(arrays, *earlier), *([] if result is None else [result]))

        def in_order(own, rows, beside):
            return [own, *rows, *(x for q in range(lanes - 1) for x in [y[q] for y in beside])]

        def at(arrays, index):
            return [(x, index) for x in arrays]

        leads = from_hbm(
            lead,
            [(e * owned * r + tail, o)] * len(others),
            "lead",
            [
                pltpu.VMEM((held, e), jnp.int32),
                pltpu.VMEM((held, e), jnp.float32),
                pltpu.SemaphoreType.DMA((2 + e * owned * len(others),)),
            ],
            offsets.T,
            couplings.T,
            inverse,
        )
        leads_from = [to_owner(x, d) for d, x in zip(others, leads)]
        lessers = cut([(lesser_in, d, 0, e) for d in others], leads)
        lesser_from = [[[from_energy(x, t)] for t in shifts] for x in lessers]
        rest = cut(
            [*((greater_in, d, 0, e) for d in others), (inverse, 0, 0, e), (lesser_in, 0, 0, e - 1), (lesser_in, 0, e - 1, 1)],
            lessers,
        )
        greaters, inverse_own, lesser_own = rest[: owners - 1], rest[owners - 1], rest[owners:]
        greater_rows = [to_owner(x, d) for d, x in zip(others, greaters)]

        joined, *inverse_rows = call(
            join, [(owners, tail, LANES)] + [block] * len(others), "join", leads[0], *leads_from
        )
        tables = call(
            weights,
            [jax.ShapeDtypeStruct((e, tile, LANES), jnp.float32)] * (1 + len(shifts)),
            "weights",
            joined,
            *to_lanes(joined),
        )
        tables_for = [
            lax.ppermute(table, "en", [(i, (i + t) % en) for i in range(en)])
            for t, table in zip(shifts, tables[1:])
        ]
        lesser_own = after(lesser_own, *tables)
        lesser_own_from = [[from_energy(x, t) for x in lesser_own] for t in shifts]

        groups = [tuple(range(e - 1)), (e - 1,)]
        singles = [(n,) for n in range(e)]
        lesser_rows = []
        last = []
        for d, came in zip(others, lesser_from):
            last = mix(tables, came, d, groups, last)
            lesser_rows.append([to_owner(x, d) for x in last])
        inverse_own_beside = to_lanes(inverse_own)
        last = [*last, *inverse_own_beside]
        received = [[] for _ in singles]
        for t, table in zip(shifts, tables_for):
            last = partial_sums(table, greater_rows, singles, last)
            for g, part in enumerate(last):
                received[g].append(from_energy(part, t))
        inverse_rows_beside = [to_lanes(x) for x in inverse_rows]
        lesser_mixed = mix(tables, lesser_own_from, 0, groups, last)
        lesser_mixed_beside = [to_lanes(x) for x in lesser_mixed]
        last = lesser_mixed

        def find(groups, n):
            return next((g, group.index(n)) for g, group in enumerate(groups) if n in group)

        def inverse_at(n):
            beside = [at(inverse_own_beside, (n,)), *(at(x, (n,)) for x in inverse_rows_beside)]
            return in_order((inverse_own, (n,)), at(inverse_rows, (n,)), beside)

        def lesser_job(n):
            g, i = find(groups, n)
            h, k = find(groups, n)
            rows = [x[g] for x in lesser_rows]
            beside = [at(lesser_mixed_beside[h], (k,))]
            for x in lesser_rows_beside:
                beside.append(at(x[g], (i,)))
            return inverse_at(n), in_order((lesser_mixed[h], (k,)), at(rows, (i,)), beside)

        lesser_rows_beside = [[*(to_lanes(x) for x in rows[:-1]), None] for rows in lesser_rows]

        results = {"L": None, "G": None}
        waiting = {"L": [], "G": []}

        def put(kind, some, earlier):
            parts = [part for part in waiting[kind] if some(part)]
            waiting[kind] = [part for part in waiting[kind] if not some(part)]
            if parts:
                results[kind] = place(results[kind], parts, earlier)
                return [results[kind]]
            return earlier

        sigmas = {}
        steps = ["L0", "a0", "L1+G0"]
        for n in range(1, e):
            steps += [f"a{n}", "pL0", f"G{n}"] if n == 1 else [f"a{n}", f"G{n}"]
        for step in steps:
            if step[0] == "p":
                last = put(step[1], lambda part: len(step) < 3 or part[4] == int(step[2]), last)
                continue
            if step[0] == "a":
                g = int(step[1])
                group = singles[g]
                sigma = add_partial(group, tables[0], greater_rows, received[g], last)
                last = sigma
                sigmas[g] = (sigma, [to_lanes(x) for x in sigma])
                continue
            jobs, made = [], []
            for kind, g in step.split("+"):
                g = int(g)
                for i, n in enumerate(groups[g] if kind == "L" else singles[g]):
                    made.append((kind, n, g))
                    if kind == "L":
                        jobs.append(lesser_job(n))
                    else:
                        sigma, beside = sigmas[g]
                        beside = [at(x, (i,)) for x in beside]
                        jobs.append((inverse_at(n), in_order((sigma[0], (i,)), at(sigma[1:], (i,)), beside)))
            last = product(jobs, last)
            back = back_to_rows(last)
            if step == "L0":
                for rows, beside in zip(lesser_rows, lesser_rows_beside):
                    rows[-1] = after([rows[-1]], *last)[0]
                    beside[-1] = to_lanes(rows[-1])
            for k, (kind, n, g) in enumerate(made):
                waiting[kind] += [(n, d, x, k, g) for d, x in enumerate(back)]
        last = put("L", lambda part: part[1] == 0, last)
        last = put("G", lambda part: part[1] == 0, last)
        for kind, g in [*(("L", g) for g in range(len(groups))), *(("G", n) for n in range(e))]:
            last = put(kind, lambda part: part[4] == g, last)
        lesser_out, greater_out = results["L"], results["G"]
        return lesser_out, greater_out

    block, coupled = P("en", "blk", "ph", None), P("en", "ph")
    return jax.shard_map(
        on_device,
        mesh=mesh,
        in_specs=(block, block, block, coupled, coupled),
        out_specs=(block, block),
        check_vma=False,
    )
```

```python
import math

import jax
import jax.numpy as jnp
from jax import lax
from jax.experimental import pallas as pl
from jax.experimental.pallas import tpu as pltpu
from jax.sharding import PartitionSpec as P

MAXOFF = 9
BF16 = jnp.bfloat16
STEP = 16
LANES = 128
WHOLE = pl.BlockSpec(memory_space=pltpu.VMEM)
PARAMS = pltpu.CompilerParams(vmem_limit_bytes=12 * 1024 * 1024)
COST = pl.CostEstimate(flops=1, bytes_accessed=1, transcendentals=0)


def call(kernel, outs, name, *args):
    outs = [x if isinstance(x, jax.ShapeDtypeStruct) else jax.ShapeDtypeStruct(x, BF16) for x in outs]
    return pl.pallas_call(
        kernel,
        in_specs=[WHOLE] * len(args),
        out_specs=[WHOLE] * len(outs),
        out_shape=outs,
        compiler_params=PARAMS,
        cost_estimate=COST,
        name=name,
    )(*args)


def after(xs, *earlier):
    return lax.optimization_barrier((tuple(xs), earlier))[0]


def chunks(rows, body):
    @pl.loop(0, rows // STEP, unroll=math.gcd(rows // STEP, 4))
    def _(i):
        body(pl.ds(pl.multiple_of(i * STEP, STEP), STEP))


def weighted(tables, energies, load):
    totals = [None] * len(energies)
    for t, table in enumerate(tables):
        for m in range(table.shape[0]):
            g = load(t, m).astype(jnp.float32)
            for i, n in enumerate(energies):
                row = table[m, n : n + 1, :]
                term = jnp.concatenate([row] * (g.shape[1] // LANES), axis=1) * g
                totals[i] = term if totals[i] is None else totals[i] + term
    return totals


def solution(mesh):
    en, ph = mesh.shape["en"], mesh.shape["ph"]

    def on_device(lesser_in, greater_in, inverse, offsets, couplings):
        e, nb, r, o = lesser_in.shape
        held = offsets.shape[1]
        owners = math.gcd(nb, ph)
        lanes = ph // owners
        owned = nb // owners
        pieces = ph
        others = range(1, owners)
        reach = (MAXOFF + e - 1) // e
        shifts = [t for t in range(1, en) if t <= reach or en - t <= reach]
        block = (e, owned, r, o)
        tile = -(-e // 8) * 8
        tail = -(-4 * held // 16) * 16

        def owner_at(d):
            return lax.rem(lax.div(lax.axis_index("ph"), lanes) + d, owners)

        def place_of(j):
            at = lax.axis_index("ph")
            back = lax.rem(lax.div(at, lanes) + owners - j % owners, owners)
            return back * lanes + lax.rem(lax.rem(at, lanes) + lanes - j // owners, lanes)

        def to_owner(x, d):
            pairs = [(p, (p // lanes + d) % owners * lanes + p % lanes) for p in range(ph)]
            return lax.ppermute(x, "ph", pairs)

        def to_lanes(x):
            return [
                lax.ppermute(
                    x, "ph", [(p, p // lanes * lanes + (p % lanes + q) % lanes) for p in range(ph)]
                )
                for q in range(1, lanes)
            ]

        def from_energy(x, t):
            return lax.ppermute(x, "en", [((i + t) % en, i) for i in range(en)])


        def lead(offsets_ref, couplings_ref, inverse_ref, *refs):
            leads, (offsets_at, couplings_at, sems) = refs[:-3], refs[-3:]
            copies = [(offsets_ref, offsets_at), (couplings_ref, couplings_at)]
            for i, d in enumerate(others):
                for n in range(e):
                    for b in range(owned):
                        to = leads[i].at[pl.ds((n * owned + b) * r, r)]
                        copies.append((inverse_ref.at[n, owner_at(d) * owned + b], to))
            copies = [pltpu.make_async_copy(x, y, sems.at[i]) for i, (x, y) in enumerate(copies)]
            for copy in copies:
                copy.start()
            for copy in copies[:2]:
                copy.wait()
            rest = couplings_at[...]
            parts = [offsets_at[...].astype(jnp.float32)]
            for _ in range(3):
                parts.append(rest.astype(BF16).astype(jnp.float32))
                rest = rest - parts[-1]
            row = lax.broadcasted_iota(jnp.int32, (tail, e), 0)
            packed = jnp.zeros((tail, e), jnp.float32)
            for i, x in enumerate(parts):
                for k in range(held):
                    packed = jnp.where(row == i * held + k, x[k : k + 1, :], packed)
            packed = jnp.concatenate([packed, jnp.zeros((tail, LANES - e), jnp.float32)], axis=1)
            for out in leads:
                out[e * owned * r :, :LANES] = packed.astype(BF16)
                out[e * owned * r :, LANES:] = jnp.zeros((tail, o - LANES), BF16)
            for copy in copies[2:]:
                copy.wait()

        def cut(wanted, earlier):
            arrays = after([x for x, *_ in wanted], *earlier)

            def kernel(*refs):
                for i, (_, d, n, k) in enumerate(wanted):
                    for b in range(owned):
                        refs[len(wanted) + i][:, b] = refs[i][n : n + k, owner_at(d) * owned + b]

            return call(kernel, [(k,) + block[1:] for *_, k in wanted], "cut", *arrays)

        def join(*refs):
            for d in range(owners):
                refs[owners][d] = refs[d][e * owned * r :, :LANES]
            for d in others:
                for n in range(e):
                    for b in range(owned):
                        at_row = (n * owned + b) * r
                        refs[owners + d][n, b] = refs[d][at_row : at_row + r]

        def from_hbm(kernel, outs, name, scratch, *args):
            far = pl.BlockSpec(memory_space=pltpu.HBM)
            return pl.pallas_call(
                kernel,
                in_specs=[far] * len(args),
                out_specs=[WHOLE] * len(outs),
                out_shape=[jax.ShapeDtypeStruct(x, BF16) for x in outs],
                scratch_shapes=scratch,
                compiler_params=pltpu.CompilerParams(vmem_limit_bytes=61 * 1024 * 1024),
                cost_estimate=COST,
                name=name,
            )(*args)

        def weights(*refs):
            ins, outs = refs[:lanes], refs[lanes:]
            at = lax.axis_index("en")
            row = lax.broadcasted_iota(jnp.int32, (tile, LANES), 0)
            lane = lax.broadcasted_iota(jnp.int32, (tile, LANES), 1)
            pairs = []
            for ref in ins:
                for d in range(owners):
                    x = ref[d].astype(jnp.float32)
                    for k in range(held):
                        shift, *terms = [x[i * held + k : i * held + k + 1, :] for i in range(4)]
                        pairs.append((shift, terms[0] + terms[1] + terms[2]))
            for i, t in enumerate([0] + shifts):
                away = (lax.rem(at + t, en) - at) * e
                for m in range(e):
                    apart = (away + m - lane[:1]).astype(jnp.float32)
                    total = jnp.zeros((1, LANES), jnp.float32)
                    for shift, coupling in pairs:
                        total += jnp.where(shift == apart, coupling, 0.0)
                    spread = jnp.where(row == lane, jnp.broadcast_to(total, (tile, LANES)), 0.0)
                    outs[i][m] = jnp.broadcast_to(
                        jnp.sum(spread, axis=1, keepdims=True), (tile, LANES)
                    )

        def mix(tables, received, d, groups, earlier):
            flat = [x for came in received for x in came]
            stands = [
                [(1 + i, k) for i, x in enumerate(flat) if any(x is y for y in came) for k in range(x.shape[0])]
                for came in received
            ]

            def load(ins, t, m, at_block, b, at):
                if not t:
                    return ins[0][m, at_block, at, :]
                i, k = stands[t - 1][m]
                return ins[i][k, b, at, :]

            def kernel(*refs):
                table_refs, refs = refs[: len(tables)], refs[len(tables) :]
                ins, outs = refs[: 1 + len(flat)], refs[1 + len(flat) :]
                for b in range(owned):
                    at_block = owner_at(d) * owned + b

                    def body(at):
                        totals = weighted(
                            table_refs, range(e), lambda t, m: load(ins, t, m, at_block, b, at)
                        )
                        for out, group in zip(outs, groups):
                            for i, n in enumerate(group):
                                out[i, b, at, :] = totals[n].astype(BF16)

                    chunks(r, body)

            shapes = [(len(group),) + block[1:] for group in groups]
            return call(kernel, shapes, "mix", *after(tables, *earlier), lesser_in, *flat)

        def greater_at(refs, m, d, b, at):
            return refs[d][m, b if d else owner_at(0) * owned + b, at, :]

        def partial_sums(table, rows, groups, earlier):
            def kernel(table_ref, *refs):
                for d in range(owners):
                    for b in range(owned):

                        def body(at):
                            totals = weighted(
                                [table_ref], range(e), lambda t, m: greater_at(refs, m, d, b, at)
                            )
                            for out, group in zip(refs[owners:], groups):
                                for i, n in enumerate(group):
                                    out[i, d, b, at, :] = totals[n].astype(BF16)

                        chunks(r, body)

            (table,) = after([table], *earlier)
            spare = [STEP] * (len(groups) - 1) + [0]
            shapes = [(len(group), owners, owned, r + x, o) for group, x in zip(groups, spare)]
            return call(kernel, shapes, "partial_sums", table, greater_in, *rows)

        def add_partial(group, table, rows, received, earlier):
            def kernel(table_ref, *refs):
                for d in range(owners):
                    for b in range(owned):

                        def body(at):
                            totals = weighted(
                                [table_ref], group, lambda t, m: greater_at(refs, m, d, b, at)
                            )
                            for i in range(len(group)):
                                for ref in refs[owners:-owners]:
                                    totals[i] += ref[i, d, b, at, :].astype(jnp.float32)
                                refs[d - owners][i, b, at, :] = totals[i].astype(BF16)

                        chunks(r, body)

            (table,) = after([table], *earlier)
            shape = (len(group),) + block[1:]
            return call(kernel, [shape] * owners, "add_partial", table, greater_in, *rows, *received)

        def product(jobs, earlier, pad=0):
            arrays = []
            for job in jobs:
                for x, _ in [*job[0], *job[1]]:
                    if not any(x is y for y in arrays):
                        arrays.append(x)
            where = {id(x): i for i, x in enumerate(arrays)}

            def kernel(*refs):
                outs = refs[-owners:]
                spans = [pl.ds(pl.multiple_of(place_of(j) * r, r), r) for j in range(pieces)]
                for k, job in enumerate(jobs):
                    a_in, s_in = ([(refs[where[id(x)]], index) for x, index in part] for part in job)
                    for b in range(owned):
                        left = jnp.concatenate(
                            [
                                jnp.concatenate([a[(*index, b, slice(None), at)] for at in spans], axis=1)
                                for a, index in a_in[:owners]
                            ],
                            axis=0,
                        )
                        right = jnp.concatenate([x[(*index, b)] for x, index in s_in], axis=0)
                        half = jnp.dot(left, right, preferred_element_type=jnp.float32).astype(BF16)
                        full = lax.dot_general(
                            half,
                            jnp.concatenate([a[(*index, b)] for a, index in a_in], axis=0),
                            (((1,), (1,)), ((), ())),
                            preferred_element_type=jnp.float32,
                        ).astype(BF16)
                        for i in range(owners):
                            for j, at in enumerate(spans):
                                outs[i][k, b, :r, at] = full[i * r : (i + 1) * r, j * r : (j + 1) * r]

            shapes = [(len(jobs), owned, r + pad if d else r, o) for d in range(owners)]
            return call(kernel, shapes, "product", *after(arrays, *earlier))

        def back_to_rows(outs):
            return [outs[0]] + [to_owner(outs[d], owners - d) for d in others]

        def place(result, parts, earlier):
            arrays = []
            for _, _, x, _, _ in parts:
                if not any(x is y for y in arrays):
                    arrays.append(x)
            where = {id(x): i for i, x in enumerate(arrays)}

            def kernel(*refs):
                sems, out = refs[-1], refs[-2]
                copies = [
                    pltpu.make_async_copy(
                        refs[where[id(x)]].at[k, :, pl.ds(0, r)],
                        out.at[n, pl.ds(owner_at(d) * owned, owned)],
                        sems.at[i],
                    )
                    for i, (n, d, x, k, _) in enumerate(parts)
                ]
                for copy in copies:
                    copy.start()
                for copy in copies:
                    copy.wait()

            far = pl.BlockSpec(memory_space=pltpu.HBM)
            return pl.pallas_call(
                kernel,
                in_specs=[WHOLE] * len(arrays) + [far] * (result is not None),
                out_specs=far,
                out_shape=jax.ShapeDtypeStruct((e, nb, r, o), BF16),
                scratch_shapes=[pltpu.SemaphoreType.DMA((len(parts),))],
                input_output_aliases={} if result is None else {len(arrays): 0},
                compiler_params=PARAMS,
                cost_estimate=COST,
                name="place",
            )(*after(arrays, *earlier), *([] if result is None else [result]))

        def in_order(own, rows, beside):
            return [own, *rows, *(x for q in range(lanes - 1) for x in [y[q] for y in beside])]

        def at(arrays, index):
            return [(x, index) for x in arrays]

        leads = from_hbm(
            lead,
            [(e * owned * r + tail, o)] * len(others),
            "lead",
            [
                pltpu.VMEM((held, e), jnp.int32),
                pltpu.VMEM((held, e), jnp.float32),
                pltpu.SemaphoreType.DMA((2 + e * owned * len(others),)),
            ],
            offsets.T,
            couplings.T,
            inverse,
        )
        leads_from = [to_owner(x, d) for d, x in zip(others, leads)]
        lessers = cut([(lesser_in, d, 0, e) for d in others], leads)
        lesser_from = [[[from_energy(x, t)] for t in shifts] for x in lessers]
        rest = cut(
            [*((greater_in, d, 0, e) for d in others), (inverse, 0, 0, e), (lesser_in, 0, 0, e - 1), (lesser_in, 0, e - 1, 1)],
            lessers,
        )
        greaters, inverse_own, lesser_own = rest[: owners - 1], rest[owners - 1], rest[owners:]
        greater_rows = [to_owner(x, d) for d, x in zip(others, greaters)]

        joined, *inverse_rows = call(
            join, [(owners, tail, LANES)] + [block] * len(others), "join", leads[0], *leads_from
        )
        tables = call(
            weights,
            [jax.ShapeDtypeStruct((e, tile, LANES), jnp.float32)] * (1 + len(shifts)),
            "weights",
            joined,
            *to_lanes(joined),
        )
        tables_for = [
            lax.ppermute(table, "en", [(i, (i + t) % en) for i in range(en)])
            for t, table in zip(shifts, tables[1:])
        ]
        lesser_own_from = [[from_energy(x, t) for x in lesser_own] for t in shifts]

        groups = [tuple(range(e - 1)), (e - 1,)]
        singles = [(n,) for n in range(e)]
        lesser_rows = []
        last = []
        for d, came in zip(others, lesser_from):
            last = mix(tables, came, d, groups, last)
            lesser_rows.append([to_owner(x, d) for x in last])
        inverse_own_beside = to_lanes(inverse_own)
        last = [*last, *inverse_own_beside]
        received = [[] for _ in singles]
        for t, table in zip(shifts, tables_for):
            last = partial_sums(table, greater_rows, singles, last)
            for g, part in enumerate(last):
                received[g].append(from_energy(part, t))
        inverse_rows_beside = [to_lanes(x) for x in inverse_rows]
        lesser_mixed = mix(tables, lesser_own_from, 0, groups, last)
        lesser_mixed_beside = [to_lanes(x) for x in lesser_mixed]
        last = lesser_mixed

        def find(groups, n):
            return next((g, group.index(n)) for g, group in enumerate(groups) if n in group)

        def inverse_at(n):
            beside = [at(inverse_own_beside, (n,)), *(at(x, (n,)) for x in inverse_rows_beside)]
            return in_order((inverse_own, (n,)), at(inverse_rows, (n,)), beside)

        def lesser_job(n):
            g, i = find(groups, n)
            h, k = find(groups, n)
            rows = [x[g] for x in lesser_rows]
            beside = [at(lesser_mixed_beside[h], (k,))]
            for x in lesser_rows_beside:
                beside.append(at(x[g], (i,)))
            return inverse_at(n), in_order((lesser_mixed[h], (k,)), at(rows, (i,)), beside)

        lesser_rows_beside = [[*(to_lanes(x) for x in rows[:-1]), None] for rows in lesser_rows]

        results = {"L": None, "G": None}
        waiting = {"L": [], "G": []}

        def put(kind, some, earlier):
            parts = [part for part in waiting[kind] if some(part)]
            waiting[kind] = [part for part in waiting[kind] if not some(part)]
            if parts:
                results[kind] = place(results[kind], parts, earlier)
                return [results[kind]]
            return earlier

        sigmas = {}
        steps = ["L0", "a0", "L1+G0"]
        for n in range(1, e):
            steps += [f"a{n}", "pL0", f"G{n}"] if n == 1 else [f"a{n}", f"G{n}"]
        for step in steps:
            if step[0] == "p":
                last = put(step[1], lambda part: len(step) < 3 or part[4] == int(step[2]), last)
                continue
            if step[0] == "a":
                g = int(step[1])
                group = singles[g]
                sigma = add_partial(group, tables[0], greater_rows, received[g], last)
                last = sigma
                sigmas[g] = (sigma, [to_lanes(x) for x in sigma])
                continue
            jobs, made = [], []
            for kind, g in step.split("+"):
                g = int(g)
                for i, n in enumerate(groups[g] if kind == "L" else singles[g]):
                    made.append((kind, n, g))
                    if kind == "L":
                        jobs.append(lesser_job(n))
                    else:
                        sigma, beside = sigmas[g]
                        beside = [at(x, (i,)) for x in beside]
                        jobs.append((inverse_at(n), in_order((sigma[0], (i,)), at(sigma[1:], (i,)), beside)))
            last = product(jobs, last, STEP if step == "L0" else 0)
            back = back_to_rows(last)
            if step == "L0":
                for rows, beside in zip(lesser_rows, lesser_rows_beside):
                    rows[-1] = after([rows[-1]], *last)[0]
                    beside[-1] = to_lanes(rows[-1])
            for k, (kind, n, g) in enumerate(made):
                waiting[kind] += [(n, d, x, k, g) for d, x in enumerate(back)]
        last = put("L", lambda part: part[1] == 0, last)
        last = put("G", lambda part: part[1] == 0, last)
        for kind, g in [*(("L", g) for g in range(len(groups))), *(("G", n) for n in range(e))]:
            last = put(kind, lambda part: part[4] == g, last)
        lesser_out, greater_out = results["L"], results["G"]
        return lesser_out, greater_out

    block, coupled = P("en", "blk", "ph", None), P("en", "ph")
    return jax.shard_map(
        on_device,
        mesh=mesh,
        in_specs=(block, block, block, coupled, coupled),
        out_specs=(block, block),
        check_vma=False,
    )
```

```python
import math

import jax
import jax.numpy as jnp
from jax import lax
from jax.experimental import pallas as pl
from jax.experimental.pallas import tpu as pltpu
from jax.sharding import PartitionSpec as P

MAXOFF = 9
BF16 = jnp.bfloat16
STEP = 16
LANES = 128
WHOLE = pl.BlockSpec(memory_space=pltpu.VMEM)
PARAMS = pltpu.CompilerParams(vmem_limit_bytes=12 * 1024 * 1024)
COST = pl.CostEstimate(flops=1, bytes_accessed=1, transcendentals=0)


def call(kernel, outs, name, *args):
    outs = [x if isinstance(x, jax.ShapeDtypeStruct) else jax.ShapeDtypeStruct(x, BF16) for x in outs]
    return pl.pallas_call(
        kernel,
        in_specs=[WHOLE] * len(args),
        out_specs=[WHOLE] * len(outs),
        out_shape=outs,
        compiler_params=PARAMS,
        cost_estimate=COST,
        name=name,
    )(*args)


def after(xs, *earlier):
    return lax.optimization_barrier((tuple(xs), earlier))[0]


def chunks(rows, body):
    @pl.loop(0, rows // STEP, unroll=math.gcd(rows // STEP, 4))
    def _(i):
        body(pl.ds(pl.multiple_of(i * STEP, STEP), STEP))


def weighted(tables, energies, load):
    totals = [None] * len(energies)
    for t, table in enumerate(tables):
        for m in range(table.shape[0]):
            g = load(t, m).astype(jnp.float32)
            for i, n in enumerate(energies):
                row = table[m, n : n + 1, :]
                term = jnp.concatenate([row] * (g.shape[1] // LANES), axis=1) * g
                totals[i] = term if totals[i] is None else totals[i] + term
    return totals


def solution(mesh):
    en, ph = mesh.shape["en"], mesh.shape["ph"]

    def on_device(lesser_in, greater_in, inverse, offsets, couplings):
        e, nb, r, o = lesser_in.shape
        held = offsets.shape[1]
        owners = math.gcd(nb, ph)
        lanes = ph // owners
        owned = nb // owners
        pieces = ph
        others = range(1, owners)
        reach = (MAXOFF + e - 1) // e
        shifts = [t for t in range(1, en) if t <= reach or en - t <= reach]
        block = (e, owned, r, o)
        tile = -(-e // 8) * 8
        tail = -(-4 * held // 16) * 16

        def owner_at(d):
            return lax.rem(lax.div(lax.axis_index("ph"), lanes) + d, owners)

        def place_of(j):
            at = lax.axis_index("ph")
            back = lax.rem(lax.div(at, lanes) + owners - j % owners, owners)
            return back * lanes + lax.rem(lax.rem(at, lanes) + lanes - j // owners, lanes)

        def to_owner(x, d):
            pairs = [(p, (p // lanes + d) % owners * lanes + p % lanes) for p in range(ph)]
            return lax.ppermute(x, "ph", pairs)

        def to_lanes(x):
            return [
                lax.ppermute(
                    x, "ph", [(p, p // lanes * lanes + (p % lanes + q) % lanes) for p in range(ph)]
                )
                for q in range(1, lanes)
            ]

        def from_energy(x, t):
            return lax.ppermute(x, "en", [((i + t) % en, i) for i in range(en)])


        def lead(offsets_ref, couplings_ref, inverse_ref, *refs):
            leads, (offsets_at, couplings_at, sems) = refs[:-3], refs[-3:]
            copies = [(offsets_ref, offsets_at), (couplings_ref, couplings_at)]
            for i, d in enumerate(others):
                for n in range(e):
                    for b in range(owned):
                        to = leads[i].at[pl.ds((n * owned + b) * r, r)]
                        copies.append((inverse_ref.at[n, owner_at(d) * owned + b], to))
            copies = [pltpu.make_async_copy(x, y, sems.at[i]) for i, (x, y) in enumerate(copies)]
            for copy in copies:
                copy.start()
            for copy in copies[:2]:
                copy.wait()
            rest = couplings_at[...]
            parts = [offsets_at[...].astype(jnp.float32)]
            for _ in range(3):
                parts.append(rest.astype(BF16).astype(jnp.float32))
                rest = rest - parts[-1]
            row = lax.broadcasted_iota(jnp.int32, (tail, e), 0)
            packed = jnp.zeros((tail, e), jnp.float32)
            for i, x in enumerate(parts):
                for k in range(held):
                    packed = jnp.where(row == i * held + k, x[k : k + 1, :], packed)
            packed = jnp.concatenate([packed, jnp.zeros((tail, LANES - e), jnp.float32)], axis=1)
            for out in leads:
                out[e * owned * r :, :LANES] = packed.astype(BF16)
                out[e * owned * r :, LANES:] = jnp.zeros((tail, o - LANES), BF16)
            for copy in copies[2:]:
                copy.wait()

        def cut(wanted, earlier):
            arrays = after([x for x, *_ in wanted], *earlier)

            def kernel(*refs):
                for i, (_, d, n, k, _) in enumerate(wanted):
                    for b in range(owned):
                        refs[len(wanted) + i][:, b, :r] = refs[i][n : n + k, owner_at(d) * owned + b]

            return call(kernel, [(k, owned, r + spare, o) for *_, k, spare in wanted], "cut", *arrays)

        def join(*refs):
            for d in range(owners):
                refs[owners][d] = refs[d][e * owned * r :, :LANES]
            for d in others:
                for n in range(e):
                    for b in range(owned):
                        at_row = (n * owned + b) * r
                        refs[owners + d][n, b] = refs[d][at_row : at_row + r]

        def from_hbm(kernel, outs, name, scratch, *args):
            far = pl.BlockSpec(memory_space=pltpu.HBM)
            return pl.pallas_call(
                kernel,
                in_specs=[far] * len(args),
                out_specs=[WHOLE] * len(outs),
                out_shape=[jax.ShapeDtypeStruct(x, BF16) for x in outs],
                scratch_shapes=scratch,
                compiler_params=pltpu.CompilerParams(vmem_limit_bytes=61 * 1024 * 1024),
                cost_estimate=COST,
                name=name,
            )(*args)

        def weights(*refs):
            ins, outs = refs[:lanes], refs[lanes:]
            at = lax.axis_index("en")
            row = lax.broadcasted_iota(jnp.int32, (tile, LANES), 0)
            lane = lax.broadcasted_iota(jnp.int32, (tile, LANES), 1)
            pairs = []
            for ref in ins:
                for d in range(owners):
                    x = ref[d].astype(jnp.float32)
                    for k in range(held):
                        shift, *terms = [x[i * held + k : i * held + k + 1, :] for i in range(4)]
                        pairs.append((shift, terms[0] + terms[1] + terms[2]))
            for i, t in enumerate([0] + shifts):
                away = (lax.rem(at + t, en) - at) * e
                for m in range(e):
                    apart = (away + m - lane[:1]).astype(jnp.float32)
                    total = jnp.zeros((1, LANES), jnp.float32)
                    for shift, coupling in pairs:
                        total += jnp.where(shift == apart, coupling, 0.0)
                    spread = jnp.where(row == lane, jnp.broadcast_to(total, (tile, LANES)), 0.0)
                    outs[i][m] = jnp.broadcast_to(
                        jnp.sum(spread, axis=1, keepdims=True), (tile, LANES)
                    )

        def mix(tables, received, d, groups, earlier):
            flat = [x for came in received for x in came]
            stands = [
                [(1 + i, k) for i, x in enumerate(flat) if any(x is y for y in came) for k in range(x.shape[0])]
                for came in received
            ]

            def load(ins, t, m, at_block, b, at):
                if not t:
                    return ins[0][m, at_block, at, :]
                i, k = stands[t - 1][m]
                return ins[i][k, b, at, :]

            def kernel(*refs):
                table_refs, refs = refs[: len(tables)], refs[len(tables) :]
                ins, outs = refs[: 1 + len(flat)], refs[1 + len(flat) :]
                for b in range(owned):
                    at_block = owner_at(d) * owned + b

                    def body(at):
                        totals = weighted(
                            table_refs, range(e), lambda t, m: load(ins, t, m, at_block, b, at)
                        )
                        for out, group in zip(outs, groups):
                            for i, n in enumerate(group):
                                out[i, b, at, :] = totals[n].astype(BF16)

                    chunks(r, body)

            shapes = [(len(group),) + block[1:] for group in groups]
            return call(kernel, shapes, "mix", *after(tables, *earlier), lesser_in, *flat)

        def greater_at(refs, m, d, b, at):
            return refs[d][m, b if d else owner_at(0) * owned + b, at, :]

        def partial_sums(table, rows, groups, earlier):
            def kernel(table_ref, *refs):
                for d in range(owners):
                    for b in range(owned):

                        def body(at):
                            totals = weighted(
                                [table_ref], range(e), lambda t, m: greater_at(refs, m, d, b, at)
                            )
                            for out, group in zip(refs[owners:], groups):
                                for i, n in enumerate(group):
                                    out[i, d, b, at, :] = totals[n].astype(BF16)

                        chunks(r, body)

            (table,) = after([table], *earlier)
            spare = [STEP] * (len(groups) - 1) + [0]
            shapes = [(len(group), owners, owned, r + x, o) for group, x in zip(groups, spare)]
            return call(kernel, shapes, "partial_sums", table, greater_in, *rows)

        def add_partial(group, table, rows, received, earlier):
            def kernel(table_ref, *refs):
                for d in range(owners):
                    for b in range(owned):

                        def body(at):
                            totals = weighted(
                                [table_ref], group, lambda t, m: greater_at(refs, m, d, b, at)
                            )
                            for i in range(len(group)):
                                for ref in refs[owners:-owners]:
                                    totals[i] += ref[i, d, b, at, :].astype(jnp.float32)
                                refs[d - owners][i, b, at, :] = totals[i].astype(BF16)

                        chunks(r, body)

            (table,) = after([table], *earlier)
            shape = (len(group),) + block[1:]
            return call(kernel, [shape] * owners, "add_partial", table, greater_in, *rows, *received)

        def product(jobs, earlier, pad=0):
            arrays = []
            for job in jobs:
                for x, _ in [*job[0], *job[1]]:
                    if not any(x is y for y in arrays):
                        arrays.append(x)
            where = {id(x): i for i, x in enumerate(arrays)}

            def kernel(*refs):
                outs = refs[-owners:]
                spans = [pl.ds(pl.multiple_of(place_of(j) * r, r), r) for j in range(pieces)]
                for k, job in enumerate(jobs):
                    a_in, s_in = ([(refs[where[id(x)]], index) for x, index in part] for part in job)
                    for b in range(owned):
                        left = jnp.concatenate(
                            [
                                jnp.concatenate([a[(*index, b, slice(None), at)] for at in spans], axis=1)
                                for a, index in a_in[:owners]
                            ],
                            axis=0,
                        )
                        right = jnp.concatenate([x[(*index, b)] for x, index in s_in], axis=0)
                        half = jnp.dot(left, right, preferred_element_type=jnp.float32).astype(BF16)
                        full = lax.dot_general(
                            half,
                            jnp.concatenate([a[(*index, b)] for a, index in a_in], axis=0),
                            (((1,), (1,)), ((), ())),
                            preferred_element_type=jnp.float32,
                        ).astype(BF16)
                        for i in range(owners):
                            for j, at in enumerate(spans):
                                outs[i][k, b, :r, at] = full[i * r : (i + 1) * r, j * r : (j + 1) * r]

            shapes = [(len(jobs), owned, r + pad if d else r, o) for d in range(owners)]
            return call(kernel, shapes, "product", *after(arrays, *earlier))

        def back_to_rows(outs):
            return [outs[0]] + [to_owner(outs[d], owners - d) for d in others]

        def place(result, parts, earlier):
            arrays = []
            for _, _, x, _, _ in parts:
                if not any(x is y for y in arrays):
                    arrays.append(x)
            where = {id(x): i for i, x in enumerate(arrays)}

            def kernel(*refs):
                sems, out = refs[-1], refs[-2]
                copies = [
                    pltpu.make_async_copy(
                        refs[where[id(x)]].at[k, :, pl.ds(0, r)],
                        out.at[n, pl.ds(owner_at(d) * owned, owned)],
                        sems.at[i],
                    )
                    for i, (n, d, x, k, _) in enumerate(parts)
                ]
                for copy in copies:
                    copy.start()
                for copy in copies:
                    copy.wait()

            far = pl.BlockSpec(memory_space=pltpu.HBM)
            return pl.pallas_call(
                kernel,
                in_specs=[WHOLE] * len(arrays) + [far] * (result is not None),
                out_specs=far,
                out_shape=jax.ShapeDtypeStruct((e, nb, r, o), BF16),
                scratch_shapes=[pltpu.SemaphoreType.DMA((len(parts),))],
                input_output_aliases={} if result is None else {len(arrays): 0},
                compiler_params=PARAMS,
                cost_estimate=COST,
                name="place",
            )(*after(arrays, *earlier), *([] if result is None else [result]))

        def in_order(own, rows, beside):
            return [own, *rows, *(x for q in range(lanes - 1) for x in [y[q] for y in beside])]

        def at(arrays, index):
            return [(x, index) for x in arrays]

        leads = from_hbm(
            lead,
            [(e * owned * r + tail, o)] * len(others),
            "lead",
            [
                pltpu.VMEM((held, e), jnp.int32),
                pltpu.VMEM((held, e), jnp.float32),
                pltpu.SemaphoreType.DMA((2 + e * owned * len(others),)),
            ],
            offsets.T,
            couplings.T,
            inverse,
        )
        leads_from = [to_owner(x, d) for d, x in zip(others, leads)]
        lessers = cut([(lesser_in, d, 0, e, 0) for d in others], leads)
        lesser_from = [[[from_energy(x, t)] for t in shifts] for x in lessers]
        rest = cut(
            [*((greater_in, d, 0, e, 0) for d in others), (inverse, 0, 0, e, 0), (lesser_in, 0, 0, e - 1, STEP), (lesser_in, 0, e - 1, 1, 0)],
            lessers,
        )
        greaters, inverse_own, lesser_own = rest[: owners - 1], rest[owners - 1], rest[owners:]
        greater_rows = [to_owner(x, d) for d, x in zip(others, greaters)]

        joined, *inverse_rows = call(
            join, [(owners, tail, LANES)] + [block] * len(others), "join", leads[0], *leads_from
        )
        tables = call(
            weights,
            [jax.ShapeDtypeStruct((e, tile, LANES), jnp.float32)] * (1 + len(shifts)),
            "weights",
            joined,
            *to_lanes(joined),
        )
        tables_for = [
            lax.ppermute(table, "en", [(i, (i + t) % en) for i in range(en)])
            for t, table in zip(shifts, tables[1:])
        ]
        lesser_own_from = [[from_energy(x, t) for x in lesser_own] for t in shifts]

        groups = [tuple(range(e - 1)), (e - 1,)]
        singles = [(n,) for n in range(e)]
        lesser_rows = []
        last = []
        for d, came in zip(others, lesser_from):
            last = mix(tables, came, d, groups, last)
            lesser_rows.append([to_owner(x, d) for x in last])
        inverse_own_beside = to_lanes(inverse_own)
        last = [*last, *inverse_own_beside]
        received = [[] for _ in singles]
        for t, table in zip(shifts, tables_for):
            last = partial_sums(table, greater_rows, singles, last)
            for g, part in enumerate(last):
                received[g].append(from_energy(part, t))
        inverse_rows_beside = [to_lanes(x) for x in inverse_rows]
        lesser_mixed = mix(tables, lesser_own_from, 0, groups, last)
        lesser_mixed_beside = [to_lanes(x) for x in lesser_mixed]
        last = lesser_mixed

        def find(groups, n):
            return next((g, group.index(n)) for g, group in enumerate(groups) if n in group)

        def inverse_at(n):
            beside = [at(inverse_own_beside, (n,)), *(at(x, (n,)) for x in inverse_rows_beside)]
            return in_order((inverse_own, (n,)), at(inverse_rows, (n,)), beside)

        def lesser_job(n):
            g, i = find(groups, n)
            h, k = find(groups, n)
            rows = [x[g] for x in lesser_rows]
            beside = [at(lesser_mixed_beside[h], (k,))]
            for x in lesser_rows_beside:
                beside.append(at(x[g], (i,)))
            return inverse_at(n), in_order((lesser_mixed[h], (k,)), at(rows, (i,)), beside)

        lesser_rows_beside = [[*(to_lanes(x) for x in rows[:-1]), None] for rows in lesser_rows]

        results = {"L": None, "G": None}
        waiting = {"L": [], "G": []}

        def put(kind, some, earlier):
            parts = [part for part in waiting[kind] if some(part)]
            waiting[kind] = [part for part in waiting[kind] if not some(part)]
            if parts:
                results[kind] = place(results[kind], parts, earlier)
                return [results[kind]]
            return earlier

        sigmas = {}
        steps = ["L0", "a0", "L1+G0"]
        for n in range(1, e):
            steps += [f"a{n}", "pL0", f"G{n}"] if n == 1 else [f"a{n}", f"G{n}"]
        for step in steps:
            if step[0] == "p":
                last = put(step[1], lambda part: len(step) < 3 or part[4] == int(step[2]), last)
                continue
            if step[0] == "a":
                g = int(step[1])
                group = singles[g]
                sigma = add_partial(group, tables[0], greater_rows, received[g], last)
                last = sigma
                sigmas[g] = (sigma, [to_lanes(x) for x in sigma])
                continue
            jobs, made = [], []
            for kind, g in step.split("+"):
                g = int(g)
                for i, n in enumerate(groups[g] if kind == "L" else singles[g]):
                    made.append((kind, n, g))
                    if kind == "L":
                        jobs.append(lesser_job(n))
                    else:
                        sigma, beside = sigmas[g]
                        beside = [at(x, (i,)) for x in beside]
                        jobs.append((inverse_at(n), in_order((sigma[0], (i,)), at(sigma[1:], (i,)), beside)))
            last = product(jobs, last, STEP if step == "L0" else 0)
            back = back_to_rows(last)
            if step == "L0":
                for rows, beside in zip(lesser_rows, lesser_rows_beside):
                    rows[-1] = after([rows[-1]], *last)[0]
                    beside[-1] = to_lanes(rows[-1])
            for k, (kind, n, g) in enumerate(made):
                waiting[kind] += [(n, d, x, k, g) for d, x in enumerate(back)]
        last = put("L", lambda part: part[1] == 0, last)
        last = put("G", lambda part: part[1] == 0, last)
        for kind, g in [*(("L", g) for g in range(len(groups))), *(("G", n) for n in range(e))]:
            last = put(kind, lambda part: part[4] == g, last)
        lesser_out, greater_out = results["L"], results["G"]
        return lesser_out, greater_out

    block, coupled = P("en", "blk", "ph", None), P("en", "ph")
    return jax.shard_map(
        on_device,
        mesh=mesh,
        in_specs=(block, block, block, coupled, coupled),
        out_specs=(block, block),
        check_vma=False,
    )
```

```python
import math

import jax
import jax.numpy as jnp
from jax import lax
from jax.experimental import pallas as pl
from jax.experimental.pallas import tpu as pltpu
from jax.sharding import PartitionSpec as P

MAXOFF = 9
BF16 = jnp.bfloat16
STEP = 16
LANES = 128
WHOLE = pl.BlockSpec(memory_space=pltpu.VMEM)
PARAMS = pltpu.CompilerParams(vmem_limit_bytes=12 * 1024 * 1024)
COST = pl.CostEstimate(flops=1, bytes_accessed=1, transcendentals=0)


def call(kernel, outs, name, *args):
    outs = [x if isinstance(x, jax.ShapeDtypeStruct) else jax.ShapeDtypeStruct(x, BF16) for x in outs]
    return pl.pallas_call(
        kernel,
        in_specs=[WHOLE] * len(args),
        out_specs=[WHOLE] * len(outs),
        out_shape=outs,
        compiler_params=PARAMS,
        cost_estimate=COST,
        name=name,
    )(*args)


def after(xs, *earlier):
    return lax.optimization_barrier((tuple(xs), earlier))[0]


def chunks(rows, body):
    @pl.loop(0, rows // STEP, unroll=math.gcd(rows // STEP, 4))
    def _(i):
        body(pl.ds(pl.multiple_of(i * STEP, STEP), STEP))


def weighted(tables, energies, load):
    totals = [None] * len(energies)
    for t, table in enumerate(tables):
        for m in range(table.shape[0]):
            g = load(t, m).astype(jnp.float32)
            for i, n in enumerate(energies):
                row = table[m, n : n + 1, :]
                term = jnp.concatenate([row] * (g.shape[1] // LANES), axis=1) * g
                totals[i] = term if totals[i] is None else totals[i] + term
    return totals


def solution(mesh):
    en, ph = mesh.shape["en"], mesh.shape["ph"]

    def on_device(lesser_in, greater_in, inverse, offsets, couplings):
        e, nb, r, o = lesser_in.shape
        held = offsets.shape[1]
        owners = math.gcd(nb, ph)
        lanes = ph // owners
        owned = nb // owners
        pieces = ph
        others = range(1, owners)
        reach = (MAXOFF + e - 1) // e
        shifts = [t for t in range(1, en) if t <= reach or en - t <= reach]
        block = (e, owned, r, o)
        tile = -(-e // 8) * 8
        tail = -(-4 * held // 16) * 16

        def owner_at(d):
            return lax.rem(lax.div(lax.axis_index("ph"), lanes) + d, owners)

        def place_of(j):
            at = lax.axis_index("ph")
            back = lax.rem(lax.div(at, lanes) + owners - j % owners, owners)
            return back * lanes + lax.rem(lax.rem(at, lanes) + lanes - j // owners, lanes)

        def to_owner(x, d):
            pairs = [(p, (p // lanes + d) % owners * lanes + p % lanes) for p in range(ph)]
            return lax.ppermute(x, "ph", pairs)

        def to_lanes(x):
            return [
                lax.ppermute(
                    x, "ph", [(p, p // lanes * lanes + (p % lanes + q) % lanes) for p in range(ph)]
                )
                for q in range(1, lanes)
            ]

        def from_energy(x, t):
            return lax.ppermute(x, "en", [((i + t) % en, i) for i in range(en)])


        def lead(offsets_ref, couplings_ref, inverse_ref, *refs):
            leads, (offsets_at, couplings_at, sems) = refs[:-3], refs[-3:]
            copies = [(offsets_ref, offsets_at), (couplings_ref, couplings_at)]
            for i, d in enumerate(others):
                for n in range(e):
                    for b in range(owned):
                        to = leads[i].at[pl.ds((n * owned + b) * r, r)]
                        copies.append((inverse_ref.at[n, owner_at(d) * owned + b], to))
            copies = [pltpu.make_async_copy(x, y, sems.at[i]) for i, (x, y) in enumerate(copies)]
            for copy in copies:
                copy.start()
            for copy in copies[:2]:
                copy.wait()
            rest = couplings_at[...]
            parts = [offsets_at[...].astype(jnp.float32)]
            for _ in range(3):
                parts.append(rest.astype(BF16).astype(jnp.float32))
                rest = rest - parts[-1]
            row = lax.broadcasted_iota(jnp.int32, (tail, e), 0)
            packed = jnp.zeros((tail, e), jnp.float32)
            for i, x in enumerate(parts):
                for k in range(held):
                    packed = jnp.where(row == i * held + k, x[k : k + 1, :], packed)
            packed = jnp.concatenate([packed, jnp.zeros((tail, LANES - e), jnp.float32)], axis=1)
            for out in leads:
                out[e * owned * r :, :LANES] = packed.astype(BF16)
                out[e * owned * r :, LANES:] = jnp.zeros((tail, o - LANES), BF16)
            for copy in copies[2:]:
                copy.wait()

        def cut(wanted, earlier):
            arrays = after([x for x, *_ in wanted], *earlier)

            def kernel(*refs):
                for i, (_, d, n, k, _) in enumerate(wanted):
                    for b in range(owned):
                        refs[len(wanted) + i][:, b, :r] = refs[i][n : n + k, owner_at(d) * owned + b]

            return call(kernel, [(k, owned, r + spare, o) for *_, k, spare in wanted], "cut", *arrays)

        def join(*refs):
            for d in range(owners):
                refs[owners][d] = refs[d][e * owned * r :, :LANES]
            for d in others:
                for n in range(e):
                    for b in range(owned):
                        at_row = (n * owned + b) * r
                        refs[owners + d][n, b] = refs[d][at_row : at_row + r]

        def from_hbm(kernel, outs, name, scratch, *args):
            far = pl.BlockSpec(memory_space=pltpu.HBM)
            return pl.pallas_call(
                kernel,
                in_specs=[far] * len(args),
                out_specs=[WHOLE] * len(outs),
                out_shape=[jax.ShapeDtypeStruct(x, BF16) for x in outs],
                scratch_shapes=scratch,
                compiler_params=pltpu.CompilerParams(vmem_limit_bytes=61 * 1024 * 1024),
                cost_estimate=COST,
                name=name,
            )(*args)

        def weights(*refs):
            ins, outs = refs[:lanes], refs[lanes:]
            at = lax.axis_index("en")
            row = lax.broadcasted_iota(jnp.int32, (tile, LANES), 0)
            lane = lax.broadcasted_iota(jnp.int32, (tile, LANES), 1)
            pairs = []
            for ref in ins:
                for d in range(owners):
                    x = ref[d].astype(jnp.float32)
                    for k in range(held):
                        shift, *terms = [x[i * held + k : i * held + k + 1, :] for i in range(4)]
                        pairs.append((shift, terms[0] + terms[1] + terms[2]))
            for i, t in enumerate([0] + shifts):
                away = (lax.rem(at + t, en) - at) * e
                for m in range(e):
                    apart = (away + m - lane[:1]).astype(jnp.float32)
                    total = jnp.zeros((1, LANES), jnp.float32)
                    for shift, coupling in pairs:
                        total += jnp.where(shift == apart, coupling, 0.0)
                    spread = jnp.where(row == lane, jnp.broadcast_to(total, (tile, LANES)), 0.0)
                    outs[i][m] = jnp.broadcast_to(
                        jnp.sum(spread, axis=1, keepdims=True), (tile, LANES)
                    )

        def mix(tables, received, d, groups, earlier):
            flat = [x for came in received for x in came]
            stands = [
                [(1 + i, k) for i, x in enumerate(flat) if any(x is y for y in came) for k in range(x.shape[0])]
                for came in received
            ]

            def load(ins, t, m, at_block, b, at):
                if not t:
                    return ins[0][m, at_block, at, :]
                i, k = stands[t - 1][m]
                return ins[i][k, b, at, :]

            def kernel(*refs):
                table_refs, refs = refs[: len(tables)], refs[len(tables) :]
                ins, outs = refs[: 1 + len(flat)], refs[1 + len(flat) :]
                for b in range(owned):
                    at_block = owner_at(d) * owned + b

                    def body(at):
                        totals = weighted(
                            table_refs, range(e), lambda t, m: load(ins, t, m, at_block, b, at)
                        )
                        for out, group in zip(outs, groups):
                            for i, n in enumerate(group):
                                out[i, b, at, :] = totals[n].astype(BF16)

                    chunks(r, body)

            shapes = [(len(group),) + block[1:] for group in groups]
            return call(kernel, shapes, "mix", *after(tables, *earlier), lesser_in, *flat)

        def greater_at(refs, m, d, b, at):
            return refs[d][m, b if d else owner_at(0) * owned + b, at, :]

        def partial_sums(table, rows, groups, earlier):
            def kernel(table_ref, *refs):
                for d in range(owners):
                    for b in range(owned):

                        def body(at):
                            totals = weighted(
                                [table_ref], range(e), lambda t, m: greater_at(refs, m, d, b, at)
                            )
                            for out, group in zip(refs[owners:], groups):
                                for i, n in enumerate(group):
                                    out[i, d, b, at, :] = totals[n].astype(BF16)

                        chunks(r, body)

            (table,) = after([table], *earlier)
            spare = [STEP] + [0] * (len(groups) - 1)
            shapes = [(len(group), owners, owned, r + x, o) for group, x in zip(groups, spare)]
            return call(kernel, shapes, "partial_sums", table, greater_in, *rows)

        def add_partial(group, table, rows, received, earlier):
            def kernel(table_ref, *refs):
                for d in range(owners):
                    for b in range(owned):

                        def body(at):
                            totals = weighted(
                                [table_ref], group, lambda t, m: greater_at(refs, m, d, b, at)
                            )
                            for i in range(len(group)):
                                for ref in refs[owners:-owners]:
                                    totals[i] += ref[i, d, b, at, :].astype(jnp.float32)
                                refs[d - owners][i, b, at, :] = totals[i].astype(BF16)

                        chunks(r, body)

            (table,) = after([table], *earlier)
            shape = (len(group),) + block[1:]
            return call(kernel, [shape] * owners, "add_partial", table, greater_in, *rows, *received)

        def product(jobs, earlier, pad=0):
            arrays = []
            for job in jobs:
                for x, _ in [*job[0], *job[1]]:
                    if not any(x is y for y in arrays):
                        arrays.append(x)
            where = {id(x): i for i, x in enumerate(arrays)}

            def kernel(*refs):
                outs = refs[-owners:]
                spans = [pl.ds(pl.multiple_of(place_of(j) * r, r), r) for j in range(pieces)]
                for k, job in enumerate(jobs):
                    a_in, s_in = ([(refs[where[id(x)]], index) for x, index in part] for part in job)
                    for b in range(owned):
                        left = jnp.concatenate(
                            [
                                jnp.concatenate([a[(*index, b, slice(None), at)] for at in spans], axis=1)
                                for a, index in a_in[:owners]
                            ],
                            axis=0,
                        )
                        right = jnp.concatenate([x[(*index, b)] for x, index in s_in], axis=0)
                        half = jnp.dot(left, right, preferred_element_type=jnp.float32).astype(BF16)
                        full = lax.dot_general(
                            half,
                            jnp.concatenate([a[(*index, b)] for a, index in a_in], axis=0),
                            (((1,), (1,)), ((), ())),
                            preferred_element_type=jnp.float32,
                        ).astype(BF16)
                        for i in range(owners):
                            for j, at in enumerate(spans):
                                outs[i][k, b, :r, at] = full[i * r : (i + 1) * r, j * r : (j + 1) * r]

            shapes = [(len(jobs), owned, r + pad if d else r, o) for d in range(owners)]
            return call(kernel, shapes, "product", *after(arrays, *earlier))

        def back_to_rows(outs):
            return [outs[0]] + [to_owner(outs[d], owners - d) for d in others]

        def place(result, parts, earlier):
            arrays = []
            for _, _, x, _, _ in parts:
                if not any(x is y for y in arrays):
                    arrays.append(x)
            where = {id(x): i for i, x in enumerate(arrays)}

            def kernel(*refs):
                sems, out = refs[-1], refs[-2]
                copies = [
                    pltpu.make_async_copy(
                        refs[where[id(x)]].at[k, :, pl.ds(0, r)],
                        out.at[n, pl.ds(owner_at(d) * owned, owned)],
                        sems.at[i],
                    )
                    for i, (n, d, x, k, _) in enumerate(parts)
                ]
                for copy in copies:
                    copy.start()
                for copy in copies:
                    copy.wait()

            far = pl.BlockSpec(memory_space=pltpu.HBM)
            return pl.pallas_call(
                kernel,
                in_specs=[WHOLE] * len(arrays) + [far] * (result is not None),
                out_specs=far,
                out_shape=jax.ShapeDtypeStruct((e, nb, r, o), BF16),
                scratch_shapes=[pltpu.SemaphoreType.DMA((len(parts),))],
                input_output_aliases={} if result is None else {len(arrays): 0},
                compiler_params=PARAMS,
                cost_estimate=COST,
                name="place",
            )(*after(arrays, *earlier), *([] if result is None else [result]))

        def in_order(own, rows, beside):
            return [own, *rows, *(x for q in range(lanes - 1) for x in [y[q] for y in beside])]

        def at(arrays, index):
            return [(x, index) for x in arrays]

        leads = from_hbm(
            lead,
            [(e * owned * r + tail, o)] * len(others),
            "lead",
            [
                pltpu.VMEM((held, e), jnp.int32),
                pltpu.VMEM((held, e), jnp.float32),
                pltpu.SemaphoreType.DMA((2 + e * owned * len(others),)),
            ],
            offsets.T,
            couplings.T,
            inverse,
        )
        leads_from = [to_owner(x, d) for d, x in zip(others, leads)]
        lessers = cut([(lesser_in, d, 0, e, 0) for d in others], leads)
        lesser_from = [[[from_energy(x, t)] for t in shifts] for x in lessers]
        rest = cut(
            [*((greater_in, d, 0, e, 0) for d in others), (inverse, 0, 0, e, 0), (lesser_in, 0, 0, e - 1, STEP), (lesser_in, 0, e - 1, 1, 0)],
            lessers,
        )
        greaters, inverse_own, lesser_own = rest[: owners - 1], rest[owners - 1], rest[owners:]
        greater_rows = [to_owner(x, d) for d, x in zip(others, greaters)]

        joined, *inverse_rows = call(
            join, [(owners, tail, LANES)] + [block] * len(others), "join", leads[0], *leads_from
        )
        tables = call(
            weights,
            [jax.ShapeDtypeStruct((e, tile, LANES), jnp.float32)] * (1 + len(shifts)),
            "weights",
            joined,
            *to_lanes(joined),
        )
        tables_for = [
            lax.ppermute(table, "en", [(i, (i + t) % en) for i in range(en)])
            for t, table in zip(shifts, tables[1:])
        ]
        lesser_own_from = [[from_energy(x, t) for x in lesser_own] for t in shifts]

        groups = [tuple(range(e - 1)), (e - 1,)]
        singles = [(n,) for n in range(e)]
        lesser_rows = []
        last = []
        for d, came in zip(others, lesser_from):
            last = mix(tables, came, d, groups, last)
            lesser_rows.append([to_owner(x, d) for x in last])
        inverse_own_beside = to_lanes(inverse_own)
        last = [*last, *inverse_own_beside]
        received = [[] for _ in singles]
        for t, table in zip(shifts, tables_for):
            last = partial_sums(table, greater_rows, singles, last)
            for g, part in enumerate(last):
                received[g].append(from_energy(part, t))
        inverse_rows_beside = [to_lanes(x) for x in inverse_rows]
        lesser_mixed = mix(tables, lesser_own_from, 0, groups, last)
        lesser_mixed_beside = [to_lanes(x) for x in lesser_mixed]
        last = lesser_mixed

        def find(groups, n):
            return next((g, group.index(n)) for g, group in enumerate(groups) if n in group)

        def inverse_at(n):
            beside = [at(inverse_own_beside, (n,)), *(at(x, (n,)) for x in inverse_rows_beside)]
            return in_order((inverse_own, (n,)), at(inverse_rows, (n,)), beside)

        def lesser_job(n):
            g, i = find(groups, n)
            h, k = find(groups, n)
            rows = [x[g] for x in lesser_rows]
            beside = [at(lesser_mixed_beside[h], (k,))]
            for x in lesser_rows_beside:
                beside.append(at(x[g], (i,)))
            return inverse_at(n), in_order((lesser_mixed[h], (k,)), at(rows, (i,)), beside)

        lesser_rows_beside = [[*(to_lanes(x) for x in rows[:-1]), None] for rows in lesser_rows]

        results = {"L": None, "G": None}
        waiting = {"L": [], "G": []}

        def put(kind, some, earlier):
            parts = [part for part in waiting[kind] if some(part)]
            waiting[kind] = [part for part in waiting[kind] if not some(part)]
            if parts:
                results[kind] = place(results[kind], parts, earlier)
                return [results[kind]]
            return earlier

        sigmas = {}
        steps = ["L0", "a0", "L1+G0"]
        for n in range(1, e):
            steps += [f"a{n}", f"G{n}", "pL0"] if n == 1 else [f"a{n}", f"G{n}"]
        for step in steps:
            if step[0] == "p":
                last = put(step[1], lambda part: len(step) < 3 or part[4] == int(step[2]), last)
                continue
            if step[0] == "a":
                g = int(step[1])
                group = singles[g]
                sigma = add_partial(group, tables[0], greater_rows, received[g], last)
                last = sigma
                sigmas[g] = (sigma, [to_lanes(x) for x in sigma])
                continue
            jobs, made = [], []
            for kind, g in step.split("+"):
                g = int(g)
                for i, n in enumerate(groups[g] if kind == "L" else singles[g]):
                    made.append((kind, n, g))
                    if kind == "L":
                        jobs.append(lesser_job(n))
                    else:
                        sigma, beside = sigmas[g]
                        beside = [at(x, (i,)) for x in beside]
                        jobs.append((inverse_at(n), in_order((sigma[0], (i,)), at(sigma[1:], (i,)), beside)))
            last = product(jobs, last, STEP if step == "L0" else 0)
            back = back_to_rows(last)
            if step == "L0":
                for rows, beside in zip(lesser_rows, lesser_rows_beside):
                    rows[-1] = after([rows[-1]], *last)[0]
                    beside[-1] = to_lanes(rows[-1])
            for k, (kind, n, g) in enumerate(made):
                waiting[kind] += [(n, d, x, k, g) for d, x in enumerate(back)]
        last = put("L", lambda part: part[1] == 0, last)
        last = put("G", lambda part: part[1] == 0, last)
        for kind, g in [*(("L", g) for g in range(len(groups))), *(("G", n) for n in range(e))]:
            last = put(kind, lambda part: part[4] == g, last)
        lesser_out, greater_out = results["L"], results["G"]
        return lesser_out, greater_out

    block, coupled = P("en", "blk", "ph", None), P("en", "ph")
    return jax.shard_map(
        on_device,
        mesh=mesh,
        in_specs=(block, block, block, coupled, coupled),
        out_specs=(block, block),
        check_vma=False,
    )
```

```python
import math

import jax
import jax.numpy as jnp
from jax import lax
from jax.experimental import pallas as pl
from jax.experimental.pallas import tpu as pltpu
from jax.sharding import PartitionSpec as P

MAXOFF = 9
BF16 = jnp.bfloat16
STEP = 16
LANES = 128
WHOLE = pl.BlockSpec(memory_space=pltpu.VMEM)
PARAMS = pltpu.CompilerParams(vmem_limit_bytes=12 * 1024 * 1024)
COST = pl.CostEstimate(flops=1, bytes_accessed=1, transcendentals=0)


def call(kernel, outs, name, *args):
    outs = [x if isinstance(x, jax.ShapeDtypeStruct) else jax.ShapeDtypeStruct(x, BF16) for x in outs]
    return pl.pallas_call(
        kernel,
        in_specs=[WHOLE] * len(args),
        out_specs=[WHOLE] * len(outs),
        out_shape=outs,
        compiler_params=PARAMS,
        cost_estimate=COST,
        name=name,
    )(*args)


def after(xs, *earlier):
    return lax.optimization_barrier((tuple(xs), earlier))[0]


def chunks(rows, body):
    @pl.loop(0, rows // STEP, unroll=math.gcd(rows // STEP, 4))
    def _(i):
        body(pl.ds(pl.multiple_of(i * STEP, STEP), STEP))


def weighted(tables, energies, load):
    totals = [None] * len(energies)
    for t, table in enumerate(tables):
        for m in range(table.shape[0]):
            g = load(t, m).astype(jnp.float32)
            for i, n in enumerate(energies):
                row = table[m, n : n + 1, :]
                term = jnp.concatenate([row] * (g.shape[1] // LANES), axis=1) * g
                totals[i] = term if totals[i] is None else totals[i] + term
    return totals


def solution(mesh):
    en, ph = mesh.shape["en"], mesh.shape["ph"]

    def on_device(lesser_in, greater_in, inverse, offsets, couplings):
        e, nb, r, o = lesser_in.shape
        held = offsets.shape[1]
        owners = math.gcd(nb, ph)
        lanes = ph // owners
        owned = nb // owners
        pieces = ph
        others = range(1, owners)
        reach = (MAXOFF + e - 1) // e
        shifts = [t for t in range(1, en) if t <= reach or en - t <= reach]
        block = (e, owned, r, o)
        tile = -(-e // 8) * 8
        tail = -(-4 * held // 16) * 16

        def owner_at(d):
            return lax.rem(lax.div(lax.axis_index("ph"), lanes) + d, owners)

        def place_of(j):
            at = lax.axis_index("ph")
            back = lax.rem(lax.div(at, lanes) + owners - j % owners, owners)
            return back * lanes + lax.rem(lax.rem(at, lanes) + lanes - j // owners, lanes)

        def to_owner(x, d):
            pairs = [(p, (p // lanes + d) % owners * lanes + p % lanes) for p in range(ph)]
            return lax.ppermute(x, "ph", pairs)

        def to_lanes(x):
            return [
                lax.ppermute(
                    x, "ph", [(p, p // lanes * lanes + (p % lanes + q) % lanes) for p in range(ph)]
                )
                for q in range(1, lanes)
            ]

        def from_energy(x, t):
            return lax.ppermute(x, "en", [((i + t) % en, i) for i in range(en)])


        def lead(offsets_ref, couplings_ref, inverse_ref, *refs):
            leads, (offsets_at, couplings_at, sems) = refs[:-3], refs[-3:]
            copies = [(offsets_ref, offsets_at), (couplings_ref, couplings_at)]
            for i, d in enumerate(others):
                for n in range(e):
                    for b in range(owned):
                        to = leads[i].at[pl.ds((n * owned + b) * r, r)]
                        copies.append((inverse_ref.at[n, owner_at(d) * owned + b], to))
            copies = [pltpu.make_async_copy(x, y, sems.at[i]) for i, (x, y) in enumerate(copies)]
            for copy in copies:
                copy.start()
            for copy in copies[:2]:
                copy.wait()
            rest = couplings_at[...]
            parts = [offsets_at[...].astype(jnp.float32)]
            for _ in range(3):
                parts.append(rest.astype(BF16).astype(jnp.float32))
                rest = rest - parts[-1]
            row = lax.broadcasted_iota(jnp.int32, (tail, e), 0)
            packed = jnp.zeros((tail, e), jnp.float32)
            for i, x in enumerate(parts):
                for k in range(held):
                    packed = jnp.where(row == i * held + k, x[k : k + 1, :], packed)
            packed = jnp.concatenate([packed, jnp.zeros((tail, LANES - e), jnp.float32)], axis=1)
            for out in leads:
                out[e * owned * r :, :LANES] = packed.astype(BF16)
                out[e * owned * r :, LANES:] = jnp.zeros((tail, o - LANES), BF16)
            for copy in copies[2:]:
                copy.wait()

        def cut(wanted, earlier):
            arrays = after([x for x, *_ in wanted], *earlier)

            def kernel(*refs):
                for i, (_, d, n, k, _) in enumerate(wanted):
                    for b in range(owned):
                        refs[len(wanted) + i][:, b, :r] = refs[i][n : n + k, owner_at(d) * owned + b]

            return call(kernel, [(k, owned, r + spare, o) for *_, k, spare in wanted], "cut", *arrays)

        def join(*refs):
            for d in range(owners):
                refs[owners][d] = refs[d][e * owned * r :, :LANES]
            for d in others:
                for n in range(e):
                    for b in range(owned):
                        at_row = (n * owned + b) * r
                        refs[owners + d][n, b] = refs[d][at_row : at_row + r]

        def from_hbm(kernel, outs, name, scratch, *args):
            far = pl.BlockSpec(memory_space=pltpu.HBM)
            return pl.pallas_call(
                kernel,
                in_specs=[far] * len(args),
                out_specs=[WHOLE] * len(outs),
                out_shape=[jax.ShapeDtypeStruct(x, BF16) for x in outs],
                scratch_shapes=scratch,
                compiler_params=pltpu.CompilerParams(vmem_limit_bytes=61 * 1024 * 1024),
                cost_estimate=COST,
                name=name,
            )(*args)

        def weights(*refs):
            ins, outs = refs[:lanes], refs[lanes:]
            at = lax.axis_index("en")
            row = lax.broadcasted_iota(jnp.int32, (tile, LANES), 0)
            lane = lax.broadcasted_iota(jnp.int32, (tile, LANES), 1)
            pairs = []
            for ref in ins:
                for d in range(owners):
                    x = ref[d].astype(jnp.float32)
                    for k in range(held):
                        shift, *terms = [x[i * held + k : i * held + k + 1, :] for i in range(4)]
                        pairs.append((shift, terms[0] + terms[1] + terms[2]))
            for i, t in enumerate([0] + shifts):
                away = (lax.rem(at + t, en) - at) * e
                for m in range(e):
                    apart = (away + m - lane[:1]).astype(jnp.float32)
                    total = jnp.zeros((1, LANES), jnp.float32)
                    for shift, coupling in pairs:
                        total += jnp.where(shift == apart, coupling, 0.0)
                    spread = jnp.where(row == lane, jnp.broadcast_to(total, (tile, LANES)), 0.0)
                    outs[i][m] = jnp.broadcast_to(
                        jnp.sum(spread, axis=1, keepdims=True), (tile, LANES)
                    )

        def mix(tables, received, d, groups, earlier):
            flat = [x for came in received for x in came]
            stands = [
                [(1 + i, k) for i, x in enumerate(flat) if any(x is y for y in came) for k in range(x.shape[0])]
                for came in received
            ]

            def load(ins, t, m, at_block, b, at):
                if not t:
                    return ins[0][m, at_block, at, :]
                i, k = stands[t - 1][m]
                return ins[i][k, b, at, :]

            def kernel(*refs):
                table_refs, refs = refs[: len(tables)], refs[len(tables) :]
                ins, outs = refs[: 1 + len(flat)], refs[1 + len(flat) :]
                for b in range(owned):
                    at_block = owner_at(d) * owned + b

                    def body(at):
                        totals = weighted(
                            table_refs, range(e), lambda t, m: load(ins, t, m, at_block, b, at)
                        )
                        for out, group in zip(outs, groups):
                            for i, n in enumerate(group):
                                out[i, b, at, :] = totals[n].astype(BF16)

                    chunks(r, body)

            shapes = [(len(group),) + block[1:] for group in groups]
            return call(kernel, shapes, "mix", *after(tables, *earlier), lesser_in, *flat)

        def greater_at(refs, m, d, b, at):
            return refs[d][m, b if d else owner_at(0) * owned + b, at, :]

        def partial_sums(table, rows, groups, earlier):
            def kernel(table_ref, *refs):
                for d in range(owners):
                    for b in range(owned):

                        def body(at):
                            totals = weighted(
                                [table_ref], range(e), lambda t, m: greater_at(refs, m, d, b, at)
                            )
                            for out, group in zip(refs[owners:], groups):
                                for i, n in enumerate(group):
                                    out[i, d, b, at, :] = totals[n].astype(BF16)

                        chunks(r, body)

            (table,) = after([table], *earlier)
            spare = [STEP] + [0] * (len(groups) - 1)
            shapes = [(len(group), owners, owned, r + x, o) for group, x in zip(groups, spare)]
            return call(kernel, shapes, "partial_sums", table, greater_in, *rows)

        def add_partial(group, table, rows, received, earlier):
            def kernel(table_ref, *refs):
                for d in range(owners):
                    for b in range(owned):

                        def body(at):
                            totals = weighted(
                                [table_ref], group, lambda t, m: greater_at(refs, m, d, b, at)
                            )
                            for i in range(len(group)):
                                for ref in refs[owners:-owners]:
                                    totals[i] += ref[i, d, b, at, :].astype(jnp.float32)
                                refs[d - owners][i, b, at, :] = totals[i].astype(BF16)

                        chunks(r, body)

            (table,) = after([table], *earlier)
            shape = (len(group),) + block[1:]
            return call(kernel, [shape] * owners, "add_partial", table, greater_in, *rows, *received)

        def product(jobs, earlier):
            arrays = []
            for job in jobs:
                for x, _ in [*job[0], *job[1]]:
                    if not any(x is y for y in arrays):
                        arrays.append(x)
            where = {id(x): i for i, x in enumerate(arrays)}

            def kernel(*refs):
                outs = refs[-owners:]
                spans = [pl.ds(pl.multiple_of(place_of(j) * r, r), r) for j in range(pieces)]
                for k, job in enumerate(jobs):
                    a_in, s_in = ([(refs[where[id(x)]], index) for x, index in part] for part in job)
                    for b in range(owned):
                        left = jnp.concatenate(
                            [
                                jnp.concatenate([a[(*index, b, slice(None), at)] for at in spans], axis=1)
                                for a, index in a_in[:owners]
                            ],
                            axis=0,
                        )
                        right = jnp.concatenate([x[(*index, b)] for x, index in s_in], axis=0)
                        half = jnp.dot(left, right, preferred_element_type=jnp.float32).astype(BF16)
                        full = lax.dot_general(
                            half,
                            jnp.concatenate([a[(*index, b)] for a, index in a_in], axis=0),
                            (((1,), (1,)), ((), ())),
                            preferred_element_type=jnp.float32,
                        ).astype(BF16)
                        for i in range(owners):
                            for j, at in enumerate(spans):
                                outs[i][k, b, :, at] = full[i * r : (i + 1) * r, j * r : (j + 1) * r]

            shape = (len(jobs),) + block[1:]
            return call(kernel, [shape] * owners, "product", *after(arrays, *earlier))

        def back_to_rows(outs):
            return [outs[0]] + [to_owner(outs[d], owners - d) for d in others]

        def place(result, parts, earlier):
            arrays = []
            for _, _, x, _, _ in parts:
                if not any(x is y for y in arrays):
                    arrays.append(x)
            where = {id(x): i for i, x in enumerate(arrays)}

            def kernel(*refs):
                sems, out = refs[-1], refs[-2]
                copies = [
                    pltpu.make_async_copy(
                        refs[where[id(x)]].at[k],
                        out.at[n, pl.ds(owner_at(d) * owned, owned)],
                        sems.at[i],
                    )
                    for i, (n, d, x, k, _) in enumerate(parts)
                ]
                for copy in copies:
                    copy.start()
                for copy in copies:
                    copy.wait()

            far = pl.BlockSpec(memory_space=pltpu.HBM)
            return pl.pallas_call(
                kernel,
                in_specs=[WHOLE] * len(arrays) + [far] * (result is not None),
                out_specs=far,
                out_shape=jax.ShapeDtypeStruct((e, nb, r, o), BF16),
                scratch_shapes=[pltpu.SemaphoreType.DMA((len(parts),))],
                input_output_aliases={} if result is None else {len(arrays): 0},
                compiler_params=PARAMS,
                cost_estimate=COST,
                name="place",
            )(*after(arrays, *earlier), *([] if result is None else [result]))

        def in_order(own, rows, beside):
            return [own, *rows, *(x for q in range(lanes - 1) for x in [y[q] for y in beside])]

        def at(arrays, index):
            return [(x, index) for x in arrays]

        leads = from_hbm(
            lead,
            [(e * owned * r + tail, o)] * len(others),
            "lead",
            [
                pltpu.VMEM((held, e), jnp.int32),
                pltpu.VMEM((held, e), jnp.float32),
                pltpu.SemaphoreType.DMA((2 + e * owned * len(others),)),
            ],
            offsets.T,
            couplings.T,
            inverse,
        )
        leads_from = [to_owner(x, d) for d, x in zip(others, leads)]
        lessers = cut([(lesser_in, d, 0, e, 0) for d in others], leads)
        lesser_from = [[[from_energy(x, t)] for t in shifts] for x in lessers]
        rest = cut(
            [*((greater_in, d, 0, e, 0) for d in others), (inverse, 0, 0, e, 0), (lesser_in, 0, 0, e - 1, STEP), (lesser_in, 0, e - 1, 1, 0)],
            lessers,
        )
        greaters, inverse_own, lesser_own = rest[: owners - 1], rest[owners - 1], rest[owners:]
        greater_rows = [to_owner(x, d) for d, x in zip(others, greaters)]

        joined, *inverse_rows = call(
            join, [(owners, tail, LANES)] + [block] * len(others), "join", leads[0], *leads_from
        )
        tables = call(
            weights,
            [jax.ShapeDtypeStruct((e, tile, LANES), jnp.float32)] * (1 + len(shifts)),
            "weights",
            joined,
            *to_lanes(joined),
        )
        tables_for = [
            lax.ppermute(table, "en", [(i, (i + t) % en) for i in range(en)])
            for t, table in zip(shifts, tables[1:])
        ]
        lesser_own_from = [[from_energy(x, t) for x in lesser_own] for t in shifts]

        groups = [tuple(range(e - 1)), (e - 1,)]
        singles = [(n,) for n in range(e)]
        lesser_rows = []
        last = []
        for d, came in zip(others, lesser_from):
            last = mix(tables, came, d, groups, last)
            lesser_rows.append([to_owner(x, d) for x in last])
        inverse_own_beside = to_lanes(inverse_own)
        last = [*last, *inverse_own_beside]
        received = [[] for _ in singles]
        for t, table in zip(shifts, tables_for):
            last = partial_sums(table, greater_rows, singles, last)
            for g, part in enumerate(last):
                received[g].append(from_energy(part, t))
        inverse_rows_beside = [to_lanes(x) for x in inverse_rows]
        lesser_mixed = mix(tables, lesser_own_from, 0, groups, last)
        lesser_mixed_beside = [to_lanes(x) for x in lesser_mixed]
        last = lesser_mixed

        def find(groups, n):
            return next((g, group.index(n)) for g, group in enumerate(groups) if n in group)

        def inverse_at(n):
            beside = [at(inverse_own_beside, (n,)), *(at(x, (n,)) for x in inverse_rows_beside)]
            return in_order((inverse_own, (n,)), at(inverse_rows, (n,)), beside)

        def lesser_job(n):
            g, i = find(groups, n)
            h, k = find(groups, n)
            rows = [x[g] for x in lesser_rows]
            beside = [at(lesser_mixed_beside[h], (k,))]
            for x in lesser_rows_beside:
                beside.append(at(x[g], (i,)))
            return inverse_at(n), in_order((lesser_mixed[h], (k,)), at(rows, (i,)), beside)

        lesser_rows_beside = [[*(to_lanes(x) for x in rows[:-1]), None] for rows in lesser_rows]

        results = {"L": None, "G": None}
        waiting = {"L": [], "G": []}

        def put(kind, some, earlier):
            parts = [part for part in waiting[kind] if some(part)]
            waiting[kind] = [part for part in waiting[kind] if not some(part)]
            if parts:
                results[kind] = place(results[kind], parts, earlier)
                return [results[kind]]
            return earlier

        sigmas = {}
        steps = ["L0", "a0", "L1+G0"]
        for n in range(1, e):
            steps += [f"a{n}", f"G{n}", "pL0"] if n == 1 else [f"a{n}", f"G{n}"]
        for step in steps:
            if step[0] == "p":
                last = put(step[1], lambda part: len(step) < 3 or part[4] == int(step[2]), last)
                continue
            if step[0] == "a":
                g = int(step[1])
                group = singles[g]
                sigma = add_partial(group, tables[0], greater_rows, received[g], last)
                last = sigma
                sigmas[g] = (sigma, [to_lanes(x) for x in sigma])
                continue
            jobs, made = [], []
            for kind, g in step.split("+"):
                g = int(g)
                for i, n in enumerate(groups[g] if kind == "L" else singles[g]):
                    made.append((kind, n, g))
                    if kind == "L":
                        jobs.append(lesser_job(n))
                    else:
                        sigma, beside = sigmas[g]
                        beside = [at(x, (i,)) for x in beside]
                        jobs.append((inverse_at(n), in_order((sigma[0], (i,)), at(sigma[1:], (i,)), beside)))
            last = product(jobs, last)
            back = back_to_rows(last)
            if step == "L0":
                for rows, beside in zip(lesser_rows, lesser_rows_beside):
                    rows[-1] = after([rows[-1]], *last)[0]
                    beside[-1] = to_lanes(rows[-1])
            for k, (kind, n, g) in enumerate(made):
                waiting[kind] += [(n, d, x, k, g) for d, x in enumerate(back)]
        last = put("L", lambda part: part[1] == 0, last)
        last = put("G", lambda part: part[1] == 0, last)
        for kind, g in [*(("L", g) for g in range(len(groups))), *(("G", n) for n in range(e))]:
            last = put(kind, lambda part: part[4] == g, last)
        lesser_out, greater_out = results["L"], results["G"]
        return lesser_out, greater_out

    block, coupled = P("en", "blk", "ph", None), P("en", "ph")
    return jax.shard_map(
        on_device,
        mesh=mesh,
        in_specs=(block, block, block, coupled, coupled),
        out_specs=(block, block),
        check_vma=False,
    )
```

```python
import math

import jax
import jax.numpy as jnp
from jax import lax
from jax.experimental import pallas as pl
from jax.experimental.pallas import tpu as pltpu
from jax.sharding import PartitionSpec as P

MAXOFF = 9
BF16 = jnp.bfloat16
STEP = 16
LANES = 128
WHOLE = pl.BlockSpec(memory_space=pltpu.VMEM)
PARAMS = pltpu.CompilerParams(vmem_limit_bytes=12 * 1024 * 1024)
COST = pl.CostEstimate(flops=1, bytes_accessed=1, transcendentals=0)


def call(kernel, outs, name, *args):
    outs = [x if isinstance(x, jax.ShapeDtypeStruct) else jax.ShapeDtypeStruct(x, BF16) for x in outs]
    return pl.pallas_call(
        kernel,
        in_specs=[WHOLE] * len(args),
        out_specs=[WHOLE] * len(outs),
        out_shape=outs,
        compiler_params=PARAMS,
        cost_estimate=COST,
        name=name,
    )(*args)


def after(xs, *earlier):
    return lax.optimization_barrier((tuple(xs), earlier))[0]


def chunks(rows, body):
    @pl.loop(0, rows // STEP, unroll=math.gcd(rows // STEP, 4))
    def _(i):
        body(pl.ds(pl.multiple_of(i * STEP, STEP), STEP))


def weighted(tables, energies, load):
    totals = [None] * len(energies)
    for t, table in enumerate(tables):
        for m in range(table.shape[0]):
            g = load(t, m).astype(jnp.float32)
            for i, n in enumerate(energies):
                row = table[m, n : n + 1, :]
                term = jnp.concatenate([row] * (g.shape[1] // LANES), axis=1) * g
                totals[i] = term if totals[i] is None else totals[i] + term
    return totals


def solution(mesh):
    en, ph = mesh.shape["en"], mesh.shape["ph"]

    def on_device(lesser_in, greater_in, inverse, offsets, couplings):
        e, nb, r, o = lesser_in.shape
        held = offsets.shape[1]
        owners = math.gcd(nb, ph)
        lanes = ph // owners
        owned = nb // owners
        pieces = ph
        others = range(1, owners)
        reach = (MAXOFF + e - 1) // e
        shifts = [t for t in range(1, en) if t <= reach or en - t <= reach]
        block = (e, owned, r, o)
        tile = -(-e // 8) * 8
        tail = -(-4 * held // 16) * 16

        def owner_at(d):
            return lax.rem(lax.div(lax.axis_index("ph"), lanes) + d, owners)

        def place_of(j):
            at = lax.axis_index("ph")
            back = lax.rem(lax.div(at, lanes) + owners - j % owners, owners)
            return back * lanes + lax.rem(lax.rem(at, lanes) + lanes - j // owners, lanes)

        def to_owner(x, d):
            pairs = [(p, (p // lanes + d) % owners * lanes + p % lanes) for p in range(ph)]
            return lax.ppermute(x, "ph", pairs)

        def to_lanes(x):
            return [
                lax.ppermute(
                    x, "ph", [(p, p // lanes * lanes + (p % lanes + q) % lanes) for p in range(ph)]
                )
                for q in range(1, lanes)
            ]

        def from_energy(x, t):
            return lax.ppermute(x, "en", [((i + t) % en, i) for i in range(en)])


        def lead(offsets_ref, couplings_ref, inverse_ref, *refs):
            leads, (offsets_at, couplings_at, sems) = refs[:-3], refs[-3:]
            copies = [(offsets_ref, offsets_at), (couplings_ref, couplings_at)]
            for i, d in enumerate(others):
                for n in range(e):
                    for b in range(owned):
                        to = leads[i].at[pl.ds((n * owned + b) * r, r)]
                        copies.append((inverse_ref.at[n, owner_at(d) * owned + b], to))
            copies = [pltpu.make_async_copy(x, y, sems.at[i]) for i, (x, y) in enumerate(copies)]
            for copy in copies:
                copy.start()
            for copy in copies[:2]:
                copy.wait()
            rest = couplings_at[...]
            parts = [offsets_at[...].astype(jnp.float32)]
            for _ in range(3):
                parts.append(rest.astype(BF16).astype(jnp.float32))
                rest = rest - parts[-1]
            row = lax.broadcasted_iota(jnp.int32, (tail, e), 0)
            packed = jnp.zeros((tail, e), jnp.float32)
            for i, x in enumerate(parts):
                for k in range(held):
                    packed = jnp.where(row == i * held + k, x[k : k + 1, :], packed)
            packed = jnp.concatenate([packed, jnp.zeros((tail, LANES - e), jnp.float32)], axis=1)
            for out in leads:
                out[e * owned * r :, :LANES] = packed.astype(BF16)
                out[e * owned * r :, LANES:] = jnp.zeros((tail, o - LANES), BF16)
            for copy in copies[2:]:
                copy.wait()

        def cut(wanted, earlier):
            arrays = after([x for x, *_ in wanted], *earlier)

            def kernel(*refs):
                for i, (_, d, n, k, _) in enumerate(wanted):
                    for b in range(owned):
                        refs[len(wanted) + i][:, b, :r] = refs[i][n : n + k, owner_at(d) * owned + b]

            return call(kernel, [(k, owned, r + spare, o) for *_, k, spare in wanted], "cut", *arrays)

        def join(*refs):
            for d in range(owners):
                refs[owners][d] = refs[d][e * owned * r :, :LANES]
            for d in others:
                for n in range(e):
                    for b in range(owned):
                        at_row = (n * owned + b) * r
                        refs[owners + d][n, b] = refs[d][at_row : at_row + r]

        def from_hbm(kernel, outs, name, scratch, *args):
            far = pl.BlockSpec(memory_space=pltpu.HBM)
            return pl.pallas_call(
                kernel,
                in_specs=[far] * len(args),
                out_specs=[WHOLE] * len(outs),
                out_shape=[jax.ShapeDtypeStruct(x, BF16) for x in outs],
                scratch_shapes=scratch,
                compiler_params=pltpu.CompilerParams(vmem_limit_bytes=61 * 1024 * 1024),
                cost_estimate=COST,
                name=name,
            )(*args)

        def weights(*refs):
            ins, outs = refs[:lanes], refs[lanes:]
            at = lax.axis_index("en")
            row = lax.broadcasted_iota(jnp.int32, (tile, LANES), 0)
            lane = lax.broadcasted_iota(jnp.int32, (tile, LANES), 1)
            pairs = []
            for ref in ins:
                for d in range(owners):
                    x = ref[d].astype(jnp.float32)
                    for k in range(held):
                        shift, *terms = [x[i * held + k : i * held + k + 1, :] for i in range(4)]
                        pairs.append((shift, terms[0] + terms[1] + terms[2]))
            for i, t in enumerate([0] + shifts):
                away = (lax.rem(at + t, en) - at) * e
                for m in range(e):
                    apart = (away + m - lane[:1]).astype(jnp.float32)
                    total = jnp.zeros((1, LANES), jnp.float32)
                    for shift, coupling in pairs:
                        total += jnp.where(shift == apart, coupling, 0.0)
                    spread = jnp.where(row == lane, jnp.broadcast_to(total, (tile, LANES)), 0.0)
                    outs[i][m] = jnp.broadcast_to(
                        jnp.sum(spread, axis=1, keepdims=True), (tile, LANES)
                    )

        def mix(tables, received, d, groups, earlier):
            flat = [x for came in received for x in came]
            stands = [
                [(1 + i, k) for i, x in enumerate(flat) if any(x is y for y in came) for k in range(x.shape[0])]
                for came in received
            ]

            def load(ins, t, m, at_block, b, at):
                if not t:
                    return ins[0][m, at_block, at, :]
                i, k = stands[t - 1][m]
                return ins[i][k, b, at, :]

            def kernel(*refs):
                table_refs, refs = refs[: len(tables)], refs[len(tables) :]
                ins, outs = refs[: 1 + len(flat)], refs[1 + len(flat) :]
                for b in range(owned):
                    at_block = owner_at(d) * owned + b

                    def body(at):
                        totals = weighted(
                            table_refs, range(e), lambda t, m: load(ins, t, m, at_block, b, at)
                        )
                        for out, group in zip(outs, groups):
                            for i, n in enumerate(group):
                                out[i, b, at, :] = totals[n].astype(BF16)

                    chunks(r, body)

            shapes = [(len(group),) + block[1:] for group in groups]
            return call(kernel, shapes, "mix", *after(tables, *earlier), lesser_in, *flat)

        def greater_at(refs, m, d, b, at):
            return refs[d][m, b if d else owner_at(0) * owned + b, at, :]

        def partial_sums(table, rows, groups, earlier):
            def kernel(table_ref, *refs):
                for d in range(owners):
                    for b in range(owned):

                        def body(at):
                            totals = weighted(
                                [table_ref], range(e), lambda t, m: greater_at(refs, m, d, b, at)
                            )
                            for out, group in zip(refs[owners:], groups):
                                for i, n in enumerate(group):
                                    out[i, d, b, at, :] = totals[n].astype(BF16)

                        chunks(r, body)

            (table,) = after([table], *earlier)
            spare = [STEP] + [0] * (len(groups) - 1)
            shapes = [(len(group), owners, owned, r + x, o) for group, x in zip(groups, spare)]
            return call(kernel, shapes, "partial_sums", table, greater_in, *rows)

        def add_partial(group, table, rows, received, earlier):
            def kernel(table_ref, *refs):
                for d in range(owners):
                    for b in range(owned):

                        def body(at):
                            totals = weighted(
                                [table_ref], group, lambda t, m: greater_at(refs, m, d, b, at)
                            )
                            for i in range(len(group)):
                                for ref in refs[owners:-owners]:
                                    totals[i] += ref[i, d, b, at, :].astype(jnp.float32)
                                refs[d - owners][i, b, at, :] = totals[i].astype(BF16)

                        chunks(r, body)

            (table,) = after([table], *earlier)
            shape = (len(group),) + block[1:]
            return call(kernel, [shape] * owners, "add_partial", table, greater_in, *rows, *received)

        def product(jobs, earlier, pad=0):
            arrays = []
            for job in jobs:
                for x, _ in [*job[0], *job[1]]:
                    if not any(x is y for y in arrays):
                        arrays.append(x)
            where = {id(x): i for i, x in enumerate(arrays)}

            def kernel(*refs):
                outs = refs[-owners:]
                spans = [pl.ds(pl.multiple_of(place_of(j) * r, r), r) for j in range(pieces)]
                for k, job in enumerate(jobs):
                    a_in, s_in = ([(refs[where[id(x)]], index) for x, index in part] for part in job)
                    for b in range(owned):
                        left = jnp.concatenate(
                            [
                                jnp.concatenate([a[(*index, b, slice(None), at)] for at in spans], axis=1)
                                for a, index in a_in[:owners]
                            ],
                            axis=0,
                        )
                        right = jnp.concatenate([x[(*index, b)] for x, index in s_in], axis=0)
                        half = jnp.dot(left, right, preferred_element_type=jnp.float32).astype(BF16)
                        full = lax.dot_general(
                            half,
                            jnp.concatenate([a[(*index, b)] for a, index in a_in], axis=0),
                            (((1,), (1,)), ((), ())),
                            preferred_element_type=jnp.float32,
                        ).astype(BF16)
                        for i in range(owners):
                            for j, at in enumerate(spans):
                                piece = full[i * r : (i + 1) * r, j * r : (j + 1) * r]
                                if len(shapes[i]) == 2:
                                    outs[i][pl.ds((k * owned + b) * r, r), at] = piece
                                else:
                                    outs[i][k, b, :, at] = piece

            shape = (len(jobs),) + block[1:]
            shapes = [(len(jobs) * owned * r + pad, o) if d and pad else shape for d in range(owners)]
            return call(kernel, shapes, "product", *after(arrays, *earlier))

        def back_to_rows(outs):
            return [outs[0]] + [to_owner(outs[d], owners - d) for d in others]

        def place(result, parts, earlier):
            arrays = []
            for _, _, x, _, _ in parts:
                if not any(x is y for y in arrays):
                    arrays.append(x)
            where = {id(x): i for i, x in enumerate(arrays)}

            def kernel(*refs):
                sems, out = refs[-1], refs[-2]
                copies = []
                for n, d, x, k, _ in parts:
                    ref = refs[where[id(x)]]
                    for b in range(owned):
                        one = ref.at[pl.ds((k * owned + b) * r, r)] if len(x.shape) == 2 else ref.at[k, b]
                        to = out.at[n, owner_at(d) * owned + b]
                        copies.append(pltpu.make_async_copy(one, to, sems.at[len(copies)]))
                for copy in copies:
                    copy.start()
                for copy in copies:
                    copy.wait()

            far = pl.BlockSpec(memory_space=pltpu.HBM)
            return pl.pallas_call(
                kernel,
                in_specs=[WHOLE] * len(arrays) + [far] * (result is not None),
                out_specs=far,
                out_shape=jax.ShapeDtypeStruct((e, nb, r, o), BF16),
                scratch_shapes=[pltpu.SemaphoreType.DMA((len(parts) * owned,))],
                input_output_aliases={} if result is None else {len(arrays): 0},
                compiler_params=PARAMS,
                cost_estimate=COST,
                name="place",
            )(*after(arrays, *earlier), *([] if result is None else [result]))

        def in_order(own, rows, beside):
            return [own, *rows, *(x for q in range(lanes - 1) for x in [y[q] for y in beside])]

        def at(arrays, index):
            return [(x, index) for x in arrays]

        leads = from_hbm(
            lead,
            [(e * owned * r + tail, o)] * len(others),
            "lead",
            [
                pltpu.VMEM((held, e), jnp.int32),
                pltpu.VMEM((held, e), jnp.float32),
                pltpu.SemaphoreType.DMA((2 + e * owned * len(others),)),
            ],
            offsets.T,
            couplings.T,
            inverse,
        )
        leads_from = [to_owner(x, d) for d, x in zip(others, leads)]
        lessers = cut([(lesser_in, d, 0, e, 0) for d in others], leads)
        lesser_from = [[[from_energy(x, t)] for t in shifts] for x in lessers]
        rest = cut(
            [*((greater_in, d, 0, e, 0) for d in others), (inverse, 0, 0, e, 0), (lesser_in, 0, 0, e - 1, STEP), (lesser_in, 0, e - 1, 1, 0)],
            lessers,
        )
        greaters, inverse_own, lesser_own = rest[: owners - 1], rest[owners - 1], rest[owners:]
        greater_rows = [to_owner(x, d) for d, x in zip(others, greaters)]

        joined, *inverse_rows = call(
            join, [(owners, tail, LANES)] + [block] * len(others), "join", leads[0], *leads_from
        )
        tables = call(
            weights,
            [jax.ShapeDtypeStruct((e, tile, LANES), jnp.float32)] * (1 + len(shifts)),
            "weights",
            joined,
            *to_lanes(joined),
        )
        tables_for = [
            lax.ppermute(table, "en", [(i, (i + t) % en) for i in range(en)])
            for t, table in zip(shifts, tables[1:])
        ]
        lesser_own_from = [[from_energy(x, t) for x in lesser_own] for t in shifts]

        groups = [tuple(range(e - 1)), (e - 1,)]
        singles = [(n,) for n in range(e)]
        lesser_rows = []
        last = []
        for d, came in zip(others, lesser_from):
            last = mix(tables, came, d, groups, last)
            lesser_rows.append([to_owner(x, d) for x in last])
        inverse_own_beside = to_lanes(inverse_own)
        last = [*last, *inverse_own_beside]
        received = [[] for _ in singles]
        for t, table in zip(shifts, tables_for):
            last = partial_sums(table, greater_rows, singles, last)
            for g, part in enumerate(last):
                received[g].append(from_energy(part, t))
        inverse_rows_beside = [to_lanes(x) for x in inverse_rows]
        lesser_mixed = mix(tables, lesser_own_from, 0, groups, last)
        lesser_mixed_beside = [to_lanes(x) for x in lesser_mixed]
        last = lesser_mixed

        def find(groups, n):
            return next((g, group.index(n)) for g, group in enumerate(groups) if n in group)

        def inverse_at(n):
            beside = [at(inverse_own_beside, (n,)), *(at(x, (n,)) for x in inverse_rows_beside)]
            return in_order((inverse_own, (n,)), at(inverse_rows, (n,)), beside)

        def lesser_job(n):
            g, i = find(groups, n)
            h, k = find(groups, n)
            rows = [x[g] for x in lesser_rows]
            beside = [at(lesser_mixed_beside[h], (k,))]
            for x in lesser_rows_beside:
                beside.append(at(x[g], (i,)))
            return inverse_at(n), in_order((lesser_mixed[h], (k,)), at(rows, (i,)), beside)

        lesser_rows_beside = [[*(to_lanes(x) for x in rows[:-1]), None] for rows in lesser_rows]

        results = {"L": None, "G": None}
        waiting = {"L": [], "G": []}

        def put(kind, some, earlier):
            parts = [part for part in waiting[kind] if some(part)]
            waiting[kind] = [part for part in waiting[kind] if not some(part)]
            if parts:
                results[kind] = place(results[kind], parts, earlier)
                return [results[kind]]
            return earlier

        sigmas = {}
        steps = ["L0", "a0", "L1+G0"]
        for n in range(1, e):
            steps += [f"a{n}", f"G{n}", "pL0"] if n == 1 else [f"a{n}", f"G{n}"]
        for step in steps:
            if step[0] == "p":
                last = put(step[1], lambda part: len(step) < 3 or part[4] == int(step[2]), last)
                continue
            if step[0] == "a":
                g = int(step[1])
                group = singles[g]
                sigma = add_partial(group, tables[0], greater_rows, received[g], last)
                last = sigma
                sigmas[g] = (sigma, [to_lanes(x) for x in sigma])
                continue
            jobs, made = [], []
            for kind, g in step.split("+"):
                g = int(g)
                for i, n in enumerate(groups[g] if kind == "L" else singles[g]):
                    made.append((kind, n, g))
                    if kind == "L":
                        jobs.append(lesser_job(n))
                    else:
                        sigma, beside = sigmas[g]
                        beside = [at(x, (i,)) for x in beside]
                        jobs.append((inverse_at(n), in_order((sigma[0], (i,)), at(sigma[1:], (i,)), beside)))
            last = product(jobs, last, STEP if step == "L0" else 0)
            back = back_to_rows(last)
            if step == "L0":
                for rows, beside in zip(lesser_rows, lesser_rows_beside):
                    rows[-1] = after([rows[-1]], *last)[0]
                    beside[-1] = to_lanes(rows[-1])
            for k, (kind, n, g) in enumerate(made):
                waiting[kind] += [(n, d, x, k, g) for d, x in enumerate(back)]
        last = put("L", lambda part: part[1] == 0, last)
        last = put("G", lambda part: part[1] == 0, last)
        for kind, g in [*(("L", g) for g in range(len(groups))), *(("G", n) for n in range(e))]:
            last = put(kind, lambda part: part[4] == g, last)
        lesser_out, greater_out = results["L"], results["G"]
        return lesser_out, greater_out

    block, coupled = P("en", "blk", "ph", None), P("en", "ph")
    return jax.shard_map(
        on_device,
        mesh=mesh,
        in_specs=(block, block, block, coupled, coupled),
        out_specs=(block, block),
        check_vma=False,
    )
```

```python
import math

import jax
import jax.numpy as jnp
from jax import lax
from jax.experimental import pallas as pl
from jax.experimental.pallas import tpu as pltpu
from jax.sharding import PartitionSpec as P

MAXOFF = 9
BF16 = jnp.bfloat16
STEP = 16
LANES = 128
WHOLE = pl.BlockSpec(memory_space=pltpu.VMEM)
PARAMS = pltpu.CompilerParams(vmem_limit_bytes=12 * 1024 * 1024)
COST = pl.CostEstimate(flops=1, bytes_accessed=1, transcendentals=0)


def call(kernel, outs, name, *args):
    outs = [x if isinstance(x, jax.ShapeDtypeStruct) else jax.ShapeDtypeStruct(x, BF16) for x in outs]
    return pl.pallas_call(
        kernel,
        in_specs=[WHOLE] * len(args),
        out_specs=[WHOLE] * len(outs),
        out_shape=outs,
        compiler_params=PARAMS,
        cost_estimate=COST,
        name=name,
    )(*args)


def after(xs, *earlier):
    return lax.optimization_barrier((tuple(xs), earlier))[0]


def chunks(rows, body):
    @pl.loop(0, rows // STEP, unroll=math.gcd(rows // STEP, 4))
    def _(i):
        body(pl.ds(pl.multiple_of(i * STEP, STEP), STEP))


def weighted(tables, energies, load):
    totals = [None] * len(energies)
    for t, table in enumerate(tables):
        for m in range(table.shape[0]):
            g = load(t, m).astype(jnp.float32)
            for i, n in enumerate(energies):
                row = table[m, n : n + 1, :]
                term = jnp.concatenate([row] * (g.shape[1] // LANES), axis=1) * g
                totals[i] = term if totals[i] is None else totals[i] + term
    return totals


def solution(mesh):
    en, ph = mesh.shape["en"], mesh.shape["ph"]

    def on_device(lesser_in, greater_in, inverse, offsets, couplings):
        e, nb, r, o = lesser_in.shape
        held = offsets.shape[1]
        owners = math.gcd(nb, ph)
        lanes = ph // owners
        owned = nb // owners
        pieces = ph
        others = range(1, owners)
        reach = (MAXOFF + e - 1) // e
        shifts = [t for t in range(1, en) if t <= reach or en - t <= reach]
        block = (e, owned, r, o)
        tile = -(-e // 8) * 8
        tail = -(-4 * held // 16) * 16

        def owner_at(d):
            return lax.rem(lax.div(lax.axis_index("ph"), lanes) + d, owners)

        def place_of(j):
            at = lax.axis_index("ph")
            back = lax.rem(lax.div(at, lanes) + owners - j % owners, owners)
            return back * lanes + lax.rem(lax.rem(at, lanes) + lanes - j // owners, lanes)

        def to_owner(x, d):
            pairs = [(p, (p // lanes + d) % owners * lanes + p % lanes) for p in range(ph)]
            return lax.ppermute(x, "ph", pairs)

        def to_lanes(x):
            return [
                lax.ppermute(
                    x, "ph", [(p, p // lanes * lanes + (p % lanes + q) % lanes) for p in range(ph)]
                )
                for q in range(1, lanes)
            ]

        def from_energy(x, t):
            return lax.ppermute(x, "en", [((i + t) % en, i) for i in range(en)])


        def lead(offsets_ref, couplings_ref, inverse_ref, *refs):
            leads, (offsets_at, couplings_at, sems) = refs[:-3], refs[-3:]
            copies = [(offsets_ref, offsets_at), (couplings_ref, couplings_at)]
            for i, d in enumerate(others):
                for n in range(e):
                    for b in range(owned):
                        to = leads[i].at[pl.ds((n * owned + b) * r, r)]
                        copies.append((inverse_ref.at[n, owner_at(d) * owned + b], to))
            copies = [pltpu.make_async_copy(x, y, sems.at[i]) for i, (x, y) in enumerate(copies)]
            for copy in copies[2:] + copies[:2]:
                copy.start()
            for copy in copies[:2]:
                copy.wait()
            rest = couplings_at[...]
            parts = [offsets_at[...].astype(jnp.float32)]
            for _ in range(3):
                parts.append(rest.astype(BF16).astype(jnp.float32))
                rest = rest - parts[-1]
            row = lax.broadcasted_iota(jnp.int32, (tail, e), 0)
            packed = jnp.zeros((tail, e), jnp.float32)
            for i, x in enumerate(parts):
                for k in range(held):
                    packed = jnp.where(row == i * held + k, x[k : k + 1, :], packed)
            packed = jnp.concatenate([packed, jnp.zeros((tail, LANES - e), jnp.float32)], axis=1)
            for out in leads:
                out[e * owned * r :, :LANES] = packed.astype(BF16)
                out[e * owned * r :, LANES:] = jnp.zeros((tail, o - LANES), BF16)
            for copy in copies[2:]:
                copy.wait()

        def cut(wanted, earlier):
            arrays = after([x for x, *_ in wanted], *earlier)

            def kernel(*refs):
                for i, (_, d, n, k, _) in enumerate(wanted):
                    for b in range(owned):
                        refs[len(wanted) + i][:, b, :r] = refs[i][n : n + k, owner_at(d) * owned + b]

            return call(kernel, [(k, owned, r + spare, o) for *_, k, spare in wanted], "cut", *arrays)

        def join(*refs):
            for d in range(owners):
                refs[owners][d] = refs[d][e * owned * r :, :LANES]
            for d in others:
                for n in range(e):
                    for b in range(owned):
                        at_row = (n * owned + b) * r
                        refs[owners + d][n, b] = refs[d][at_row : at_row + r]

        def from_hbm(kernel, outs, name, scratch, *args):
            far = pl.BlockSpec(memory_space=pltpu.HBM)
            return pl.pallas_call(
                kernel,
                in_specs=[far] * len(args),
                out_specs=[WHOLE] * len(outs),
                out_shape=[jax.ShapeDtypeStruct(x, BF16) for x in outs],
                scratch_shapes=scratch,
                compiler_params=pltpu.CompilerParams(vmem_limit_bytes=61 * 1024 * 1024),
                cost_estimate=COST,
                name=name,
            )(*args)

        def weights(*refs):
            ins, outs = refs[:lanes], refs[lanes:]
            at = lax.axis_index("en")
            row = lax.broadcasted_iota(jnp.int32, (tile, LANES), 0)
            lane = lax.broadcasted_iota(jnp.int32, (tile, LANES), 1)
            pairs = []
            for ref in ins:
                for d in range(owners):
                    x = ref[d].astype(jnp.float32)
                    for k in range(held):
                        shift, *terms = [x[i * held + k : i * held + k + 1, :] for i in range(4)]
                        pairs.append((shift, terms[0] + terms[1] + terms[2]))
            for i, t in enumerate([0] + shifts):
                away = (lax.rem(at + t, en) - at) * e
                for m in range(e):
                    apart = (away + m - lane[:1]).astype(jnp.float32)
                    total = jnp.zeros((1, LANES), jnp.float32)
                    for shift, coupling in pairs:
                        total += jnp.where(shift == apart, coupling, 0.0)
                    spread = jnp.where(row == lane, jnp.broadcast_to(total, (tile, LANES)), 0.0)
                    outs[i][m] = jnp.broadcast_to(
                        jnp.sum(spread, axis=1, keepdims=True), (tile, LANES)
                    )

        def mix(tables, received, d, groups, earlier):
            flat = [x for came in received for x in came]
            stands = [
                [(1 + i, k) for i, x in enumerate(flat) if any(x is y for y in came) for k in range(x.shape[0])]
                for came in received
            ]

            def load(ins, t, m, at_block, b, at):
                if not t:
                    return ins[0][m, at_block, at, :]
                i, k = stands[t - 1][m]
                return ins[i][k, b, at, :]

            def kernel(*refs):
                table_refs, refs = refs[: len(tables)], refs[len(tables) :]
                ins, outs = refs[: 1 + len(flat)], refs[1 + len(flat) :]
                for b in range(owned):
                    at_block = owner_at(d) * owned + b

                    def body(at):
                        totals = weighted(
                            table_refs, range(e), lambda t, m: load(ins, t, m, at_block, b, at)
                        )
                        for out, group in zip(outs, groups):
                            for i, n in enumerate(group):
                                out[i, b, at, :] = totals[n].astype(BF16)

                    chunks(r, body)

            shapes = [(len(group),) + block[1:] for group in groups]
            return call(kernel, shapes, "mix", *after(tables, *earlier), lesser_in, *flat)

        def greater_at(refs, m, d, b, at):
            return refs[d][m, b if d else owner_at(0) * owned + b, at, :]

        def partial_sums(table, rows, groups, earlier):
            def kernel(table_ref, *refs):
                for d in range(owners):
                    for b in range(owned):

                        def body(at):
                            totals = weighted(
                                [table_ref], range(e), lambda t, m: greater_at(refs, m, d, b, at)
                            )
                            for out, group in zip(refs[owners:], groups):
                                for i, n in enumerate(group):
                                    out[i, d, b, at, :] = totals[n].astype(BF16)

                        chunks(r, body)

            (table,) = after([table], *earlier)
            spare = [STEP] + [0] * (len(groups) - 1)
            shapes = [(len(group), owners, owned, r + x, o) for group, x in zip(groups, spare)]
            return call(kernel, shapes, "partial_sums", table, greater_in, *rows)

        def add_partial(group, table, rows, received, earlier):
            def kernel(table_ref, *refs):
                for d in range(owners):
                    for b in range(owned):

                        def body(at):
                            totals = weighted(
                                [table_ref], group, lambda t, m: greater_at(refs, m, d, b, at)
                            )
                            for i in range(len(group)):
                                for ref in refs[owners:-owners]:
                                    totals[i] += ref[i, d, b, at, :].astype(jnp.float32)
                                refs[d - owners][i, b, at, :] = totals[i].astype(BF16)

                        chunks(r, body)

            (table,) = after([table], *earlier)
            shape = (len(group),) + block[1:]
            return call(kernel, [shape] * owners, "add_partial", table, greater_in, *rows, *received)

        def product(jobs, earlier, pad=0):
            arrays = []
            for job in jobs:
                for x, _ in [*job[0], *job[1]]:
                    if not any(x is y for y in arrays):
                        arrays.append(x)
            where = {id(x): i for i, x in enumerate(arrays)}

            def kernel(*refs):
                outs = refs[-owners:]
                spans = [pl.ds(pl.multiple_of(place_of(j) * r, r), r) for j in range(pieces)]
                for k, job in enumerate(jobs):
                    a_in, s_in = ([(refs[where[id(x)]], index) for x, index in part] for part in job)
                    for b in range(owned):
                        left = jnp.concatenate(
                            [
                                jnp.concatenate([a[(*index, b, slice(None), at)] for at in spans], axis=1)
                                for a, index in a_in[:owners]
                            ],
                            axis=0,
                        )
                        right = jnp.concatenate([x[(*index, b)] for x, index in s_in], axis=0)
                        half = jnp.dot(left, right, preferred_element_type=jnp.float32).astype(BF16)
                        full = lax.dot_general(
                            half,
                            jnp.concatenate([a[(*index, b)] for a, index in a_in], axis=0),
                            (((1,), (1,)), ((), ())),
                            preferred_element_type=jnp.float32,
                        ).astype(BF16)
                        for i in range(owners):
                            for j, at in enumerate(spans):
                                piece = full[i * r : (i + 1) * r, j * r : (j + 1) * r]
                                if len(shapes[i]) == 2:
                                    outs[i][pl.ds((k * owned + b) * r, r), at] = piece
                                else:
                                    outs[i][k, b, :, at] = piece

            shape = (len(jobs),) + block[1:]
            shapes = [(len(jobs) * owned * r + pad, o) if d and pad else shape for d in range(owners)]
            return call(kernel, shapes, "product", *after(arrays, *earlier))

        def back_to_rows(outs):
            return [outs[0]] + [to_owner(outs[d], owners - d) for d in others]

        def place(result, parts, earlier):
            arrays = []
            for _, _, x, _, _ in parts:
                if not any(x is y for y in arrays):
                    arrays.append(x)
            where = {id(x): i for i, x in enumerate(arrays)}

            def kernel(*refs):
                sems, out = refs[-1], refs[-2]
                copies = []
                for n, d, x, k, _ in parts:
                    ref = refs[where[id(x)]]
                    for b in range(owned):
                        one = ref.at[pl.ds((k * owned + b) * r, r)] if len(x.shape) == 2 else ref.at[k, b]
                        to = out.at[n, owner_at(d) * owned + b]
                        copies.append(pltpu.make_async_copy(one, to, sems.at[len(copies)]))
                for copy in copies:
                    copy.start()
                for copy in copies:
                    copy.wait()

            far = pl.BlockSpec(memory_space=pltpu.HBM)
            return pl.pallas_call(
                kernel,
                in_specs=[WHOLE] * len(arrays) + [far] * (result is not None),
                out_specs=far,
                out_shape=jax.ShapeDtypeStruct((e, nb, r, o), BF16),
                scratch_shapes=[pltpu.SemaphoreType.DMA((len(parts) * owned,))],
                input_output_aliases={} if result is None else {len(arrays): 0},
                compiler_params=PARAMS,
                cost_estimate=COST,
                name="place",
            )(*after(arrays, *earlier), *([] if result is None else [result]))

        def in_order(own, rows, beside):
            return [own, *rows, *(x for q in range(lanes - 1) for x in [y[q] for y in beside])]

        def at(arrays, index):
            return [(x, index) for x in arrays]

        leads = from_hbm(
            lead,
            [(e * owned * r + tail, o)] * len(others),
            "lead",
            [
                pltpu.VMEM((held, e), jnp.int32),
                pltpu.VMEM((held, e), jnp.float32),
                pltpu.SemaphoreType.DMA((2 + e * owned * len(others),)),
            ],
            offsets.T,
            couplings.T,
            inverse,
        )
        leads_from = [to_owner(x, d) for d, x in zip(others, leads)]
        lessers = cut([(lesser_in, d, 0, e, 0) for d in others], leads)
        lesser_from = [[[from_energy(x, t)] for t in shifts] for x in lessers]
        rest = cut(
            [*((greater_in, d, 0, e, 0) for d in others), (inverse, 0, 0, e, 0), (lesser_in, 0, 0, e - 1, STEP), (lesser_in, 0, e - 1, 1, 0)],
            lessers,
        )
        greaters, inverse_own, lesser_own = rest[: owners - 1], rest[owners - 1], rest[owners:]
        greater_rows = [to_owner(x, d) for d, x in zip(others, greaters)]

        joined, *inverse_rows = call(
            join, [(owners, tail, LANES)] + [block] * len(others), "join", leads[0], *leads_from
        )
        tables = call(
            weights,
            [jax.ShapeDtypeStruct((e, tile, LANES), jnp.float32)] * (1 + len(shifts)),
            "weights",
            joined,
            *to_lanes(joined),
        )
        tables_for = [
            lax.ppermute(table, "en", [(i, (i + t) % en) for i in range(en)])
            for t, table in zip(shifts, tables[1:])
        ]
        lesser_own_from = [[from_energy(x, t) for x in lesser_own] for t in shifts]

        groups = [tuple(range(e - 1)), (e - 1,)]
        singles = [(n,) for n in range(e)]
        lesser_rows = []
        last = []
        for d, came in zip(others, lesser_from):
            last = mix(tables, came, d, groups, last)
            lesser_rows.append([to_owner(x, d) for x in last])
        inverse_own_beside = to_lanes(inverse_own)
        last = [*last, *inverse_own_beside]
        received = [[] for _ in singles]
        for t, table in zip(shifts, tables_for):
            last = partial_sums(table, greater_rows, singles, last)
            for g, part in enumerate(last):
                received[g].append(from_energy(part, t))
        inverse_rows_beside = [to_lanes(x) for x in inverse_rows]
        lesser_mixed = mix(tables, lesser_own_from, 0, groups, last)
        lesser_mixed_beside = [to_lanes(x) for x in lesser_mixed]
        last = lesser_mixed

        def find(groups, n):
            return next((g, group.index(n)) for g, group in enumerate(groups) if n in group)

        def inverse_at(n):
            beside = [at(inverse_own_beside, (n,)), *(at(x, (n,)) for x in inverse_rows_beside)]
            return in_order((inverse_own, (n,)), at(inverse_rows, (n,)), beside)

        def lesser_job(n):
            g, i = find(groups, n)
            h, k = find(groups, n)
            rows = [x[g] for x in lesser_rows]
            beside = [at(lesser_mixed_beside[h], (k,))]
            for x in lesser_rows_beside:
                beside.append(at(x[g], (i,)))
            return inverse_at(n), in_order((lesser_mixed[h], (k,)), at(rows, (i,)), beside)

        lesser_rows_beside = [[*(to_lanes(x) for x in rows[:-1]), None] for rows in lesser_rows]

        results = {"L": None, "G": None}
        waiting = {"L": [], "G": []}

        def put(kind, some, earlier):
            parts = [part for part in waiting[kind] if some(part)]
            waiting[kind] = [part for part in waiting[kind] if not some(part)]
            if parts:
                results[kind] = place(results[kind], parts, earlier)
                return [results[kind]]
            return earlier

        sigmas = {}
        steps = ["L0", "a0", "L1+G0"]
        for n in range(1, e):
            steps += [f"a{n}", f"G{n}", "pL0"] if n == 1 else [f"a{n}", f"G{n}"]
        for step in steps:
            if step[0] == "p":
                last = put(step[1], lambda part: len(step) < 3 or part[4] == int(step[2]), last)
                continue
            if step[0] == "a":
                g = int(step[1])
                group = singles[g]
                sigma = add_partial(group, tables[0], greater_rows, received[g], last)
                last = sigma
                sigmas[g] = (sigma, [to_lanes(x) for x in sigma])
                continue
            jobs, made = [], []
            for kind, g in step.split("+"):
                g = int(g)
                for i, n in enumerate(groups[g] if kind == "L" else singles[g]):
                    made.append((kind, n, g))
                    if kind == "L":
                        jobs.append(lesser_job(n))
                    else:
                        sigma, beside = sigmas[g]
                        beside = [at(x, (i,)) for x in beside]
                        jobs.append((inverse_at(n), in_order((sigma[0], (i,)), at(sigma[1:], (i,)), beside)))
            last = product(jobs, last, STEP if step == "L0" else 0)
            back = back_to_rows(last)
            if step == "L0":
                for rows, beside in zip(lesser_rows, lesser_rows_beside):
                    rows[-1] = after([rows[-1]], *last)[0]
                    beside[-1] = to_lanes(rows[-1])
            for k, (kind, n, g) in enumerate(made):
                waiting[kind] += [(n, d, x, k, g) for d, x in enumerate(back)]
        last = put("L", lambda part: part[1] == 0, last)
        last = put("G", lambda part: part[1] == 0, last)
        for kind, g in [*(("L", g) for g in range(len(groups))), *(("G", n) for n in range(e))]:
            last = put(kind, lambda part: part[4] == g, last)
        lesser_out, greater_out = results["L"], results["G"]
        return lesser_out, greater_out

    block, coupled = P("en", "blk", "ph", None), P("en", "ph")
    return jax.shard_map(
        on_device,
        mesh=mesh,
        in_specs=(block, block, block, coupled, coupled),
        out_specs=(block, block),
        check_vma=False,
    )
```
